128 devices in a mesh: box: 16 (over y, x), grp: 8 (over z, core).
Axes of the slice: x: 4, y: 4, z: 4, core: 2. Of those that a mesh axis runs over, the one named last changes fastest.
Arguments:
- density: float32 [512, 768, 128], P('box', 'grp'), may hold values from 0.5 to 2
- momentum: float32 [3, 512, 768, 128], P(None, 'box', 'grp'), may hold values from -0.65 to 0.65
- energy: float32 [512, 768, 128], P('box', 'grp'), may hold values from 2 to 4
- dm_density: float32 [512, 768, 128], P('box', 'grp'), may hold values from 0.1 to 2
- box_dest: int32 [8, 16, 12, 1], P('grp', 'box'), may hold values from 0 to 15; in each aligned block of 12 rows (0 to 11, 12 to 23, ..., all dimensions but the last counted through in order) at most 2 rows name the same one
Outputs:
- new_density: float32 [512, 768, 128], P('box', 'grp')
- new_momentum: float32 [3, 512, 768, 128], P(None, 'box', 'grp')
- new_energy: float32 [512, 768, 128], P('box', 'grp')
- kd_density: float32 [8, 16, 16, 2, 32, 1024], P('grp', 'box')
The draws below stay inside these ranges and needn't reach their ends.
Inputs may be any that keep to these rules, and one draw needn't show every extreme that they name: `box_dest`: of the 12 boxes of one device, at most 2 name the same owner; every owner is named by some box of the whole array.
All inputs are finite; a program needn't handle non-finite values.
Results may differ from the reference program's by a relative error of at most 0.0003.
Values sent between devices are 32-bit elements; how exact they have to be, the bound alone decides.
No kernel may reach another device: no remote copies, remote signals or barrier semaphores. Data moves between devices by JAX's collectives and lax.ppermute only.
A program may use at most 192 MiB of HBM per device.

```python
import math
import jax
import jax.numpy as jnp
import numpy as np
from jax import lax

BOX = 32
BOX_Y = 3
BOX_Z = 4
RADIUS = 2
NX = 512
NY = 768
NZ = 128
BOXES_DEV = 12
CAP = 2
N_BOX = 16
N_GRP = 8


def draw_momentum(key, part):
    key = jax.random.fold_in(key, 7)
    phase_key = jax.random.fold_in(key, 1)
    noise_key = jax.random.fold_in(key, 2)
    phases = jax.random.uniform(phase_key, (3,), jnp.float32, 0.0, 2.0 * math.pi)
    wave_number = 2.0 * math.pi / 16.0
    along_x = jnp.sin(jnp.arange(NX, dtype=jnp.float32) * wave_number + phases[0])
    along_y = jnp.sin(jnp.arange(NY, dtype=jnp.float32) * wave_number + phases[1])
    along_z = jnp.sin(jnp.arange(NZ, dtype=jnp.float32) * wave_number + phases[2])
    full_shape = (NX, NY, NZ)
    smooth_part = jnp.stack([jnp.broadcast_to(along_x[:, None, None], full_shape), jnp.broadcast_to(along_y[None, :, None], full_shape), jnp.broadcast_to(along_z[None, None, :], full_shape)])
    noise_part = jnp.clip(0.1 * jax.random.normal(noise_key, (3, NX, NY, NZ), jnp.float32), -0.25, 0.25)
    return 0.4 * smooth_part + noise_part


def levels(rng, dims, split, least, high):
    def one(dim, shards_of):
        draws = jax.random.uniform(jax.random.fold_in(jax.random.fold_in(rng, 6), dim), (shards_of,), jnp.float32, least / len(split), high / len(split))
        return jnp.repeat(jnp.exp(draws), dims[dim] // shards_of).reshape((-1,) + (1,) * (len(dims) - dim - 1))

    factor_of = one(*split[0])
    for cut in split[1:]:
        factor_of = factor_of * one(*cut)
    return factor_of


def shared_out(rng, own, number, rows, count, top, most, lean):
    order = jax.random.permutation(rng, count)
    packed, ordinary = load_shares(count, rows * top, most, lean, True), load_shares(count, rows * top, most, lean, False)
    places = jnp.arange(count)

    def named(sizes, turn):
        used = int((sizes > 0).sum())
        fixed = max(1, used // 4)
        passed = fixed + (places - fixed + turn * (used - fixed)) % max(1, count - fixed)
        return jnp.zeros((count,), jnp.int32).at[order[jnp.where(places < fixed, places, passed)]].set(jnp.asarray(sizes, jnp.int32))

    sizes = jnp.where(number % 4 == 0, named(packed, number // 4), named(ordinary, number - number // 4 - 1))
    mixed = jax.random.permutation(jax.random.fold_in(own, 3), count)
    source_of, sink = mixed[0:count // 2 * 2:2], mixed[1:count // 2 * 2:2]
    room = jnp.minimum(sizes[source_of] - 1, most - sizes[sink]) // 2
    room = jnp.where((source_of == order[0]) | (sink == order[0]) | (sizes[sink] == 0), 0, jnp.maximum(room, 0))
    passed = jax.random.randint(jax.random.fold_in(own, 4), (count // 2,), 0, 1 << 20) % (room + 1)
    sizes = sizes.at[source_of].add(-passed).at[sink].add(passed)
    labels = jnp.searchsorted(jnp.cumsum(sizes), jnp.arange(rows * top), side="right").astype(jnp.int32)
    listing = labels.reshape(top, rows).T
    listing = listing[jax.random.permutation(jax.random.fold_in(own, 1), rows)]
    turn = jax.random.randint(jax.random.fold_in(own, 2), (rows, 1), 0, top)
    return jnp.take_along_axis(listing, (jnp.arange(top)[None, :] + turn) % top, axis=1)


def load_shares(count, total, limit, skew, full):
    loads = [(1 << 20) // math.isqrt(standing ** skew) + 1 for standing in range(1, count + 1)]
    largest = limit if full else min(limit, max(-(-total // count), total * loads[0] // sum(loads)))
    least = 1 if total - largest >= count - 1 else 0
    counts, spare = [largest] + [least] * (count - 1), total - largest - least * (count - 1)
    while spare > 0:
        free = [i for i in range(1, count) if counts[i] < largest] or [i for i in range(1, count) if counts[i] < limit]
        pool, left = sum([loads[i] for i in free]), spare
        for i in free:
            more = min(limit - counts[i], max(1, left * loads[i] // pool), spare)
            counts[i] = counts[i] + more
            spare = spare - more
    return np.array(counts)


def setup_inputs(seed: int = 0) -> dict:
    key_list = jax.random.split(jax.random.key(seed), 6)
    density = jnp.clip(jnp.exp(math.log(2.0) - 1.3862944 * jax.random.uniform(key_list[0], (NX, NY, NZ), jnp.float32) ** levels(key_list[0], (NX, NY, NZ), ((0, 16), (1, 8)), -0.2, 0.2)), 0.5, 2.0)
    momentum = draw_momentum(jax.random.fold_in(key_list[5], 71), 0)
    energy = jnp.clip(2.0 + 2.0 * jax.random.uniform(key_list[2], (NX, NY, NZ), jnp.float32) ** levels(key_list[2], (NX, NY, NZ), ((0, 16), (1, 8)), -0.2, 0.2), 2.0, 4.0)
    dm_density = jnp.clip(jnp.exp(math.log(2.0) - 2.9957323 * jax.random.uniform(key_list[3], (NX, NY, NZ), jnp.float32) ** levels(key_list[3], (NX, NY, NZ), ((0, 16), (1, 8)), -0.2, 0.2)), 0.1, 2.0)
    box_dest_keys = jax.random.split(jax.random.fold_in(key_list[4], 1), N_GRP * N_BOX * BOXES_DEV // BOXES_DEV)
    box_dest_turns = jax.random.permutation(jax.random.fold_in(key_list[4], 3), N_GRP * N_BOX * BOXES_DEV // BOXES_DEV)
    box_dest = jax.vmap(lambda own, number: shared_out(jax.random.fold_in(key_list[4], 2), own, number, BOXES_DEV, N_BOX, 1, CAP, 2))(box_dest_keys, box_dest_turns).reshape((N_GRP, N_BOX, BOXES_DEV, 1))
    return dict(density=density, momentum=momentum, energy=energy, dm_density=dm_density, box_dest=box_dest)


gamma_gas = 5.0 / 3.0
step_ratio = 0.06

def cut_along(values, offset, length, sweep_axis):
    return lax.slice_in_dim(values, offset, offset + length, axis=sweep_axis)

def flux_of(conserved, normal):
    density = conserved[0]
    energy = conserved[4]
    kinetic = 0.5 * (conserved[1] * conserved[1] + conserved[2] * conserved[2] + conserved[3] * conserved[3]) / density
    pressure = (gamma_gas - 1.0) * (energy - kinetic)
    velocity = conserved[normal] / density
    rows_added = [jnp.zeros_like(pressure)]
    for component in range(1, 4):
        rows_added.append(pressure if component == normal else jnp.zeros_like(pressure))
    rows_added.append(pressure * velocity)
    fluxes = conserved * velocity[None] + jnp.stack(rows_added)
    sound_speed = jnp.sqrt(gamma_gas * pressure / density)
    return (fluxes, jnp.abs(velocity) + sound_speed)

def sweep_line(padded, sweep_axis, normal):
    length = padded.shape[sweep_axis] - 6
    cell_prev = cut_along(padded, 0, length + 3, sweep_axis)
    cell_here = cut_along(padded, 1, length + 3, sweep_axis)
    cell_next = cut_along(padded, 2, length + 3, sweep_axis)
    cell_far = cut_along(padded, 3, length + 3, sweep_axis)
    interface = (7.0 * (cell_here + cell_next) - (cell_prev + cell_far)) / 12.0
    interface = jnp.minimum(jnp.maximum(interface, jnp.minimum(cell_here, cell_next)), jnp.maximum(cell_here, cell_next))
    centre = cut_along(padded, 2, length + 2, sweep_axis)
    dev_left = cut_along(interface, 0, length + 2, sweep_axis) - centre
    dev_right = cut_along(interface, 1, length + 2, sweep_axis) - centre
    edge_left = centre + jnp.clip(dev_left, -2.0 * jnp.abs(dev_right), 2.0 * jnp.abs(dev_right))
    edge_right = centre + jnp.clip(dev_right, -2.0 * jnp.abs(dev_left), 2.0 * jnp.abs(dev_left))
    state_left = cut_along(edge_right, 0, length + 1, sweep_axis)
    state_right = cut_along(edge_left, 1, length + 1, sweep_axis)
    flux_left, reach_left = flux_of(state_left, normal)
    flux_right, reach_right = flux_of(state_right, normal)
    wave_speed = jnp.maximum(reach_left, reach_right)
    face_flux = 0.5 * (flux_left + flux_right) - 0.5 * wave_speed[None] * (state_right - state_left)
    inside = cut_along(padded, 3, length, sweep_axis)
    return inside - step_ratio * (cut_along(face_flux, 1, length, sweep_axis) - cut_along(face_flux, 0, length, sweep_axis))

def sweep_blocks(padded, sweep_axis, normal, block_axis, block_size):
    out_shape = list(padded.shape)
    out_shape[sweep_axis] -= 6
    block_count = padded.shape[block_axis] // block_size

    def one_block(block_index, result):
        offset = (block_index * block_size).astype(jnp.int32)
        portion = lax.dynamic_slice_in_dim(padded, offset, block_size, block_axis)
        swept = sweep_line(portion, sweep_axis, normal)
        return lax.dynamic_update_slice_in_dim(result, swept, offset, block_axis)
    return lax.fori_loop(0, block_count, one_block, jnp.zeros(out_shape, padded.dtype))

def wrap_pad(values, margin, pad_axis):
    extent = values.shape[pad_axis]
    return jnp.concatenate([cut_along(values, extent - margin, margin, pad_axis), values, cut_along(values, 0, margin, pad_axis)], axis=pad_axis)

def box_filter(padded, radius):
    result = padded
    for filter_axis in range(padded.ndim - 3, padded.ndim):
        extent = result.shape[filter_axis] - 2 * radius
        summed = cut_along(result, 0, extent, filter_axis)
        for shift_by in range(1, 2 * radius + 1):
            summed = summed + cut_along(result, shift_by, extent, filter_axis)
        result = summed
    return result / float((2 * radius + 1) ** 3)

def slot_selector(destination, owners, capacity):
    box_total = destination.shape[-1]
    positions = jnp.arange(box_total, dtype=jnp.int32)
    earlier = positions[None, :] < positions[:, None]
    same_dest = destination[..., :, None] == destination[..., None, :]
    slot_rank = lax.optimization_barrier(jnp.sum((same_dest & earlier).astype(jnp.int32), axis=-1))
    owner_ids = jnp.arange(owners, dtype=jnp.int32)
    slot_ids = jnp.arange(capacity, dtype=jnp.int32)
    chosen = (destination[..., None, None, :] == owner_ids[:, None, None]) & (slot_rank[..., None, None, :] == slot_ids[None, :, None])
    return chosen.astype(jnp.float32)

def reference(density, momentum, energy, dm_density, box_dest):
    conserved = jnp.concatenate([density[None], momentum, energy[None]], axis=0)
    conserved = sweep_blocks(wrap_pad(conserved, 3, 1), 1, 1, 2, 8)
    conserved = sweep_blocks(wrap_pad(conserved, 3, 2), 2, 2, 1, 8)
    conserved = sweep_blocks(wrap_pad(conserved, 3, 3), 3, 3, 1, 8)
    total_density = conserved[0] + dm_density
    padded = wrap_pad(wrap_pad(wrap_pad(total_density, RADIUS, 0), RADIUS, 1), RADIUS, 2)
    smoothed = box_filter(padded, RADIUS)
    box_cells = smoothed.reshape(N_BOX, BOX, N_GRP, BOX_Y, BOX, BOX_Z, BOX).transpose(2, 0, 3, 5, 1, 4, 6).reshape(N_GRP, N_BOX, BOX_Y * BOX_Z, BOX, BOX * BOX)
    selector = slot_selector(box_dest[..., 0], N_BOX, CAP)
    kd_density = jnp.einsum('gsjck,gskab->gjscab', selector, box_cells, precision=lax.Precision.HIGHEST)
    return (conserved[0], conserved[1:4], conserved[4], kd_density)
```

```python
import functools
import math

import jax
import jax.numpy as jnp
from jax import lax
from jax.experimental import pallas as pl
from jax.experimental.pallas import tpu as pltpu
from jax.sharding import PartitionSpec as P

BOX = 32
BOX_Y = 3
BOX_Z = 4
NX = 32
NY = 96
NZ = 128
FRAME = 112
GROUP = 16
STEP = 0.03
SCALES = (1.0, STEP, STEP, STEP, 2.0 * STEP * STEP)
UNSCALES = (1.0, 1.0 / STEP, 1.0 / STEP, 1.0 / STEP, 1.0 / (2.0 * STEP * STEP))
SOUND = math.sqrt(5.0 / 3.0)
TINY = 1e-30
VMEM_LIMIT = 56 * 1024 * 1024


def limit(value, other):
    bound = jnp.abs(other + other)
    return jnp.maximum(jnp.minimum(value, bound), -bound)


def deviation(d_prev, d_here, d_next):
    value = 0.5 * d_here + (d_prev - d_next) * (1.0 / 12.0)
    return jnp.minimum(jnp.maximum(value, jnp.minimum(d_here, 0.0)), jnp.maximum(d_here, 0.0))


def invert(x):
    return 1.0 / x


def state_of(u, normal):
    inverse = invert(u[0])
    squares = u[1] * u[1] + u[2] * u[2] + u[3] * u[3]
    pressure = u[4] - squares * inverse
    third = pressure * (1.0 / 3.0)
    velocity = u[normal] * inverse
    ratio = jnp.maximum(third * inverse, TINY)
    reach = jnp.abs(velocity) + SOUND * (ratio * lax.rsqrt(ratio))
    return velocity, third, reach


def flux(left, right, normal):
    v_left, p_left, reach_left = state_of(left, normal)
    v_right, p_right, reach_right = state_of(right, normal)
    reach = jnp.maximum(reach_left, reach_right)
    up = v_left + reach
    down = v_right - reach
    out = [left[f] * up + right[f] * down for f in range(5)]
    out[normal] = out[normal] + (p_left + p_right)
    work = p_left * v_left + p_right * v_right
    out[4] = out[4] + (work + work)
    return out


class Line:
    def __init__(self, normal):
        self.normal = normal
        self.q = []
        self.d = []
        self.dl = None
        self.er = None
        self.flux = None

    def load(self, q, carry):
        self.q = list(q)
        self.d = [carry[0:5], carry[5:10]]
        self.dl = carry[10:15]
        self.er = carry[15:20]
        self.flux = carry[20:25]

    def carry(self):
        return tuple(self.d[0]) + tuple(self.d[1]) + tuple(self.dl) + tuple(self.er) + tuple(self.flux)

    def push(self, new):
        q, d = self.q, self.d
        out = None
        if q:
            d0 = [a - b for a, b in zip(new, q[-1])]
            if len(d) >= 2:
                d2, d1 = d[-2], d[-1]
                dr = [deviation(*t) for t in zip(d2, d1, d0)]
                if self.dl is not None:
                    here = q[-2]
                    right = [c + limit(r, l) for c, r, l in zip(here, dr, self.dl)]
                    if self.er is not None:
                        left = [c + limit(l, r) for c, r, l in zip(here, dr, self.dl)]
                        now = flux(self.er, left, self.normal)
                        if self.flux is not None:
                            out = [c - (a - b) for c, a, b in zip(q[-3], now, self.flux)]
                        self.flux = now
                    self.er = right
                self.dl = [r - s for r, s in zip(dr, d1)]
            d.append(d0)
            self.d = d[-2:]
        q.append(new)
        self.q = q[-3:]
        return out


def turn(x, shift):
    return pltpu.roll(x, shift % NZ, 1)


def sweep_lanes(q):
    d = [turn(x, -1) - x for x in q]
    dr = [deviation(turn(x, 1), x, turn(x, -1)) for x in d]
    dl = [turn(r - x, 1) for r, x in zip(dr, d)]
    right = [c + limit(r, l) for c, r, l in zip(q, dr, dl)]
    left = [turn(c + limit(l, r), -1) for c, r, l in zip(q, dr, dl)]
    now = flux(right, left, 3)
    return [c - (f - turn(f, 1)) for c, f in zip(q, now)]


def lane_sum(t):
    pair = t + turn(t, -1)
    return t + turn(pair, 2) + turn(pair, -1)


def x_sweep(q_ref, s_ref, segments):
    def tile(t, _):
        row = pl.multiple_of(t * 8, 8)
        for base, out_base, count in segments:
            line = Line(1)
            for i in range(count + 6):
                new = [q_ref[f, base + i, pl.ds(row, 8), :] * SCALES[f] if f else q_ref[f, base + i, pl.ds(row, 8), :]
                       for f in range(5)]
                out = line.push(new)
                if out is not None:
                    x = out_base + i - 6
                    for f in range(5):
                        s_ref[pl.ds((f * GROUP + x) * FRAME + row, 8), :] = out[f]
        return 0

    lax.fori_loop(0, FRAME // 8, tile, 0)


ROWS_STEP = 4


def yz_sweep(s_ref, dm_ref, o_ref, t_ref):
    def group(g, _):
        def at(f, row):
            return pl.ds((f * GROUP + g * 8) * FRAME + row, 8, stride=FRAME)

        def rows(row):
            return [s_ref[at(f, row), :] for f in range(5)]

        first = Line(2)
        for row in range(3, 9):
            first.push(rows(row))

        def some(b, carry):
            line = Line(2)
            base = 9 + b * ROWS_STEP
            line.load([rows(base - 3), rows(base - 2), rows(base - 1)], carry)
            ahead = [rows(base + r) for r in range(ROWS_STEP)]
            for r in range(ROWS_STEP):
                swept = line.push(ahead[r])
                final = sweep_lanes(swept)
                row = base + r - 3
                for f in range(5):
                    o_ref[at(f, row), :] = final[f] * UNSCALES[f] if f else final[f]
                total = final[0] + dm_ref[at(0, row), :]
                t_ref[at(0, row), :] = lane_sum(total)
            return line.carry()

        lax.fori_loop(0, 100 // ROWS_STEP, some, first.carry())
        return 0

    lax.fori_loop(0, GROUP // 8, group, 0)


def smooth(planes, dest_ref, x_ref, y_ref, send_ref, send_row):
    def x_tile(t, _):
        row = pl.multiple_of(t * 8, 8)
        values = [planes(p, row) for p in range(12)]
        pairs = [values[p] + values[p + 1] for p in range(11)]
        for p in range(8):
            x_ref[pl.ds(p * FRAME + row, 8), :] = pairs[p] + pairs[p + 2] + values[p + 4]
        return 0

    lax.fori_loop(0, FRAME // 8, x_tile, 0)

    def y_plane(p, _):
        for t in range(NY // 8):
            start = p * FRAME + 8 + 8 * t
            parts = [x_ref[pl.ds(start + k, 8), :] for k in range(-2, 3)]
            total = ((parts[0] + parts[1]) + (parts[3] + parts[4])) + parts[2]
            y_ref[pl.ds(p * NY + 8 * t, 8), :] = total * (1.0 / 125.0)
        return 0

    lax.fori_loop(0, 8, y_plane, 0)

    places = []
    dests = [dest_ref[k] for k in range(12)]
    for k in range(12):
        slot = jnp.int32(0)
        for other in range(k):
            slot = slot + (dests[other] == dests[k]).astype(jnp.int32)
        places.append(dests[k] * 2 + slot)

    quarter = lax.broadcasted_iota(jnp.int32, (8, NZ), 1) // BOX

    def pick(values):
        out = values[3]
        for b in range(3):
            out = jnp.where(quarter == b, values[b], out)
        return out

    for by in range(BOX_Y):
        for m in range(8):
            s = [y_ref[pl.ds(by * BOX + 4 * m + q, 8, stride=NY), :] for q in range(4)]
            moved = []
            for k in range(4):
                mixed = pick([s[(b + k) % 4] for b in range(4)])
                moved.append(turn(mixed, k * BOX) if k else mixed)
            for bz in range(4):
                out = pick([moved[(q - bz) % 4] for q in range(4)])
                send_ref[places[by * 4 + bz], pl.ds(send_row, 8), pl.ds(m * NZ, NZ)] = out


def clear(send_ref):
    def one(i, _):
        send_ref[i] = jnp.zeros(send_ref.shape[1:], jnp.float32)
        return 0

    lax.fori_loop(0, send_ref.shape[0], one, 0)


def fetch(copies):
    for c in copies:
        c.start()
    for c in copies:
        c.wait()


def load_copies(density, momentum, energy, sem, q_ref, own, place, count):
    mid = pl.ds(8, NY)
    src, dst = pl.ds(own, count), pl.ds(place, count)
    return [
        pltpu.make_async_copy(density.at[src], q_ref.at[0, dst, mid], sem),
        pltpu.make_async_copy(momentum.at[:, src], q_ref.at[pl.ds(1, 3), dst, mid], sem),
        pltpu.make_async_copy(energy.at[src], q_ref.at[4, dst, mid], sem),
    ]


def side_copies(before, after, sem, q_ref, own, place, count):
    src, dst = pl.ds(own, count), pl.ds(place, count)
    return [
        pltpu.make_async_copy(before.at[pl.ds(0, 5), src], q_ref.at[:, dst, pl.ds(0, 8)], sem),
        pltpu.make_async_copy(after.at[pl.ds(0, 5), src], q_ref.at[:, dst, pl.ds(104, 8)], sem),
    ]


def flat_rows(ref, count, rows):
    return ref.reshape(count, rows, NZ)


def dm_copies(dm, before, after, sem, dm_ref, own, place, count):
    src, dst = pl.ds(own, count), pl.ds(place, count)
    d3 = flat_rows(dm_ref, GROUP, FRAME)
    return [
        pltpu.make_async_copy(dm.at[src], d3.at[dst, pl.ds(8, NY)], sem),
        pltpu.make_async_copy(before.at[5, src], d3.at[dst, pl.ds(0, 8)], sem),
        pltpu.make_async_copy(after.at[5, src], d3.at[dst, pl.ds(104, 8)], sem),
    ]


def out_copies(o_ref, outs, sem, own, place, count):
    o4 = o_ref.reshape(5, GROUP, FRAME, NZ)
    src, dst, mid = pl.ds(place, count), pl.ds(own, count), pl.ds(8, NY)
    density, momentum, energy = outs
    return [
        pltpu.make_async_copy(o4.at[0, src, mid], density.at[dst], sem),
        pltpu.make_async_copy(o4.at[pl.ds(1, 3), src, mid], momentum.at[:, dst], sem),
        pltpu.make_async_copy(o4.at[4, src, mid], energy.at[dst], sem),
    ]


def inner_kernel(dest, density, momentum, energy, dm, y_before, y_after,
                 out_density, out_momentum, out_energy, out_sums, send,
                 q_ref, s_ref, o_ref, dm_ref, t_ref, x_ref, y_ref, sem, out_sem):
    fetch(load_copies(density, momentum, energy, sem, q_ref, 1, 0, 22)
          + side_copies(y_before, y_after, sem, q_ref, 1, 0, 22)
          + dm_copies(dm, y_before, y_after, sem, dm_ref, 4, 0, 16))
    x_sweep(q_ref, s_ref, ((0, 0, 16),))
    yz_sweep(s_ref, dm_ref, o_ref, t_ref)
    t3 = flat_rows(t_ref, GROUP, FRAME)
    leaving = out_copies(o_ref, (out_density, out_momentum, out_energy), out_sem, 4, 0, 16)
    leaving.append(pltpu.make_async_copy(t3, out_sums, out_sem))
    for c in leaving:
        c.start()
    clear(send)
    smooth(lambda p, row: t_ref[pl.ds((2 + p) * FRAME + row, 8), :], dest, x_ref, y_ref, send, 0)
    for c in leaving:
        c.wait()


def outer_kernel(density, momentum, energy, dm, y_before, y_after, x_before, x_after, c_before, c_after,
                 in_density, in_momentum, in_energy,
                 out_density, out_momentum, out_energy, out_sums, to_next, to_prev,
                 q_ref, s_ref, o_ref, dm_ref, t_ref, sem, out_sem):
    mid = pl.ds(8, NY)
    copies = (load_copies(density, momentum, energy, sem, q_ref, 17, 0, 15)
              + load_copies(density, momentum, energy, sem, q_ref, 0, 21, 7)
              + side_copies(y_before, y_after, sem, q_ref, 17, 0, 15)
              + side_copies(y_before, y_after, sem, q_ref, 0, 21, 7)
              + side_copies(c_before, c_after, sem, q_ref, 0, 15, 6)
              + dm_copies(dm, y_before, y_after, sem, dm_ref, 20, 0, 12)
              + dm_copies(dm, y_before, y_after, sem, dm_ref, 0, 12, 4))
    copies.append(pltpu.make_async_copy(x_after, q_ref.at[:, pl.ds(15, 3), mid], sem))
    copies.append(pltpu.make_async_copy(x_before, q_ref.at[:, pl.ds(18, 3), mid], sem))
    fetch(copies)
    x_sweep(q_ref, s_ref, ((0, 0, 12), (18, 12, 4)))
    yz_sweep(s_ref, dm_ref, o_ref, t_ref)
    t3 = flat_rows(t_ref, GROUP, FRAME)
    outs = (out_density, out_momentum, out_energy)
    leaving = out_copies(o_ref, outs, out_sem, 20, 0, 12) + out_copies(o_ref, outs, out_sem, 0, 12, 4)
    leaving.append(pltpu.make_async_copy(t3, out_sums, out_sem))
    leaving.append(pltpu.make_async_copy(t3.at[pl.ds(10, 2)], to_next, out_sem))
    leaving.append(pltpu.make_async_copy(t3.at[pl.ds(12, 2)], to_prev, out_sem))
    fetch(leaving)


def rest_kernel(dest, sums_inner, sums_outer, from_prev, from_next, send, w_ref, x_ref, y_ref, sem):
    def part(src, own, place, count):
        return pltpu.make_async_copy(src.at[pl.ds(own, count)], w_ref.at[pl.ds(place, count)], sem)

    copies = [
        part(from_prev, 0, 0, 2),
        part(sums_outer, 12, 2, 4),
        part(sums_inner, 0, 6, 6),
        part(sums_inner, 10, 12, 6),
        part(sums_outer, 0, 18, 12),
        part(from_next, 0, 30, 2),
    ]
    for c in copies:
        c.start()
    clear(send)
    for c in copies:
        c.wait()
    for row, base in ((0, 0), (8, 12), (16, 20)):
        smooth(lambda p, r: w_ref[base + p, pl.ds(r, 8), :], dest, x_ref, y_ref, send, row)


ANY = pl.BlockSpec(memory_space=pl.ANY)
SMEM = pl.BlockSpec(memory_space=pltpu.SMEM)
VMEM = pl.BlockSpec(memory_space=pltpu.VMEM)
F32 = jnp.float32


def shape(*dims):
    return jax.ShapeDtypeStruct(dims, F32)


def params():
    return pltpu.CompilerParams(vmem_limit_bytes=VMEM_LIMIT)


def main_scratch(planes):
    rows = GROUP * FRAME
    return [
        pltpu.VMEM((5, planes, FRAME, NZ), F32),
        pltpu.VMEM((5 * rows, NZ), F32),
        pltpu.VMEM((5 * rows, NZ), F32),
        pltpu.VMEM((rows, NZ), F32),
        pltpu.VMEM((rows, NZ), F32),
    ]


def smooth_scratch():
    return [pltpu.VMEM((8 * FRAME, NZ), F32), pltpu.VMEM((8 * NY, NZ), F32)]


FIELD_SHAPES = (shape(NX, NY, NZ), shape(3, NX, NY, NZ), shape(NX, NY, NZ))


def shifted(value, axis, by):
    size = lax.axis_size(axis)
    return lax.ppermute(value, axis, [(i, (i + by) % size) for i in range(size)])


def body(density, momentum, energy, dm_density, box_dest):
    dest = box_dest[0, 0, :, 0]
    fields = (density[None], momentum, energy[None])

    def cut(arrays, planes, rows):
        return jnp.concatenate([a[:, planes[0]:planes[1], rows[0]:rows[1]] for a in arrays], axis=0)

    y_before = shifted(cut(fields + (dm_density[None],), (0, NX), (NY - 8, NY)), "grp", 1)
    y_after = shifted(cut(fields + (dm_density[None],), (0, NX), (0, 8)), "grp", -1)
    x_before = shifted(cut(fields, (NX - 3, NX), (0, NY)), "box", 1)
    x_after = shifted(cut(fields, (0, 3), (0, NY)), "box", -1)

    inner = pl.pallas_call(
        inner_kernel,
        out_shape=FIELD_SHAPES + (shape(GROUP, FRAME, NZ), shape(32, 8, 1024)),
        in_specs=[SMEM] + [ANY] * 6,
        out_specs=[ANY] * 4 + [VMEM],
        scratch_shapes=main_scratch(22) + smooth_scratch() + [pltpu.SemaphoreType.DMA, pltpu.SemaphoreType.DMA],
        compiler_params=params(),
        name="inner",
    )(dest, density, momentum, energy, dm_density, y_before, y_after)
    new_density, new_momentum, new_energy, sums_inner, send_inner = inner
    got_inner = lax.all_to_all(send_inner.reshape(16, 2, 8, 1024), "box", split_axis=0, concat_axis=0, tiled=True)

    x_both = jnp.concatenate([x_after, x_before], axis=1)
    c_before = shifted(x_both[:, :, NY - 8:], "grp", 1)
    c_after = shifted(x_both[:, :, :8], "grp", -1)
    outer = pl.pallas_call(
        outer_kernel,
        out_shape=FIELD_SHAPES + (shape(GROUP, FRAME, NZ), shape(2, FRAME, NZ), shape(2, FRAME, NZ)),
        in_specs=[ANY] * 13,
        out_specs=[ANY] * 6,
        scratch_shapes=main_scratch(28) + [pltpu.SemaphoreType.DMA, pltpu.SemaphoreType.DMA],
        input_output_aliases={10: 0, 11: 1, 12: 2},
        compiler_params=params(),
        name="outer",
    )(density, momentum, energy, dm_density, y_before, y_after, x_before, x_after, c_before, c_after,
      new_density, new_momentum, new_energy)
    new_density, new_momentum, new_energy, sums_outer, to_next, to_prev = outer
    from_prev = shifted(to_next, "box", 1)
    from_next = shifted(to_prev, "box", -1)
    send_rest = pl.pallas_call(
        rest_kernel,
        out_shape=shape(32, 24, 1024),
        in_specs=[SMEM] + [ANY] * 4,
        out_specs=VMEM,
        scratch_shapes=[pltpu.VMEM((32, FRAME, NZ), F32)] + smooth_scratch() + [pltpu.SemaphoreType.DMA],
        compiler_params=params(),
        name="rest",
    )(dest, sums_inner, sums_outer, from_prev, from_next)
    got_rest = lax.all_to_all(send_rest.reshape(16, 2, 24, 1024), "box", split_axis=0, concat_axis=0, tiled=True)
    kd = jnp.concatenate([got_rest[:, :, :8], got_inner, got_rest[:, :, 8:]], axis=2)
    return (new_density, new_momentum, new_energy, kd[None, None])


def solution(mesh):
    in_specs = (
        P("box", "grp", None),
        P(None, "box", "grp", None),
        P("box", "grp", None),
        P("box", "grp", None),
        P("grp", "box", None, None),
    )
    out_specs = (
        P("box", "grp", None),
        P(None, "box", "grp", None),
        P("box", "grp", None),
        P("grp", "box", None, None, None, None),
    )
    return jax.shard_map(body, mesh=mesh, in_specs=in_specs, out_specs=out_specs, check_vma=False)
```

```python
import functools
import math

import jax
import jax.numpy as jnp
from jax import lax
from jax.experimental import pallas as pl
from jax.experimental.pallas import tpu as pltpu
from jax.sharding import PartitionSpec as P

BOX = 32
BOX_Y = 3
BOX_Z = 4
NX = 32
NY = 96
NZ = 128
FRAME = 112
TILES = FRAME // 8
STRIDE = 120
STEP = 0.03
SCALES = (1.0, STEP, STEP, STEP, 2.0 * STEP * STEP)
UNSCALES = (1.0, 1.0 / STEP, 1.0 / STEP, 1.0 / STEP, 1.0 / (2.0 * STEP * STEP))
SOUND = math.sqrt(5.0 / 3.0)
TINY = 1e-30
VMEM_LIMIT = 56 * 1024 * 1024


def limit(value, other):
    bound = jnp.abs(other + other)
    return jnp.maximum(jnp.minimum(value, bound), -bound)


def deviation(d_prev, d_here, d_next):
    value = 0.5 * d_here + (d_prev - d_next) * (1.0 / 12.0)
    return jnp.minimum(jnp.maximum(value, jnp.minimum(d_here, 0.0)), jnp.maximum(d_here, 0.0))


def invert(x):
    return 1.0 / x


def state_of(u, normal):
    inverse = invert(u[0])
    squares = u[1] * u[1] + u[2] * u[2] + u[3] * u[3]
    pressure = u[4] - squares * inverse
    third = pressure * (1.0 / 3.0)
    velocity = u[normal] * inverse
    ratio = jnp.maximum(third * inverse, TINY)
    reach = jnp.abs(velocity) + SOUND * (ratio * lax.rsqrt(ratio))
    return velocity, third, reach


def flux(left, right, normal):
    v_left, p_left, reach_left = state_of(left, normal)
    v_right, p_right, reach_right = state_of(right, normal)
    reach = jnp.maximum(reach_left, reach_right)
    up = v_left + reach
    down = v_right - reach
    out = [left[f] * up + right[f] * down for f in range(5)]
    out[normal] = out[normal] + (p_left + p_right)
    work = p_left * v_left + p_right * v_right
    out[4] = out[4] + (work + work)
    return out


class Line:
    def __init__(self, normal):
        self.normal = normal
        self.q = []
        self.d = []
        self.dl = None
        self.er = None
        self.flux = None

    def load(self, q, carry):
        self.q = list(q)
        self.d = [carry[0:5], carry[5:10]]
        self.dl = carry[10:15]
        self.er = carry[15:20]
        self.flux = carry[20:25]

    def carry(self):
        return tuple(self.d[0]) + tuple(self.d[1]) + tuple(self.dl) + tuple(self.er) + tuple(self.flux)

    def push(self, new):
        q, d = self.q, self.d
        out = None
        if q:
            d0 = [a - b for a, b in zip(new, q[-1])]
            if len(d) >= 2:
                d2, d1 = d[-2], d[-1]
                dr = [deviation(*t) for t in zip(d2, d1, d0)]
                if self.dl is not None:
                    here = q[-2]
                    right = [c + limit(r, l) for c, r, l in zip(here, dr, self.dl)]
                    if self.er is not None:
                        left = [c + limit(l, r) for c, r, l in zip(here, dr, self.dl)]
                        now = flux(self.er, left, self.normal)
                        if self.flux is not None:
                            out = [c - (a - b) for c, a, b in zip(q[-3], now, self.flux)]
                        self.flux = now
                    self.er = right
                self.dl = [r - s for r, s in zip(dr, d1)]
            d.append(d0)
            self.d = d[-2:]
        q.append(new)
        self.q = q[-3:]
        return out


def turn(x, shift):
    return pltpu.roll(x, shift % NZ, 1)


def sweep_lanes(q):
    d = [turn(x, -1) - x for x in q]
    dr = [deviation(turn(x, 1), x, turn(x, -1)) for x in d]
    dl = [turn(r - x, 1) for r, x in zip(dr, d)]
    right = [c + limit(r, l) for c, r, l in zip(q, dr, dl)]
    left = [turn(c + limit(l, r), -1) for c, r, l in zip(q, dr, dl)]
    now = flux(right, left, 3)
    return [c - (f - turn(f, 1)) for c, f in zip(q, now)]


def lane_sum(t):
    pair = t + turn(t, -1)
    return t + turn(pair, 2) + turn(pair, -1)


def x_sweep(q_ref, s_ref, planes, segments, ready):
    def tile(t, _):
        ready(t)
        row = pl.multiple_of(t * 8, 8)
        for base, out_base, count in segments:
            line = Line(1)
            for i in range(count + 6):
                new = [q_ref[f, base + i, pl.ds(row, 8), :] * SCALES[f] if f else q_ref[f, base + i, pl.ds(row, 8), :]
                       for f in range(5)]
                out = line.push(new)
                if out is not None:
                    x = out_base + i - 6
                    for f in range(5):
                        s_ref[pl.ds((f * planes + x) * STRIDE + row, 8), :] = out[f]
        return 0

    lax.fori_loop(0, TILES, tile, 0)


ROWS_STEP = 10


def yz_sweep(s_ref, dm_ref, o_ref, t_ref, planes, t_base):
    def group(g, _):
        def at(f, row, base=0):
            return pl.ds((f * planes + g * 8 + base) * STRIDE + row, 8, stride=STRIDE)

        def rows(row):
            return [s_ref[at(f, row), :] for f in range(5)]

        first = Line(2)
        for row in range(3, 9):
            first.push(rows(row))

        def some(b, carry):
            line = Line(2)
            base = 9 + b * ROWS_STEP
            line.load([rows(base - 3), rows(base - 2), rows(base - 1)], carry)
            ahead = [rows(base + r) for r in range(ROWS_STEP)]
            for r in range(ROWS_STEP):
                swept = line.push(ahead[r])
                final = sweep_lanes(swept)
                row = base + r - 3
                for f in range(5):
                    o_ref[at(f, row), :] = final[f] * UNSCALES[f] if f else final[f]
                total = final[0] + dm_ref[at(0, row), :]
                t_ref[at(0, row, t_base), :] = lane_sum(total)
            return line.carry()

        lax.fori_loop(0, 100 // ROWS_STEP, some, first.carry())
        return 0

    lax.fori_loop(0, planes // 8, group, 0)


def smooth(planes, dest_ref, x_ref, y_ref, send_ref, send_row):
    def x_tile(t, _):
        row = pl.multiple_of(t * 8, 8)
        values = [planes(p, row) for p in range(12)]
        pairs = [values[p] + values[p + 1] for p in range(11)]
        for p in range(8):
            x_ref[pl.ds(p * FRAME + row, 8), :] = pairs[p] + pairs[p + 2] + values[p + 4]
        return 0

    lax.fori_loop(0, TILES, x_tile, 0)

    def y_plane(p, _):
        for t in range(NY // 8):
            start = p * FRAME + 8 + 8 * t
            parts = [x_ref[pl.ds(start + k, 8), :] for k in range(-2, 3)]
            total = ((parts[0] + parts[1]) + (parts[3] + parts[4])) + parts[2]
            y_ref[pl.ds(p * NY + 8 * t, 8), :] = total * (1.0 / 125.0)
        return 0

    lax.fori_loop(0, 8, y_plane, 0)

    places = []
    dests = [dest_ref[k] for k in range(12)]
    for k in range(12):
        slot = jnp.int32(0)
        for other in range(k):
            slot = slot + (dests[other] == dests[k]).astype(jnp.int32)
        places.append(dests[k] * 2 + slot)

    quarter = lax.broadcasted_iota(jnp.int32, (8, NZ), 1) // BOX

    def pick(values):
        out = values[3]
        for b in range(3):
            out = jnp.where(quarter == b, values[b], out)
        return out

    for by in range(BOX_Y):
        for m in range(8):
            s = [y_ref[pl.ds(by * BOX + 4 * m + q, 8, stride=NY), :] for q in range(4)]
            moved = []
            for k in range(4):
                mixed = pick([s[(b + k) % 4] for b in range(4)])
                moved.append(turn(mixed, k * BOX) if k else mixed)
            for bz in range(4):
                out = pick([moved[(q - bz) % 4] for q in range(4)])
                send_ref[places[by * 4 + bz], pl.ds(send_row, 8), pl.ds(m * NZ, NZ)] = out


def clear(send_ref):
    def one(i, _):
        send_ref[i] = jnp.zeros(send_ref.shape[1:], jnp.float32)
        return 0

    lax.fori_loop(0, send_ref.shape[0], one, 0)


def rows_of(t):
    return pl.ds(pl.multiple_of(t * 8, 8), 8)


class Tiles:
    def __init__(self, q_ref, sems, parts):
        self.q_ref, self.sems, self.parts = q_ref, sems, parts

    def copies(self, t, kind):
        out = []
        for own, before, after, src, dst in self.parts:
            q = self.q_ref.at[:, dst, rows_of(t)]
            sem = self.sems.at[t]
            if kind == "before":
                out.append(pltpu.make_async_copy(before.at[pl.ds(0, 5), src], q, sem))
            elif kind == "after":
                out.append(pltpu.make_async_copy(after.at[pl.ds(0, 5), src], q, sem))
            elif len(own) == 1:
                out.append(pltpu.make_async_copy(own[0].at[:, src, rows_of(t - 1)], q, sem))
            else:
                density, momentum, energy = own
                rows = rows_of(t - 1)
                place = self.q_ref.at
                out.append(pltpu.make_async_copy(density.at[src, rows], place[0, dst, rows_of(t)], sem))
                out.append(pltpu.make_async_copy(momentum.at[:, src, rows], place[pl.ds(1, 3), dst, rows_of(t)], sem))
                out.append(pltpu.make_async_copy(energy.at[src, rows], place[4, dst, rows_of(t)], sem))
        return out

    def each(self, t, act):
        @pl.when(t == 0)
        def _():
            for c in self.copies(t, "before"):
                act(c)

        @pl.when(t == TILES - 1)
        def _():
            for c in self.copies(t, "after"):
                act(c)

        @pl.when((t > 0) & (t < TILES - 1))
        def _():
            for c in self.copies(t, "own"):
                act(c)

    def start(self):
        def one(t, _):
            self.each(t, lambda c: c.start())
            return 0

        lax.fori_loop(0, TILES, one, 0)

    def wait(self, t):
        self.each(t, lambda c: c.wait())


def framed(ref):
    return ref.reshape(ref.shape[0] // STRIDE, STRIDE, NZ)


def dm_copies(dm, before, after, sem, dm_ref, own, place, count):
    src, dst = pl.ds(own, count), pl.ds(place, count)
    d3 = framed(dm_ref)
    return [
        pltpu.make_async_copy(dm.at[src], d3.at[dst, pl.ds(8, NY)], sem),
        pltpu.make_async_copy(before.at[5, src], d3.at[dst, pl.ds(0, 8)], sem),
        pltpu.make_async_copy(after.at[5, src], d3.at[dst, pl.ds(104, 8)], sem),
    ]


def out_copies(o_ref, planes, outs, sem, own, place, count):
    o4 = o_ref.reshape(5, planes, STRIDE, NZ)
    src, dst, mid = pl.ds(place, count), pl.ds(own, count), pl.ds(8, NY)
    density, momentum, energy = outs
    return [
        pltpu.make_async_copy(o4.at[0, src, mid], density.at[dst], sem),
        pltpu.make_async_copy(o4.at[pl.ds(1, 3), src, mid], momentum.at[:, dst], sem),
        pltpu.make_async_copy(o4.at[4, src, mid], energy.at[dst], sem),
    ]


def start_all(copies):
    for c in copies:
        c.start()


def wait_all(copies):
    for c in copies:
        c.wait()


def sums_copy(t_ref, base, count, out, sem):
    return pltpu.make_async_copy(framed(t_ref).at[pl.ds(base, count), pl.ds(0, FRAME)], out, sem)


def inner_kernel(dest, density, momentum, energy, dm, y_before, y_after,
                 out_density, out_momentum, out_energy, out_sums, send,
                 q_ref, s_ref, o_ref, dm_ref, t_ref, x_ref, y_ref, sems, sem, out_sem):
    tiles = Tiles(q_ref, sems, [((density, momentum, energy), y_before, y_after, pl.ds(1, 22), pl.ds(0, 22))])
    tiles.start()
    copies = dm_copies(dm, y_before, y_after, sem, dm_ref, 4, 0, 16)
    start_all(copies)
    clear(send)
    x_sweep(q_ref, s_ref, 16, ((0, 0, 16),), tiles.wait)
    wait_all(copies)
    yz_sweep(s_ref, dm_ref, o_ref, t_ref, 16, 0)
    leaving = out_copies(o_ref, 16, (out_density, out_momentum, out_energy), out_sem, 4, 0, 16)
    leaving.append(sums_copy(t_ref, 0, 16, out_sums, out_sem))
    start_all(leaving)
    smooth(lambda p, row: t_ref[pl.ds((2 + p) * STRIDE + row, 8), :], dest, x_ref, y_ref, send, 0)
    wait_all(leaving)


def middle_kernel(dest, density, momentum, energy, dm, y_before, y_after, sums_inner,
                  in_density, in_momentum, in_energy,
                  out_density, out_momentum, out_energy, out_sums, send,
                  q_ref, s_ref, o_ref, dm_ref, t_ref, x_ref, y_ref, sems, sem, out_sem):
    tiles = Tiles(q_ref, sems, [((density, momentum, energy), y_before, y_after, pl.ds(17, 14), pl.ds(0, 14))])
    tiles.start()
    copies = dm_copies(dm, y_before, y_after, sem, dm_ref, 20, 0, 8)
    copies.append(pltpu.make_async_copy(
        sums_inner.at[pl.ds(10, 6)], framed(t_ref).at[pl.ds(0, 6), pl.ds(0, FRAME)], sem))
    start_all(copies)
    clear(send)
    x_sweep(q_ref, s_ref, 8, ((0, 0, 8),), tiles.wait)
    wait_all(copies)
    yz_sweep(s_ref, dm_ref, o_ref, t_ref, 8, 6)
    leaving = out_copies(o_ref, 8, (out_density, out_momentum, out_energy), out_sem, 20, 0, 8)
    leaving.append(sums_copy(t_ref, 6, 8, out_sums, out_sem))
    start_all(leaving)
    smooth(lambda p, row: t_ref[pl.ds(p * STRIDE + row, 8), :], dest, x_ref, y_ref, send, 0)
    wait_all(leaving)


def outer_kernel(density, momentum, energy, dm, y_before, y_after, x_before, x_after, c_before, c_after,
                 in_density, in_momentum, in_energy,
                 out_density, out_momentum, out_energy, out_sums, to_next, to_prev,
                 q_ref, s_ref, o_ref, dm_ref, t_ref, sems, sem, out_sem):
    fields = (density, momentum, energy)
    tiles = Tiles(q_ref, sems, [
        (fields, y_before, y_after, pl.ds(25, 7), pl.ds(0, 7)),
        ((x_after,), c_before, c_after, pl.ds(0, 3), pl.ds(7, 3)),
        ((x_before,), c_before.at[:, pl.ds(3, 3)], c_after.at[:, pl.ds(3, 3)], pl.ds(0, 3), pl.ds(10, 3)),
        (fields, y_before, y_after, pl.ds(0, 7), pl.ds(13, 7)),
    ])
    tiles.start()
    copies = (dm_copies(dm, y_before, y_after, sem, dm_ref, 28, 0, 4)
              + dm_copies(dm, y_before, y_after, sem, dm_ref, 0, 4, 4))
    start_all(copies)
    x_sweep(q_ref, s_ref, 8, ((0, 0, 4), (10, 4, 4)), tiles.wait)
    wait_all(copies)
    yz_sweep(s_ref, dm_ref, o_ref, t_ref, 8, 0)
    outs = (out_density, out_momentum, out_energy)
    leaving = out_copies(o_ref, 8, outs, out_sem, 28, 0, 4) + out_copies(o_ref, 8, outs, out_sem, 0, 4, 4)
    leaving.append(sums_copy(t_ref, 0, 8, out_sums, out_sem))
    leaving.append(sums_copy(t_ref, 2, 2, to_next, out_sem))
    leaving.append(sums_copy(t_ref, 4, 2, to_prev, out_sem))
    start_all(leaving)
    wait_all(leaving)


def rest_kernel(dest, sums_inner, sums_middle, sums_outer, from_prev, from_next, send, w_ref, x_ref, y_ref, sem):
    def part(src, own, place, count):
        return pltpu.make_async_copy(src.at[pl.ds(own, count)], w_ref.at[pl.ds(place, count)], sem)

    copies = [
        part(from_prev, 0, 0, 2),
        part(sums_outer, 4, 2, 4),
        part(sums_inner, 0, 6, 6),
        part(sums_middle, 2, 12, 6),
        part(sums_outer, 0, 18, 4),
        part(from_next, 0, 22, 2),
    ]
    start_all(copies)
    clear(send)
    wait_all(copies)
    for row, base in ((0, 0), (8, 12)):
        smooth(lambda p, r: w_ref[base + p, pl.ds(r, 8), :], dest, x_ref, y_ref, send, row)


ANY = pl.BlockSpec(memory_space=pl.ANY)
SMEM = pl.BlockSpec(memory_space=pltpu.SMEM)
VMEM = pl.BlockSpec(memory_space=pltpu.VMEM)
F32 = jnp.float32


def shape(*dims):
    return jax.ShapeDtypeStruct(dims, F32)


def params():
    return pltpu.CompilerParams(vmem_limit_bytes=VMEM_LIMIT)


def cost(planes):
    return pl.CostEstimate(flops=planes * 40_000_000_000, bytes_accessed=planes * 600_000, transcendentals=0)


def main_scratch(planes, held, sums):
    return [
        pltpu.VMEM((5, held, FRAME, NZ), F32),
        pltpu.VMEM((5 * planes * STRIDE, NZ), F32),
        pltpu.VMEM((5 * planes * STRIDE, NZ), F32),
        pltpu.VMEM((planes * STRIDE, NZ), F32),
        pltpu.VMEM((sums * STRIDE, NZ), F32),
    ]


def semaphores():
    return [pltpu.SemaphoreType.DMA((TILES,)), pltpu.SemaphoreType.DMA, pltpu.SemaphoreType.DMA]


def smooth_scratch():
    return [pltpu.VMEM((8 * FRAME, NZ), F32), pltpu.VMEM((8 * NY, NZ), F32)]


FIELD_SHAPES = (shape(NX, NY, NZ), shape(3, NX, NY, NZ), shape(NX, NY, NZ))


def shifted(value, axis, by):
    size = lax.axis_size(axis)
    return lax.ppermute(value, axis, [(i, (i + by) % size) for i in range(size)])


def body(density, momentum, energy, dm_density, box_dest):
    dest = box_dest[0, 0, :, 0]
    fields = (density[None], momentum, energy[None])

    def cut(arrays, planes, rows):
        return jnp.concatenate([a[:, planes[0]:planes[1], rows[0]:rows[1]] for a in arrays], axis=0)

    y_before = shifted(cut(fields + (dm_density[None],), (0, NX), (NY - 8, NY)), "grp", 1)
    y_after = shifted(cut(fields + (dm_density[None],), (0, NX), (0, 8)), "grp", -1)
    x_before = shifted(cut(fields, (NX - 3, NX), (0, NY)), "box", 1)
    x_after = shifted(cut(fields, (0, 3), (0, NY)), "box", -1)

    def exchange(send, planes):
        return lax.all_to_all(send.reshape(16, 2, planes, 1024), "box", split_axis=0, concat_axis=0, tiled=True)

    inner = pl.pallas_call(
        inner_kernel,
        out_shape=FIELD_SHAPES + (shape(16, FRAME, NZ), shape(32, 8, 1024)),
        in_specs=[SMEM] + [ANY] * 6,
        out_specs=[ANY] * 4 + [VMEM],
        scratch_shapes=main_scratch(16, 22, 16) + smooth_scratch() + semaphores(),
        compiler_params=params(),
        cost_estimate=cost(16),
        name="inner",
    )(dest, density, momentum, energy, dm_density, y_before, y_after)
    *made, sums_inner, send_inner = inner
    got_inner = exchange(send_inner, 8)

    x_before, x_after, sums_inner = lax.optimization_barrier((x_before, x_after, sums_inner))
    x_both = jnp.concatenate([x_after, x_before], axis=1)
    c_before = shifted(x_both[:, :, NY - 8:], "grp", 1)
    c_after = shifted(x_both[:, :, :8], "grp", -1)
    middle = pl.pallas_call(
        middle_kernel,
        out_shape=FIELD_SHAPES + (shape(8, FRAME, NZ), shape(32, 8, 1024)),
        in_specs=[SMEM] + [ANY] * 10,
        out_specs=[ANY] * 4 + [VMEM],
        scratch_shapes=main_scratch(8, 14, 14) + smooth_scratch() + semaphores(),
        input_output_aliases={8: 0, 9: 1, 10: 2},
        compiler_params=params(),
        cost_estimate=cost(8),
        name="middle",
    )(dest, density, momentum, energy, dm_density, y_before, y_after, sums_inner, *made)
    *made, sums_middle, send_middle = middle
    send_middle, got_inner = lax.optimization_barrier((send_middle, got_inner))
    got_middle = exchange(send_middle, 8)

    outer = pl.pallas_call(
        outer_kernel,
        out_shape=FIELD_SHAPES + (shape(8, FRAME, NZ), shape(2, FRAME, NZ), shape(2, FRAME, NZ)),
        in_specs=[ANY] * 13,
        out_specs=[ANY] * 6,
        scratch_shapes=main_scratch(8, 20, 8) + semaphores(),
        input_output_aliases={10: 0, 11: 1, 12: 2},
        compiler_params=params(),
        cost_estimate=cost(8),
        name="outer",
    )(density, momentum, energy, dm_density, y_before, y_after, x_before, x_after, c_before, c_after, *made)
    new_density, new_momentum, new_energy, sums_outer, to_next, to_prev = outer
    from_prev = shifted(to_next, "box", 1)
    from_next = shifted(to_prev, "box", -1)
    send_rest = pl.pallas_call(
        rest_kernel,
        out_shape=shape(32, 16, 1024),
        in_specs=[SMEM] + [ANY] * 5,
        out_specs=VMEM,
        scratch_shapes=[pltpu.VMEM((24, FRAME, NZ), F32)] + smooth_scratch() + [pltpu.SemaphoreType.DMA],
        compiler_params=params(),
        cost_estimate=cost(2),
        name="rest",
    )(dest, sums_inner, sums_middle, sums_outer, from_prev, from_next)
    send_rest, got_middle = lax.optimization_barrier((send_rest, got_middle))
    got_rest = exchange(send_rest, 16)
    kd = jnp.concatenate([got_rest[:, :, :8], got_inner, got_middle, got_rest[:, :, 8:]], axis=2)
    return (new_density, new_momentum, new_energy, kd[None, None])


def solution(mesh):
    in_specs = (
        P("box", "grp", None),
        P(None, "box", "grp", None),
        P("box", "grp", None),
        P("box", "grp", None),
        P("grp", "box", None, None),
    )
    out_specs = (
        P("box", "grp", None),
        P(None, "box", "grp", None),
        P("box", "grp", None),
        P("grp", "box", None, None, None, None),
    )
    return jax.shard_map(body, mesh=mesh, in_specs=in_specs, out_specs=out_specs, check_vma=False)
```

```python
import functools
import math

import jax
import jax.numpy as jnp
from jax import lax
from jax.experimental import pallas as pl
from jax.experimental.pallas import tpu as pltpu
from jax.sharding import PartitionSpec as P

BOX = 32
BOX_Y = 3
BOX_Z = 4
NX = 32
NY = 96
NZ = 128
FRAME = 112
TILES = FRAME // 8
STRIDE = 120
STEP = 0.03
SCALES = (1.0, STEP, STEP, STEP, 2.0 * STEP * STEP)
UNSCALES = (1.0, 1.0 / STEP, 1.0 / STEP, 1.0 / STEP, 1.0 / (2.0 * STEP * STEP))
SOUND = math.sqrt(5.0 / 3.0)
TINY = 1e-30
COST = 1_100_000_000
VMEM_LIMIT = 56 * 1024 * 1024


def limit(value, other):
    bound = jnp.abs(other + other)
    return jnp.maximum(jnp.minimum(value, bound), -bound)


def deviation(d_prev, d_here, d_next):
    value = 0.5 * d_here + (d_prev - d_next) * (1.0 / 12.0)
    return jnp.minimum(jnp.maximum(value, jnp.minimum(d_here, 0.0)), jnp.maximum(d_here, 0.0))


def invert(x):
    return 1.0 / x


def state_of(u, normal):
    inverse = invert(u[0])
    squares = u[1] * u[1] + u[2] * u[2] + u[3] * u[3]
    pressure = u[4] - squares * inverse
    third = pressure * (1.0 / 3.0)
    velocity = u[normal] * inverse
    ratio = jnp.maximum(third * inverse, TINY)
    reach = jnp.abs(velocity) + SOUND * (ratio * lax.rsqrt(ratio))
    return velocity, third, reach


def flux(left, right, normal):
    v_left, p_left, reach_left = state_of(left, normal)
    v_right, p_right, reach_right = state_of(right, normal)
    reach = jnp.maximum(reach_left, reach_right)
    up = v_left + reach
    down = v_right - reach
    out = [left[f] * up + right[f] * down for f in range(5)]
    out[normal] = out[normal] + (p_left + p_right)
    work = p_left * v_left + p_right * v_right
    out[4] = out[4] + (work + work)
    return out


class Line:
    def __init__(self, normal):
        self.normal = normal
        self.q = []
        self.d = []
        self.dl = None
        self.er = None
        self.flux = None

    def load(self, q, carry):
        self.q = list(q)
        self.d = [carry[0:5], carry[5:10]]
        self.dl = carry[10:15]
        self.er = carry[15:20]
        self.flux = carry[20:25]

    def carry(self):
        return tuple(self.d[0]) + tuple(self.d[1]) + tuple(self.dl) + tuple(self.er) + tuple(self.flux)

    def push(self, new):
        q, d = self.q, self.d
        out = None
        if q:
            d0 = [a - b for a, b in zip(new, q[-1])]
            if len(d) >= 2:
                d2, d1 = d[-2], d[-1]
                dr = [deviation(*t) for t in zip(d2, d1, d0)]
                if self.dl is not None:
                    here = q[-2]
                    right = [c + limit(r, l) for c, r, l in zip(here, dr, self.dl)]
                    if self.er is not None:
                        left = [c + limit(l, r) for c, r, l in zip(here, dr, self.dl)]
                        now = flux(self.er, left, self.normal)
                        if self.flux is not None:
                            out = [c - (a - b) for c, a, b in zip(q[-3], now, self.flux)]
                        self.flux = now
                    self.er = right
                self.dl = [r - s for r, s in zip(dr, d1)]
            d.append(d0)
            self.d = d[-2:]
        q.append(new)
        self.q = q[-3:]
        return out


def turn(x, shift):
    return pltpu.roll(x, shift % NZ, 1)


def sweep_lanes(q):
    d = [turn(x, -1) - x for x in q]
    dr = [deviation(turn(x, 1), x, turn(x, -1)) for x in d]
    dl = [turn(r - x, 1) for r, x in zip(dr, d)]
    right = [c + limit(r, l) for c, r, l in zip(q, dr, dl)]
    left = [turn(c + limit(l, r), -1) for c, r, l in zip(q, dr, dl)]
    now = flux(right, left, 3)
    return [c - (f - turn(f, 1)) for c, f in zip(q, now)]


def lane_sum(t):
    pair = t + turn(t, -1)
    return t + turn(pair, 2) + turn(pair, -1)


def x_lines(segments, read, write):
    for base, out_base, count in segments:
        line = Line(1)
        for i in range(count + 6):
            new = [read(f, base + i) * SCALES[f] if f else read(f, base + i) for f in range(5)]
            out = line.push(new)
            if out is not None:
                for f in range(5):
                    write(f, out_base + i - 6, out[f])


def x_sweep(q_ref, s_ref, planes, segments, tiles, ready, place):
    def tile(t, _):
        ready(t)
        row = pl.multiple_of(t * 8, 8)
        to = pl.multiple_of(place(t), 8)

        def write(f, x, value):
            s_ref[pl.ds((f * planes + x) * STRIDE + to, 8), :] = value

        x_lines(segments, lambda f, i: q_ref[f, i, pl.ds(row, 8), :], write)
        return 0

    lax.fori_loop(0, tiles, tile, 0)


ROWS_STEP = 10


def yz_sweep(s_ref, dm_ref, o_ref, t_ref, planes, ready, done):
    def group(g, _):
        ready(g)

        def at(f, row):
            return pl.ds((f * planes + g * 8) * STRIDE + row, 8, stride=STRIDE)

        def rows(row):
            return [s_ref[at(f, row), :] for f in range(5)]

        first = Line(2)
        for row in range(3, 9):
            first.push(rows(row))

        def some(b, carry):
            line = Line(2)
            base = 9 + b * ROWS_STEP
            line.load([rows(base - 3), rows(base - 2), rows(base - 1)], carry)
            ahead = [rows(base + r) for r in range(ROWS_STEP)]
            for r in range(ROWS_STEP):
                swept = line.push(ahead[r])
                final = sweep_lanes(swept)
                row = base + r - 3
                for f in range(5):
                    o_ref[at(f, row), :] = final[f] * UNSCALES[f] if f else final[f]
                total = final[0] + dm_ref[at(0, row), :]
                t_ref[at(0, row), :] = lane_sum(total)
            return line.carry()

        lax.fori_loop(0, 100 // ROWS_STEP, some, first.carry())
        done(g)
        return 0

    lax.fori_loop(0, planes // 8, group, 0)


def smooth(planes, dest_ref, x_ref, y_ref, send_ref, send_row):
    def x_tile(t, _):
        row = pl.multiple_of(t * 8, 8)
        values = [planes(p, row) for p in range(12)]
        pairs = [values[p] + values[p + 1] for p in range(11)]
        for p in range(8):
            x_ref[pl.ds(p * FRAME + row, 8), :] = pairs[p] + pairs[p + 2] + values[p + 4]
        return 0

    lax.fori_loop(0, TILES, x_tile, 0)

    def y_plane(p, _):
        for t in range(NY // 8):
            start = p * FRAME + 8 + 8 * t
            parts = [x_ref[pl.ds(start + k, 8), :] for k in range(-2, 3)]
            total = ((parts[0] + parts[1]) + (parts[3] + parts[4])) + parts[2]
            y_ref[pl.ds(p * NY + 8 * t, 8), :] = total * (1.0 / 125.0)
        return 0

    lax.fori_loop(0, 8, y_plane, 0)

    places = []
    dests = [dest_ref[k] for k in range(12)]
    for k in range(12):
        slot = jnp.int32(0)
        for other in range(k):
            slot = slot + (dests[other] == dests[k]).astype(jnp.int32)
        places.append(dests[k] * 2 + slot)

    quarter = lax.broadcasted_iota(jnp.int32, (8, NZ), 1) // BOX

    def pick(values):
        out = values[3]
        for b in range(3):
            out = jnp.where(quarter == b, values[b], out)
        return out

    for by in range(BOX_Y):
        for m in range(8):
            s = [y_ref[pl.ds(by * BOX + 4 * m + q, 8, stride=NY), :] for q in range(4)]
            moved = []
            for k in range(4):
                mixed = pick([s[(b + k) % 4] for b in range(4)])
                moved.append(turn(mixed, k * BOX) if k else mixed)
            for bz in range(4):
                out = pick([moved[(q - bz) % 4] for q in range(4)])
                send_ref[places[by * 4 + bz], pl.ds(send_row, 8), pl.ds(m * NZ, NZ)] = out


def clear(send_ref):
    def one(i, _):
        send_ref[i] = jnp.zeros(send_ref.shape[1:], jnp.float32)
        return 0

    lax.fori_loop(0, send_ref.shape[0], one, 0)


def rows_of(t):
    return pl.ds(pl.multiple_of(t * 8, 8), 8)


class Tiles:
    def __init__(self, q_ref, sems, parts):
        self.q_ref, self.sems, self.parts = q_ref, sems, parts

    def copies(self, t, kind):
        out = []
        for own, before, after, src, dst in self.parts:
            q = self.q_ref.at[:, dst, rows_of(t)]
            sem = self.sems.at[t]
            if kind == "before":
                out.append(pltpu.make_async_copy(before.at[pl.ds(0, 5), src], q, sem))
            elif kind == "after":
                out.append(pltpu.make_async_copy(after.at[pl.ds(0, 5), src], q, sem))
            elif len(own) == 1:
                out.append(pltpu.make_async_copy(own[0].at[:, src, rows_of(t - 1)], q, sem))
            else:
                density, momentum, energy = own
                rows = rows_of(t - 1)
                place = self.q_ref.at
                out.append(pltpu.make_async_copy(density.at[src, rows], place[0, dst, rows_of(t)], sem))
                out.append(pltpu.make_async_copy(momentum.at[:, src, rows], place[pl.ds(1, 3), dst, rows_of(t)], sem))
                out.append(pltpu.make_async_copy(energy.at[src, rows], place[4, dst, rows_of(t)], sem))
        return out

    def each(self, t, act):
        @pl.when(t == 0)
        def _():
            for c in self.copies(t, "before"):
                act(c)

        @pl.when(t == TILES - 1)
        def _():
            for c in self.copies(t, "after"):
                act(c)

        @pl.when((t > 0) & (t < TILES - 1))
        def _():
            for c in self.copies(t, "own"):
                act(c)

    def start(self):
        def one(t, _):
            self.each(t, lambda c: c.start())
            return 0

        lax.fori_loop(0, TILES, one, 0)

    def wait(self, t):
        self.each(t, lambda c: c.wait())


def framed(ref):
    return ref.reshape(ref.shape[0] // STRIDE, STRIDE, NZ)


def dm_copies(dm, before, after, sem, dm_ref, own, place, count):
    src, dst = pl.ds(own, count), pl.ds(place, count)
    d3 = framed(dm_ref)
    return [
        pltpu.make_async_copy(dm.at[src], d3.at[dst, pl.ds(8, NY)], sem),
        pltpu.make_async_copy(before.at[5, src], d3.at[dst, pl.ds(0, 8)], sem),
        pltpu.make_async_copy(after.at[5, src], d3.at[dst, pl.ds(104, 8)], sem),
    ]


def out_copies(o_ref, planes, outs, sem, own, place, count):
    o4 = o_ref.reshape(5, planes, STRIDE, NZ)
    src, dst, mid = pl.ds(place, count), pl.ds(own, count), pl.ds(8, NY)
    density, momentum, energy = outs
    return [
        pltpu.make_async_copy(o4.at[0, src, mid], density.at[dst], sem),
        pltpu.make_async_copy(o4.at[pl.ds(1, 3), src, mid], momentum.at[:, dst], sem),
        pltpu.make_async_copy(o4.at[4, src, mid], energy.at[dst], sem),
    ]


def start_all(copies):
    for c in copies:
        c.start()


def wait_all(copies):
    for c in copies:
        c.wait()


def sums_copy(t_ref, base, count, out, sem):
    return pltpu.make_async_copy(framed(t_ref).at[pl.ds(base, count), pl.ds(0, FRAME)], out, sem)


def pack_kernel(density, momentum, energy, dm, y_last, y_first, x_last, x_first, c_ll, c_lf, c_fl, c_ff, sem):
    copies = []

    def fields(out, planes, rows):
        copies.append(pltpu.make_async_copy(density.at[planes, rows], out.at[0], sem))
        copies.append(pltpu.make_async_copy(momentum.at[:, planes, rows], out.at[pl.ds(1, 3)], sem))
        copies.append(pltpu.make_async_copy(energy.at[planes, rows], out.at[4], sem))

    ends = (pl.ds(NY - 8, 8), pl.ds(0, 8))
    for out, rows in zip((y_last, y_first), ends):
        fields(out, pl.ds(0, NX), rows)
        copies.append(pltpu.make_async_copy(dm.at[:, rows], out.at[5], sem))
    for x_out, c_out, planes in ((x_last, (c_ll, c_lf), pl.ds(NX - 3, 3)), (x_first, (c_fl, c_ff), pl.ds(0, 3))):
        fields(x_out, planes, pl.ds(0, NY))
        for n, rows in enumerate(ends):
            fields(c_out[n], planes, rows)
    start_all(copies)
    wait_all(copies)


WIDE = 24


def x_kernel(density, momentum, energy, out, q_ref, s_ref, sems, out_sem):
    held = pl.ds(1, WIDE + 6)

    def copies(t):
        rows = rows_of(t)
        return [
            pltpu.make_async_copy(density.at[held, rows], q_ref.at[0, :, rows], sems.at[t]),
            pltpu.make_async_copy(momentum.at[:, held, rows], q_ref.at[pl.ds(1, 3), :, rows], sems.at[t]),
            pltpu.make_async_copy(energy.at[held, rows], q_ref.at[4, :, rows], sems.at[t]),
        ]

    def leaving(t):
        return pltpu.make_async_copy(s_ref.at[:, :, rows_of(t)], out.at[:, :, rows_of(t)], out_sem)

    def begin(t, _):
        start_all(copies(t))
        return 0

    def tile(t, _):
        wait_all(copies(t))
        rows = rows_of(t)

        def write(f, x, value):
            s_ref[f, x, rows, :] = value

        x_lines(((0, 0, WIDE),), lambda f, i: q_ref[f, i, rows, :], write)
        leaving(t).start()
        return 0

    def end(t, _):
        leaving(t).wait()
        return 0

    lax.fori_loop(0, NY // 8, begin, 0)
    lax.fori_loop(0, NY // 8, tile, 0)
    lax.fori_loop(0, NY // 8, end, 0)


def inner_kernel(dest, swept, dm, y_before, y_after,
                 out_density, out_momentum, out_energy, out_sums, send,
                 q_ref, s_ref, o_ref, dm_ref, t_ref, x_ref, y_ref, sems, sem, out_sem):
    held = pl.ds(1, WIDE + 6)
    s4 = s_ref.reshape(5, WIDE, STRIDE, NZ)
    outs = (out_density, out_momentum, out_energy)

    def swept_copy(g):
        planes = pl.ds(g * 8, 8)
        return pltpu.make_async_copy(swept.at[:, planes], s4.at[:, planes, pl.ds(8, NY)], sems.at[g])

    def leaving(g):
        return out_copies(o_ref, WIDE, outs, out_sem, 4 + g * 8, g * 8, 8)

    halo = [
        pltpu.make_async_copy(y_before.at[pl.ds(0, 5), held], q_ref.at[:, :, pl.ds(0, 8)], sem),
        pltpu.make_async_copy(y_after.at[pl.ds(0, 5), held], q_ref.at[:, :, pl.ds(8, 8)], sem),
    ] + dm_copies(dm, y_before, y_after, sem, dm_ref, 4, 0, WIDE)
    start_all(halo)
    for g in range(WIDE // 8):
        swept_copy(g).start()
    clear(send)
    wait_all(halo)
    x_sweep(q_ref, s_ref, WIDE, ((0, 0, WIDE),), 2, lambda t: None, lambda t: t * 104)
    yz_sweep(s_ref, dm_ref, o_ref, t_ref, WIDE, lambda g: swept_copy(g).wait(), lambda g: start_all(leaving(g)))
    sums = sums_copy(t_ref, 0, WIDE, out_sums, sem)
    sums.start()
    for row, base in ((0, 2), (8, 10)):
        smooth(lambda p, r: t_ref[pl.ds((base + p) * STRIDE + r, 8), :], dest, x_ref, y_ref, send, row)
    sums.wait()
    for g in range(WIDE // 8):
        wait_all(leaving(g))


def outer_kernel(density, momentum, energy, dm, y_before, y_after, x_before, x_after, c_bb, c_ba, c_ab, c_aa,
                 in_density, in_momentum, in_energy,
                 out_density, out_momentum, out_energy, out_sums, to_next, to_prev,
                 q_ref, s_ref, o_ref, dm_ref, t_ref, sems, sem, out_sem):
    fields = (density, momentum, energy)
    tiles = Tiles(q_ref, sems, [
        (fields, y_before, y_after, pl.ds(25, 7), pl.ds(0, 7)),
        ((x_after,), c_ab, c_aa, pl.ds(0, 3), pl.ds(7, 3)),
        ((x_before,), c_bb, c_ba, pl.ds(0, 3), pl.ds(10, 3)),
        (fields, y_before, y_after, pl.ds(0, 7), pl.ds(13, 7)),
    ])
    tiles.start()
    copies = (dm_copies(dm, y_before, y_after, sem, dm_ref, 28, 0, 4)
              + dm_copies(dm, y_before, y_after, sem, dm_ref, 0, 4, 4))
    start_all(copies)
    x_sweep(q_ref, s_ref, 8, ((0, 0, 4), (10, 4, 4)), TILES, tiles.wait, lambda t: t * 8)
    wait_all(copies)
    yz_sweep(s_ref, dm_ref, o_ref, t_ref, 8, lambda g: None, lambda g: None)
    outs = (out_density, out_momentum, out_energy)
    leaving = out_copies(o_ref, 8, outs, out_sem, 28, 0, 4) + out_copies(o_ref, 8, outs, out_sem, 0, 4, 4)
    leaving.append(sums_copy(t_ref, 0, 8, out_sums, out_sem))
    leaving.append(sums_copy(t_ref, 2, 2, to_next, out_sem))
    leaving.append(sums_copy(t_ref, 4, 2, to_prev, out_sem))
    start_all(leaving)
    wait_all(leaving)


def rest_kernel(dest, sums_inner, sums_outer, from_prev, from_next, send, w_ref, x_ref, y_ref, sem):
    def part(src, own, place, count):
        return pltpu.make_async_copy(src.at[pl.ds(own, count)], w_ref.at[pl.ds(place, count)], sem)

    copies = [
        part(from_prev, 0, 0, 2),
        part(sums_outer, 4, 2, 4),
        part(sums_inner, 0, 6, 6),
        part(sums_inner, 18, 12, 6),
        part(sums_outer, 0, 18, 4),
        part(from_next, 0, 22, 2),
    ]
    start_all(copies)
    clear(send)
    wait_all(copies)
    for row, base in ((0, 0), (8, 12)):
        smooth(lambda p, r: w_ref[base + p, pl.ds(r, 8), :], dest, x_ref, y_ref, send, row)


ANY = pl.BlockSpec(memory_space=pl.ANY)
SMEM = pl.BlockSpec(memory_space=pltpu.SMEM)
VMEM = pl.BlockSpec(memory_space=pltpu.VMEM)
F32 = jnp.float32


def shape(*dims):
    return jax.ShapeDtypeStruct(dims, F32)


def params():
    return pltpu.CompilerParams(vmem_limit_bytes=VMEM_LIMIT)


def cost(micros):
    return pl.CostEstimate(flops=int(micros * COST), bytes_accessed=0, transcendentals=0)


def main_scratch(planes, held, rows):
    return [
        pltpu.VMEM((5, held, rows, NZ), F32),
        pltpu.VMEM((5 * planes * STRIDE, NZ), F32),
        pltpu.VMEM((5 * planes * STRIDE, NZ), F32),
        pltpu.VMEM((planes * STRIDE, NZ), F32),
        pltpu.VMEM((planes * STRIDE, NZ), F32),
    ]


def semaphores():
    return [pltpu.SemaphoreType.DMA((TILES,)), pltpu.SemaphoreType.DMA, pltpu.SemaphoreType.DMA]


def smooth_scratch():
    return [pltpu.VMEM((8 * FRAME, NZ), F32), pltpu.VMEM((8 * NY, NZ), F32)]


FIELD_SHAPES = (shape(NX, NY, NZ), shape(3, NX, NY, NZ), shape(NX, NY, NZ))


def shifted(value, axis, by):
    size = lax.axis_size(axis)
    return lax.ppermute(value, axis, [(i, (i + by) % size) for i in range(size)])


def diagonal(value, by_box, by_grp):
    boxes, grps = lax.axis_size("box"), lax.axis_size("grp")
    pairs = []
    for i in range(boxes):
        for j in range(grps):
            pairs.append((i * grps + j, (i + by_box) % boxes * grps + (j + by_grp) % grps))
    return lax.ppermute(value, ("box", "grp"), pairs)


def body(density, momentum, energy, dm_density, box_dest):
    dest = box_dest[0, 0, :, 0]
    fields = (density, momentum, energy)
    halo_shapes = (shape(6, NX, 8, NZ),) * 2 + (shape(5, 3, NY, NZ),) * 2 + (shape(5, 3, 8, NZ),) * 4
    y_last, y_first, x_last, x_first, c_ll, c_lf, c_fl, c_ff = pl.pallas_call(
        pack_kernel,
        out_shape=halo_shapes,
        in_specs=[ANY] * 4,
        out_specs=[ANY] * 8,
        scratch_shapes=[pltpu.SemaphoreType.DMA],
        cost_estimate=cost(2),
        name="pack",
    )(density, momentum, energy, dm_density)
    y_before = shifted(y_last, "grp", 1)
    y_after = shifted(y_first, "grp", -1)
    x_before = shifted(x_last, "box", 1)
    x_after = shifted(x_first, "box", -1)
    c_bb = diagonal(c_ll, 1, 1)
    c_ba = diagonal(c_lf, 1, -1)
    c_ab = diagonal(c_fl, -1, 1)
    c_aa = diagonal(c_ff, -1, -1)

    swept = pl.pallas_call(
        x_kernel,
        out_shape=shape(5, WIDE, NY, NZ),
        in_specs=[ANY] * 3,
        out_specs=ANY,
        scratch_shapes=[
            pltpu.VMEM((5, WIDE + 6, NY, NZ), F32), pltpu.VMEM((5, WIDE, NY, NZ), F32),
            pltpu.SemaphoreType.DMA((NY // 8,)), pltpu.SemaphoreType.DMA],
        compiler_params=params(),
        cost_estimate=cost(9),
        name="x_own",
    )(*fields)

    def exchange(send, planes):
        return lax.all_to_all(send.reshape(16, 2, planes, 1024), "box", split_axis=0, concat_axis=0, tiled=True)

    inner = pl.pallas_call(
        inner_kernel,
        out_shape=FIELD_SHAPES + (shape(WIDE, FRAME, NZ), shape(32, 16, 1024)),
        in_specs=[SMEM] + [ANY] * 4,
        out_specs=[ANY] * 4 + [VMEM],
        scratch_shapes=main_scratch(WIDE, WIDE + 6, 16) + smooth_scratch() + semaphores(),
        compiler_params=params(),
        cost_estimate=cost(33),
        name="inner",
    )(dest, swept, dm_density, y_before, y_after)
    *made, sums_inner, send_inner = inner
    got_inner = exchange(send_inner, 16)

    outer = pl.pallas_call(
        outer_kernel,
        out_shape=FIELD_SHAPES + (shape(8, FRAME, NZ), shape(2, FRAME, NZ), shape(2, FRAME, NZ)),
        in_specs=[ANY] * 15,
        out_specs=[ANY] * 6,
        scratch_shapes=main_scratch(8, 20, FRAME) + semaphores(),
        input_output_aliases={12: 0, 13: 1, 14: 2},
        compiler_params=params(),
        cost_estimate=cost(14),
        name="outer",
    )(*fields, dm_density, y_before, y_after, x_before, x_after, c_bb, c_ba, c_ab, c_aa, *made)
    new_density, new_momentum, new_energy, sums_outer, to_next, to_prev = outer
    from_prev = shifted(to_next, "box", 1)
    from_next = shifted(to_prev, "box", -1)
    send_rest = pl.pallas_call(
        rest_kernel,
        out_shape=shape(32, 16, 1024),
        in_specs=[SMEM] + [ANY] * 4,
        out_specs=VMEM,
        scratch_shapes=[pltpu.VMEM((24, FRAME, NZ), F32)] + smooth_scratch() + [pltpu.SemaphoreType.DMA],
        compiler_params=params(),
        cost_estimate=cost(5),
        name="rest",
    )(dest, sums_inner, sums_outer, from_prev, from_next)
    send_rest, got_inner = lax.optimization_barrier((send_rest, got_inner))
    got_rest = exchange(send_rest, 16)
    kd = jnp.concatenate([got_rest[:, :, :8], got_inner, got_rest[:, :, 8:]], axis=2)
    return (new_density, new_momentum, new_energy, kd[None, None])


def solution(mesh):
    in_specs = (
        P("box", "grp", None),
        P(None, "box", "grp", None),
        P("box", "grp", None),
        P("box", "grp", None),
        P("grp", "box", None, None),
    )
    out_specs = (
        P("box", "grp", None),
        P(None, "box", "grp", None),
        P("box", "grp", None),
        P("grp", "box", None, None, None, None),
    )
    return jax.shard_map(body, mesh=mesh, in_specs=in_specs, out_specs=out_specs, check_vma=False)
```

```python
import functools
import math

import jax
import jax.numpy as jnp
from jax import lax
from jax.experimental import pallas as pl
from jax.experimental.pallas import tpu as pltpu
from jax.sharding import PartitionSpec as P

BOX = 32
BOX_Y = 3
BOX_Z = 4
NX = 32
NY = 96
NZ = 128
FRAME = 112
TILES = FRAME // 8
STRIDE = 120
STEP = 0.03
SCALES = (1.0, STEP, STEP, STEP, 2.0 * STEP * STEP)
UNSCALES = (1.0, 1.0 / STEP, 1.0 / STEP, 1.0 / STEP, 1.0 / (2.0 * STEP * STEP))
SOUND = math.sqrt(5.0 / 3.0)
TINY = 1e-30
COST = 1_100_000_000
VMEM_LIMIT = 56 * 1024 * 1024


def limit(value, other):
    bound = jnp.abs(other + other)
    return jnp.maximum(jnp.minimum(value, bound), -bound)


def deviation(d_prev, d_here, d_next):
    value = 0.5 * d_here + (d_prev - d_next) * (1.0 / 12.0)
    return jnp.minimum(jnp.maximum(value, jnp.minimum(d_here, 0.0)), jnp.maximum(d_here, 0.0))


def invert(x):
    return 1.0 / x


def state_of(u, normal):
    inverse = invert(u[0])
    squares = u[1] * u[1] + u[2] * u[2] + u[3] * u[3]
    pressure = u[4] - squares * inverse
    third = pressure * (1.0 / 3.0)
    velocity = u[normal] * inverse
    ratio = jnp.maximum(third * inverse, TINY)
    reach = jnp.abs(velocity) + SOUND * (ratio * lax.rsqrt(ratio))
    return velocity, third, reach


def flux(left, right, normal):
    v_left, p_left, reach_left = state_of(left, normal)
    v_right, p_right, reach_right = state_of(right, normal)
    reach = jnp.maximum(reach_left, reach_right)
    up = v_left + reach
    down = v_right - reach
    out = [left[f] * up + right[f] * down for f in range(5)]
    out[normal] = out[normal] + (p_left + p_right)
    work = p_left * v_left + p_right * v_right
    out[4] = out[4] + (work + work)
    return out


class Line:
    def __init__(self, normal):
        self.normal = normal
        self.q = []
        self.d = []
        self.dl = None
        self.er = None
        self.flux = None

    def load(self, q, carry):
        self.q = list(q)
        self.d = [carry[0:5], carry[5:10]]
        self.dl = carry[10:15]
        self.er = carry[15:20]
        self.flux = carry[20:25]

    def carry(self):
        return tuple(self.d[0]) + tuple(self.d[1]) + tuple(self.dl) + tuple(self.er) + tuple(self.flux)

    def push(self, new):
        q, d = self.q, self.d
        out = None
        if q:
            d0 = [a - b for a, b in zip(new, q[-1])]
            if len(d) >= 2:
                d2, d1 = d[-2], d[-1]
                dr = [deviation(*t) for t in zip(d2, d1, d0)]
                if self.dl is not None:
                    here = q[-2]
                    right = [c + limit(r, l) for c, r, l in zip(here, dr, self.dl)]
                    if self.er is not None:
                        left = [c + limit(l, r) for c, r, l in zip(here, dr, self.dl)]
                        now = flux(self.er, left, self.normal)
                        if self.flux is not None:
                            out = [c - (a - b) for c, a, b in zip(q[-3], now, self.flux)]
                        self.flux = now
                    self.er = right
                self.dl = [r - s for r, s in zip(dr, d1)]
            d.append(d0)
            self.d = d[-2:]
        q.append(new)
        self.q = q[-3:]
        return out


def turn(x, shift):
    return pltpu.roll(x, shift % NZ, 1)


def sweep_lanes(q):
    d = [turn(x, -1) - x for x in q]
    dr = [deviation(turn(x, 1), x, turn(x, -1)) for x in d]
    dl = [turn(r - x, 1) for r, x in zip(dr, d)]
    right = [c + limit(r, l) for c, r, l in zip(q, dr, dl)]
    left = [turn(c + limit(l, r), -1) for c, r, l in zip(q, dr, dl)]
    now = flux(right, left, 3)
    return [c - (f - turn(f, 1)) for c, f in zip(q, now)]


def lane_sum(t):
    pair = t + turn(t, -1)
    return t + turn(pair, 2) + turn(pair, -1)


def x_lines(segments, read, write):
    for base, out_base, count in segments:
        line = Line(1)
        for i in range(count + 6):
            new = [read(f, base + i) * SCALES[f] if f else read(f, base + i) for f in range(5)]
            out = line.push(new)
            if out is not None:
                for f in range(5):
                    write(f, out_base + i - 6, out[f])


def x_sweep(q_ref, s_ref, planes, segments, tiles, ready, place):
    def tile(t, _):
        ready(t)
        row = pl.multiple_of(t * 8, 8)
        to = pl.multiple_of(place(t), 8)

        def write(f, x, value):
            s_ref[pl.ds((f * planes + x) * STRIDE + to, 8), :] = value

        x_lines(segments, lambda f, i: q_ref[f, i, pl.ds(row, 8), :], write)
        return 0

    lax.fori_loop(0, tiles, tile, 0)


ROWS_STEP = 10


def yz_sweep(s_ref, dm_ref, o_ref, t_ref, planes, ready, done):
    def group(g, _):
        ready(g)

        def at(f, row):
            return pl.ds((f * planes + g * 8) * STRIDE + row, 8, stride=STRIDE)

        def rows(row):
            return [s_ref[at(f, row), :] for f in range(5)]

        first = Line(2)
        for row in range(3, 9):
            first.push(rows(row))

        def some(b, carry):
            line = Line(2)
            base = 9 + b * ROWS_STEP
            line.load([rows(base - 3), rows(base - 2), rows(base - 1)], carry)
            ahead = [rows(base + r) for r in range(ROWS_STEP)]
            for r in range(ROWS_STEP):
                swept = line.push(ahead[r])
                final = sweep_lanes(swept)
                row = base + r - 3
                for f in range(5):
                    o_ref[at(f, row), :] = final[f] * UNSCALES[f] if f else final[f]
                total = final[0] + dm_ref[at(0, row), :]
                t_ref[at(0, row), :] = lane_sum(total)
            return line.carry()

        lax.fori_loop(0, 100 // ROWS_STEP, some, first.carry())
        done(g)
        return 0

    lax.fori_loop(0, planes // 8, group, 0)


def smooth(planes, dest_ref, x_ref, y_ref, send_ref, send_row):
    def x_tile(t, _):
        row = pl.multiple_of(t * 8, 8)
        values = [planes(p, row) for p in range(12)]
        pairs = [values[p] + values[p + 1] for p in range(11)]
        for p in range(8):
            x_ref[pl.ds(p * FRAME + row, 8), :] = pairs[p] + pairs[p + 2] + values[p + 4]
        return 0

    lax.fori_loop(0, TILES, x_tile, 0)

    def y_plane(p, _):
        for t in range(NY // 8):
            start = p * FRAME + 8 + 8 * t
            parts = [x_ref[pl.ds(start + k, 8), :] for k in range(-2, 3)]
            total = ((parts[0] + parts[1]) + (parts[3] + parts[4])) + parts[2]
            y_ref[pl.ds(p * NY + 8 * t, 8), :] = total * (1.0 / 125.0)
        return 0

    lax.fori_loop(0, 8, y_plane, 0)

    places = []
    dests = [dest_ref[k] for k in range(12)]
    for k in range(12):
        slot = jnp.int32(0)
        for other in range(k):
            slot = slot + (dests[other] == dests[k]).astype(jnp.int32)
        places.append(dests[k] * 2 + slot)

    quarter = lax.broadcasted_iota(jnp.int32, (8, NZ), 1) // BOX

    def pick(values):
        out = values[3]
        for b in range(3):
            out = jnp.where(quarter == b, values[b], out)
        return out

    for by in range(BOX_Y):
        for m in range(8):
            s = [y_ref[pl.ds(by * BOX + 4 * m + q, 8, stride=NY), :] for q in range(4)]
            moved = []
            for k in range(4):
                mixed = pick([s[(b + k) % 4] for b in range(4)])
                moved.append(turn(mixed, k * BOX) if k else mixed)
            for bz in range(4):
                out = pick([moved[(q - bz) % 4] for q in range(4)])
                send_ref[places[by * 4 + bz], pl.ds(send_row, 8), pl.ds(m * NZ, NZ)] = out


def clear(send_ref):
    def one(i, _):
        send_ref[i] = jnp.zeros(send_ref.shape[1:], jnp.float32)
        return 0

    lax.fori_loop(0, send_ref.shape[0], one, 0)


def rows_of(t):
    return pl.ds(pl.multiple_of(t * 8, 8), 8)


class Tiles:
    def __init__(self, q_ref, sems, parts):
        self.q_ref, self.sems, self.parts = q_ref, sems, parts

    def copies(self, t, kind):
        out = []
        for own, before, after, src, dst in self.parts:
            q = self.q_ref.at[:, dst, rows_of(t)]
            sem = self.sems.at[t]
            if kind == "before":
                out.append(pltpu.make_async_copy(before.at[pl.ds(0, 5), src], q, sem))
            elif kind == "after":
                out.append(pltpu.make_async_copy(after.at[pl.ds(0, 5), src], q, sem))
            elif len(own) == 1:
                out.append(pltpu.make_async_copy(own[0].at[:, src, rows_of(t - 1)], q, sem))
            else:
                density, momentum, energy = own
                rows = rows_of(t - 1)
                place = self.q_ref.at
                out.append(pltpu.make_async_copy(density.at[src, rows], place[0, dst, rows_of(t)], sem))
                out.append(pltpu.make_async_copy(momentum.at[:, src, rows], place[pl.ds(1, 3), dst, rows_of(t)], sem))
                out.append(pltpu.make_async_copy(energy.at[src, rows], place[4, dst, rows_of(t)], sem))
        return out

    def each(self, t, act):
        @pl.when(t == 0)
        def _():
            for c in self.copies(t, "before"):
                act(c)

        @pl.when(t == TILES - 1)
        def _():
            for c in self.copies(t, "after"):
                act(c)

        @pl.when((t > 0) & (t < TILES - 1))
        def _():
            for c in self.copies(t, "own"):
                act(c)

    def start(self):
        def one(t, _):
            self.each(t, lambda c: c.start())
            return 0

        lax.fori_loop(0, TILES, one, 0)

    def wait(self, t):
        self.each(t, lambda c: c.wait())


def framed(ref):
    return ref.reshape(ref.shape[0] // STRIDE, STRIDE, NZ)


def dm_copies(dm, before, after, sem, dm_ref, own, place, count):
    src, dst = pl.ds(own, count), pl.ds(place, count)
    d3 = framed(dm_ref)
    return [
        pltpu.make_async_copy(dm.at[src], d3.at[dst, pl.ds(8, NY)], sem),
        pltpu.make_async_copy(before.at[5, src], d3.at[dst, pl.ds(0, 8)], sem),
        pltpu.make_async_copy(after.at[5, src], d3.at[dst, pl.ds(104, 8)], sem),
    ]


def out_copies(o_ref, planes, outs, sem, own, place, count):
    o4 = o_ref.reshape(5, planes, STRIDE, NZ)
    src, dst, mid = pl.ds(place, count), pl.ds(own, count), pl.ds(8, NY)
    density, momentum, energy = outs
    return [
        pltpu.make_async_copy(o4.at[0, src, mid], density.at[dst], sem),
        pltpu.make_async_copy(o4.at[pl.ds(1, 3), src, mid], momentum.at[:, dst], sem),
        pltpu.make_async_copy(o4.at[4, src, mid], energy.at[dst], sem),
    ]


def start_all(copies):
    for c in copies:
        c.start()


def wait_all(copies):
    for c in copies:
        c.wait()


def sums_copy(t_ref, base, count, out, sem):
    return pltpu.make_async_copy(framed(t_ref).at[pl.ds(base, count), pl.ds(0, FRAME)], out, sem)


def pack_kernel(density, momentum, energy, dm, y_last, y_first, x_last, x_first, c_ll, c_lf, c_fl, c_ff, sem):
    copies = []

    def fields(out, planes, rows):
        copies.append(pltpu.make_async_copy(density.at[planes, rows], out.at[0], sem))
        copies.append(pltpu.make_async_copy(momentum.at[:, planes, rows], out.at[pl.ds(1, 3)], sem))
        copies.append(pltpu.make_async_copy(energy.at[planes, rows], out.at[4], sem))

    ends = (pl.ds(NY - 8, 8), pl.ds(0, 8))
    for out, rows in zip((y_last, y_first), ends):
        fields(out, pl.ds(0, NX), rows)
        copies.append(pltpu.make_async_copy(dm.at[:, rows], out.at[5], sem))
    for x_out, c_out, planes in ((x_last, (c_ll, c_lf), pl.ds(NX - 3, 3)), (x_first, (c_fl, c_ff), pl.ds(0, 3))):
        fields(x_out, planes, pl.ds(0, NY))
        for n, rows in enumerate(ends):
            fields(c_out[n], planes, rows)
    start_all(copies)
    wait_all(copies)


WIDE = 24


def x_kernel(density, momentum, energy, out, q_ref, s_ref, sems, out_sem):
    held = pl.ds(1, WIDE + 6)

    def copies(t):
        rows = rows_of(t)
        return [
            pltpu.make_async_copy(density.at[held, rows], q_ref.at[0, :, rows], sems.at[t]),
            pltpu.make_async_copy(momentum.at[:, held, rows], q_ref.at[pl.ds(1, 3), :, rows], sems.at[t]),
            pltpu.make_async_copy(energy.at[held, rows], q_ref.at[4, :, rows], sems.at[t]),
        ]

    def leaving(t):
        return pltpu.make_async_copy(s_ref.at[:, :, rows_of(t)], out.at[:, :, rows_of(t)], out_sem)

    def begin(t, _):
        start_all(copies(t))
        return 0

    def tile(t, _):
        wait_all(copies(t))
        rows = rows_of(t)

        def write(f, x, value):
            s_ref[f, x, rows, :] = value

        x_lines(((0, 0, WIDE),), lambda f, i: q_ref[f, i, rows, :], write)
        leaving(t).start()
        return 0

    def end(t, _):
        leaving(t).wait()
        return 0

    lax.fori_loop(0, NY // 8, begin, 0)
    lax.fori_loop(0, NY // 8, tile, 0)
    lax.fori_loop(0, NY // 8, end, 0)


def inner_kernel(dest, swept, dm, y_before, y_after,
                 out_density, out_momentum, out_energy, out_sums, send,
                 q_ref, s_ref, o_ref, dm_ref, t_ref, x_ref, y_ref, sems, sem, out_sem):
    held = pl.ds(1, WIDE + 6)
    s4 = s_ref.reshape(5, WIDE, STRIDE, NZ)
    outs = (out_density, out_momentum, out_energy)

    def swept_copy(g):
        planes = pl.ds(g * 8, 8)
        return pltpu.make_async_copy(swept.at[:, planes], s4.at[:, planes, pl.ds(8, NY)], sems.at[g])

    def leaving(g):
        return out_copies(o_ref, WIDE, outs, out_sem, 4 + g * 8, g * 8, 8)

    halo = [
        pltpu.make_async_copy(y_before.at[pl.ds(0, 5), held], q_ref.at[:, :, pl.ds(0, 8)], sem),
        pltpu.make_async_copy(y_after.at[pl.ds(0, 5), held], q_ref.at[:, :, pl.ds(8, 8)], sem),
    ] + dm_copies(dm, y_before, y_after, sem, dm_ref, 4, 0, WIDE)
    start_all(halo)
    for g in range(WIDE // 8):
        swept_copy(g).start()
    clear(send)
    wait_all(halo)
    x_sweep(q_ref, s_ref, WIDE, ((0, 0, WIDE),), 2, lambda t: None, lambda t: t * 104)
    yz_sweep(s_ref, dm_ref, o_ref, t_ref, WIDE, lambda g: swept_copy(g).wait(), lambda g: start_all(leaving(g)))
    sums = sums_copy(t_ref, 0, WIDE, out_sums, sem)
    sums.start()
    for row, base in ((0, 2), (8, 10)):
        smooth(lambda p, r: t_ref[pl.ds((base + p) * STRIDE + r, 8), :], dest, x_ref, y_ref, send, row)
    sums.wait()
    for g in range(WIDE // 8):
        wait_all(leaving(g))


def outer_kernel(density, momentum, energy, dm, y_before, y_after, x_before, x_after, c_bb, c_ba, c_ab, c_aa,
                 in_density, in_momentum, in_energy,
                 out_density, out_momentum, out_energy, out_sums, to_next, to_prev,
                 q_ref, s_ref, o_ref, dm_ref, t_ref, sems, sem, out_sem):
    fields = (density, momentum, energy)
    tiles = Tiles(q_ref, sems, [
        (fields, y_before, y_after, pl.ds(25, 7), pl.ds(0, 7)),
        ((x_after,), c_ab, c_aa, pl.ds(0, 3), pl.ds(7, 3)),
        ((x_before,), c_bb, c_ba, pl.ds(0, 3), pl.ds(10, 3)),
        (fields, y_before, y_after, pl.ds(0, 7), pl.ds(13, 7)),
    ])
    tiles.start()
    copies = (dm_copies(dm, y_before, y_after, sem, dm_ref, 28, 0, 4)
              + dm_copies(dm, y_before, y_after, sem, dm_ref, 0, 4, 4))
    start_all(copies)
    x_sweep(q_ref, s_ref, 8, ((0, 0, 4), (10, 4, 4)), TILES, tiles.wait, lambda t: t * 8)
    wait_all(copies)
    yz_sweep(s_ref, dm_ref, o_ref, t_ref, 8, lambda g: None, lambda g: None)
    outs = (out_density, out_momentum, out_energy)
    leaving = out_copies(o_ref, 8, outs, out_sem, 28, 0, 4) + out_copies(o_ref, 8, outs, out_sem, 0, 4, 4)
    leaving.append(sums_copy(t_ref, 0, 8, out_sums, out_sem))
    leaving.append(sums_copy(t_ref, 2, 2, to_next, out_sem))
    leaving.append(sums_copy(t_ref, 4, 2, to_prev, out_sem))
    start_all(leaving)
    wait_all(leaving)


def rest_kernel(dest, sums_inner, sums_outer, from_prev, from_next, send, w_ref, x_ref, y_ref, sem):
    def part(src, own, place, count):
        return pltpu.make_async_copy(src.at[pl.ds(own, count)], w_ref.at[pl.ds(place, count)], sem)

    copies = [
        part(from_prev, 0, 0, 2),
        part(sums_outer, 4, 2, 4),
        part(sums_inner, 0, 6, 6),
        part(sums_inner, 18, 12, 6),
        part(sums_outer, 0, 18, 4),
        part(from_next, 0, 22, 2),
    ]
    start_all(copies)
    clear(send)
    wait_all(copies)
    for row, base in ((0, 0), (8, 12)):
        smooth(lambda p, r: w_ref[base + p, pl.ds(r, 8), :], dest, x_ref, y_ref, send, row)


ANY = pl.BlockSpec(memory_space=pl.ANY)
SMEM = pl.BlockSpec(memory_space=pltpu.SMEM)
VMEM = pl.BlockSpec(memory_space=pltpu.VMEM)
F32 = jnp.float32


def shape(*dims):
    return jax.ShapeDtypeStruct(dims, F32)


def params():
    return pltpu.CompilerParams(vmem_limit_bytes=VMEM_LIMIT)


def cost(micros):
    return pl.CostEstimate(flops=int(micros * COST), bytes_accessed=0, transcendentals=0)


def main_scratch(planes, held, rows):
    return [
        pltpu.VMEM((5, held, rows, NZ), F32),
        pltpu.VMEM((5 * planes * STRIDE, NZ), F32),
        pltpu.VMEM((5 * planes * STRIDE, NZ), F32),
        pltpu.VMEM((planes * STRIDE, NZ), F32),
        pltpu.VMEM((planes * STRIDE, NZ), F32),
    ]


def semaphores():
    return [pltpu.SemaphoreType.DMA((TILES,)), pltpu.SemaphoreType.DMA, pltpu.SemaphoreType.DMA]


def smooth_scratch():
    return [pltpu.VMEM((8 * FRAME, NZ), F32), pltpu.VMEM((8 * NY, NZ), F32)]


FIELD_SHAPES = (shape(NX, NY, NZ), shape(3, NX, NY, NZ), shape(NX, NY, NZ))


def shifted(value, axis, by):
    size = lax.axis_size(axis)
    return lax.ppermute(value, axis, [(i, (i + by) % size) for i in range(size)])


def diagonal(value, by_box, by_grp):
    boxes, grps = lax.axis_size("box"), lax.axis_size("grp")
    pairs = []
    for i in range(boxes):
        for j in range(grps):
            pairs.append((i * grps + j, (i + by_box) % boxes * grps + (j + by_grp) % grps))
    return lax.ppermute(value, ("box", "grp"), pairs)


def body(density, momentum, energy, dm_density, box_dest):
    dest = box_dest[0, 0, :, 0]
    fields = (density, momentum, energy)
    halo_shapes = (shape(6, NX, 8, NZ),) * 2 + (shape(5, 3, NY, NZ),) * 2 + (shape(5, 3, 8, NZ),) * 4
    y_last, y_first, x_last, x_first, c_ll, c_lf, c_fl, c_ff = pl.pallas_call(
        pack_kernel,
        out_shape=halo_shapes,
        in_specs=[ANY] * 4,
        out_specs=[VMEM] * 8,
        scratch_shapes=[pltpu.SemaphoreType.DMA],
        compiler_params=params(),
        cost_estimate=cost(2),
        name="pack",
    )(density, momentum, energy, dm_density)
    y_before = shifted(y_last, "grp", 1)
    y_after = shifted(y_first, "grp", -1)
    x_before = shifted(x_last, "box", 1)
    x_after = shifted(x_first, "box", -1)
    c_bb = diagonal(c_ll, 1, 1)
    c_ba = diagonal(c_lf, 1, -1)
    c_ab = diagonal(c_fl, -1, 1)
    c_aa = diagonal(c_ff, -1, -1)

    swept = pl.pallas_call(
        x_kernel,
        out_shape=shape(5, WIDE, NY, NZ),
        in_specs=[ANY] * 3,
        out_specs=ANY,
        scratch_shapes=[
            pltpu.VMEM((5, WIDE + 6, NY, NZ), F32), pltpu.VMEM((5, WIDE, NY, NZ), F32),
            pltpu.SemaphoreType.DMA((NY // 8,)), pltpu.SemaphoreType.DMA],
        compiler_params=params(),
        cost_estimate=cost(9),
        name="x_own",
    )(*fields)

    def exchange(send, planes):
        return lax.all_to_all(send.reshape(16, 2, planes, 1024), "box", split_axis=0, concat_axis=0, tiled=True)

    inner = pl.pallas_call(
        inner_kernel,
        out_shape=FIELD_SHAPES + (shape(WIDE, FRAME, NZ), shape(32, 16, 1024)),
        in_specs=[SMEM] + [ANY] * 4,
        out_specs=[ANY] * 4 + [VMEM],
        scratch_shapes=main_scratch(WIDE, WIDE + 6, 16) + smooth_scratch() + semaphores(),
        compiler_params=params(),
        cost_estimate=cost(33),
        name="inner",
    )(dest, swept, dm_density, y_before, y_after)
    *made, sums_inner, send_inner = inner
    got_inner = exchange(send_inner, 16)

    outer = pl.pallas_call(
        outer_kernel,
        out_shape=FIELD_SHAPES + (shape(8, FRAME, NZ), shape(2, FRAME, NZ), shape(2, FRAME, NZ)),
        in_specs=[ANY] * 15,
        out_specs=[ANY] * 6,
        scratch_shapes=main_scratch(8, 20, FRAME) + semaphores(),
        input_output_aliases={12: 0, 13: 1, 14: 2},
        compiler_params=params(),
        cost_estimate=cost(14),
        name="outer",
    )(*fields, dm_density, y_before, y_after, x_before, x_after, c_bb, c_ba, c_ab, c_aa, *made)
    new_density, new_momentum, new_energy, sums_outer, to_next, to_prev = outer
    from_prev = shifted(to_next, "box", 1)
    from_next = shifted(to_prev, "box", -1)
    send_rest = pl.pallas_call(
        rest_kernel,
        out_shape=shape(32, 16, 1024),
        in_specs=[SMEM] + [ANY] * 4,
        out_specs=VMEM,
        scratch_shapes=[pltpu.VMEM((24, FRAME, NZ), F32)] + smooth_scratch() + [pltpu.SemaphoreType.DMA],
        compiler_params=params(),
        cost_estimate=cost(5),
        name="rest",
    )(dest, sums_inner, sums_outer, from_prev, from_next)
    send_rest, got_inner = lax.optimization_barrier((send_rest, got_inner))
    got_rest = exchange(send_rest, 16)
    kd = jnp.concatenate([got_rest[:, :, :8], got_inner, got_rest[:, :, 8:]], axis=2)
    return (new_density, new_momentum, new_energy, kd[None, None])


def solution(mesh):
    in_specs = (
        P("box", "grp", None),
        P(None, "box", "grp", None),
        P("box", "grp", None),
        P("box", "grp", None),
        P("grp", "box", None, None),
    )
    out_specs = (
        P("box", "grp", None),
        P(None, "box", "grp", None),
        P("box", "grp", None),
        P("grp", "box", None, None, None, None),
    )
    return jax.shard_map(body, mesh=mesh, in_specs=in_specs, out_specs=out_specs, check_vma=False)
```

```python
import functools
import math

import jax
import jax.numpy as jnp
import numpy as np
from jax import lax
from jax.experimental import pallas as pl
from jax.experimental.pallas import tpu as pltpu
from jax.sharding import PartitionSpec as P

F32 = jnp.float32
BOX = 32
BOX_Y = 3
BOX_Z = 4
NX = 32
NY = 96
NZ = 128
FRAME = 112
TILES = FRAME // 8
STRIDE = 120
STEP = 0.03
SCALES = (1.0, STEP, STEP, STEP, 2.0 * STEP * STEP)
UNSCALES = (1.0, 1.0 / STEP, 1.0 / STEP, 1.0 / STEP, 1.0 / (2.0 * STEP * STEP))
SOUND = math.sqrt(5.0 / 3.0)
TINY = 1e-30
COST = 1_100_000_000
VMEM_LIMIT = 54 * 1024 * 1024


def limit(value, other):
    bound = jnp.abs(other + other)
    return jnp.maximum(jnp.minimum(value, bound), -bound)


def between(value, end):
    return jnp.minimum(jnp.maximum(value, jnp.minimum(end, 0.0)), jnp.maximum(end, 0.0))


def deviation(d_prev, d_here, d_next):
    return between(0.5 * d_here + (d_prev - d_next) * (1.0 / 12.0), d_here)


def invert(x):
    return 1.0 / x


def state_of(u, normal):
    inverse = invert(u[0])
    squares = u[1] * u[1] + u[2] * u[2] + u[3] * u[3]
    pressure = u[4] - squares * inverse
    third = pressure * (1.0 / 3.0)
    velocity = u[normal] * inverse
    ratio = jnp.maximum(third * inverse, TINY)
    reach = jnp.abs(velocity) + SOUND * (ratio * lax.rsqrt(ratio))
    return velocity, third, reach


def flux(left, right, normal):
    v_left, p_left, reach_left = state_of(left, normal)
    v_right, p_right, reach_right = state_of(right, normal)
    reach = jnp.maximum(reach_left, reach_right)
    up = v_left + reach
    down = v_right - reach
    out = [left[f] * up + right[f] * down for f in range(5)]
    out[normal] = out[normal] + (p_left + p_right)
    work = p_left * v_left + p_right * v_right
    out[4] = out[4] + (work + work)
    return out


class Line:
    def __init__(self, normal):
        self.normal = normal
        self.q = []
        self.d = []
        self.dl = None
        self.er = None
        self.flux = None

    def load(self, q, carry):
        self.q = list(q)
        self.d = [carry[0:5], carry[5:10]]
        self.dl = carry[10:15]
        self.er = carry[15:20]
        self.flux = carry[20:25]

    def carry(self):
        return tuple(self.d[0]) + tuple(self.d[1]) + tuple(self.dl) + tuple(self.er) + tuple(self.flux)

    def push(self, new):
        q, d = self.q, self.d
        out = None
        if q:
            d0 = [a - b for a, b in zip(new, q[-1])]
            if len(d) >= 2:
                d2, d1 = d[-2], d[-1]
                dr = [deviation(*t) for t in zip(d2, d1, d0)]
                if self.dl is not None:
                    here = q[-2]
                    right = [c + limit(r, l) for c, r, l in zip(here, dr, self.dl)]
                    if self.er is not None:
                        left = [c + limit(l, r) for c, r, l in zip(here, dr, self.dl)]
                        now = flux(self.er, left, self.normal)
                        if self.flux is not None:
                            out = [c - (a - b) for c, a, b in zip(q[-3], now, self.flux)]
                        self.flux = now
                    self.er = right
                self.dl = [r - s for r, s in zip(dr, d1)]
            d.append(d0)
            self.d = d[-2:]
        q.append(new)
        self.q = q[-3:]
        return out


def turn(x, shift):
    return pltpu.roll(x, shift % NZ, 1)


def lane_weights():
    parts = []
    for taps in (((1, 1), (0, -1)), ((0, -5), (1, 7), (-1, -1), (2, -1)), tuple((k, 1) for k in range(-2, 3))):
        w = np.zeros((NZ, NZ), np.float32)
        for offset, value in taps:
            for j in range(NZ):
                w[(j + offset) % NZ, j] = value
        parts.append(w)
    w = np.concatenate(parts, axis=1)
    return jnp.asarray(np.concatenate([w, w], axis=0), jnp.bfloat16)


def mixed(x, weights):
    high = x.astype(jnp.bfloat16)
    low = (x - high.astype(F32)).astype(jnp.bfloat16)
    return jnp.dot(jnp.concatenate([high, low], axis=1), weights, preferred_element_type=F32)


def x_lines(segments, read, write):
    for base, out_base, count in segments:
        line = Line(1)
        for i in range(count + 6):
            new = [read(f, base + i) * SCALES[f] if f else read(f, base + i) for f in range(5)]
            out = line.push(new)
            if out is not None:
                for f in range(5):
                    write(f, out_base + i - 6, out[f])


def x_sweep(q_ref, s_ref, planes, segments, tiles, ready, place):
    def tile(t, _):
        ready(t)
        row = pl.multiple_of(t * 8, 8)
        to = pl.multiple_of(place(t), 8)

        def write(f, x, value):
            s_ref[pl.ds((f * planes + x) * STRIDE + to, 8), :] = value

        x_lines(segments, lambda f, i: q_ref[f, i, pl.ds(row, 8), :], write)
        return 0

    lax.fori_loop(0, tiles, tile, 0)


U = 20
PAIR = 2


def yz_sweep(s_ref, dm_ref, o_ref, t_ref, w_ref, swept_ref, edge_ref, planes, ready, done):
    def group(g, _):
        ready(g)

        def at(f, row):
            return pl.ds((f * planes + g * 8) * STRIDE + row, 8, stride=STRIDE)

        def rows(row):
            return [s_ref[at(f, row), :] for f in range(5)]

        def block(k, row, count):
            return pl.ds((k * U + row) * 8, count * 8)

        first = Line(2)
        for row in range(3, 9):
            first.push(rows(row))

        def some(b, carry):
            base = b * U + 6
            line = Line(2)
            line.load([rows(base), rows(base + 1), rows(base + 2)], carry)
            for r in range(U):
                swept = line.push(rows(base + 3 + r))
                for f in range(5):
                    swept_ref[block(f, r, 1), :] = swept[f]
            for f in range(5):
                q = swept_ref[block(f, 0, U), :]
                both = mixed(q, w_ref[:, :2 * NZ])
                d = both[:, :NZ]
                dr = between(both[:, NZ:] * (1.0 / 12.0), d)
                dl = turn(dr - d, 1)
                edge_ref[block(f, 0, U), :] = q + limit(dr, dl)
                edge_ref[block(5 + f, 0, U), :] = turn(q + limit(dl, dr), -1)
            for r in range(0, U, PAIR):
                left = [edge_ref[block(f, r, PAIR), :] for f in range(5)]
                right = [edge_ref[block(5 + f, r, PAIR), :] for f in range(5)]
                now = flux(left, right, 3)
                for f in range(5):
                    final = swept_ref[block(f, r, PAIR), :] - (now[f] - turn(now[f], 1))
                    if f == 0:
                        density = final
                    else:
                        final = final * UNSCALES[f]
                    for i in range(PAIR):
                        o_ref[at(f, base + r + i), :] = final[8 * i:8 * i + 8]
                for i in range(PAIR):
                    total = density[8 * i:8 * i + 8] + dm_ref[at(0, base + r + i), :]
                    edge_ref[block(0, r + i, 1), :] = total
            sums = mixed(edge_ref[block(0, 0, U), :], w_ref[:, 2 * NZ:])
            for r in range(U):
                t_ref[at(0, base + r), :] = sums[8 * r:8 * r + 8]
            return line.carry()

        lax.fori_loop(0, 100 // U, some, first.carry())
        done(g)
        return 0

    lax.fori_loop(0, planes // 8, group, 0)


def smooth(planes, dest_ref, x_ref, y_ref, send_ref, send_row):
    def x_tile(t, _):
        row = pl.multiple_of(t * 8, 8)
        values = [planes(p, row) for p in range(12)]
        pairs = [values[p] + values[p + 1] for p in range(11)]
        for p in range(8):
            x_ref[pl.ds(p * FRAME + row, 8), :] = pairs[p] + pairs[p + 2] + values[p + 4]
        return 0

    lax.fori_loop(0, TILES, x_tile, 0)

    def y_plane(p, _):
        for t in range(NY // 8):
            start = p * FRAME + 8 + 8 * t
            parts = [x_ref[pl.ds(start + k, 8), :] for k in range(-2, 3)]
            total = ((parts[0] + parts[1]) + (parts[3] + parts[4])) + parts[2]
            y_ref[pl.ds(p * NY + 8 * t, 8), :] = total * (1.0 / 125.0)
        return 0

    lax.fori_loop(0, 8, y_plane, 0)

    places = []
    dests = [dest_ref[k] for k in range(12)]
    for k in range(12):
        slot = jnp.int32(0)
        for other in range(k):
            slot = slot + (dests[other] == dests[k]).astype(jnp.int32)
        places.append(dests[k] * 2 + slot)

    quarter = lax.broadcasted_iota(jnp.int32, (8, NZ), 1) // BOX

    def pick(values):
        out = values[3]
        for b in range(3):
            out = jnp.where(quarter == b, values[b], out)
        return out

    for by in range(BOX_Y):
        for m in range(8):
            s = [y_ref[pl.ds(by * BOX + 4 * m + q, 8, stride=NY), :] for q in range(4)]
            moved = []
            for k in range(4):
                mixed = pick([s[(b + k) % 4] for b in range(4)])
                moved.append(turn(mixed, k * BOX) if k else mixed)
            for bz in range(4):
                out = pick([moved[(q - bz) % 4] for q in range(4)])
                send_ref[places[by * 4 + bz], pl.ds(send_row, 8), pl.ds(m * NZ, NZ)] = out


def clear(send_ref):
    def one(i, _):
        send_ref[i] = jnp.zeros(send_ref.shape[1:], jnp.float32)
        return 0

    lax.fori_loop(0, send_ref.shape[0], one, 0)


def rows_of(t):
    return pl.ds(pl.multiple_of(t * 8, 8), 8)


class Tiles:
    def __init__(self, q_ref, sems, parts):
        self.q_ref, self.sems, self.parts = q_ref, sems, parts

    def copies(self, t, kind):
        out = []
        for own, before, after, src, dst in self.parts:
            q = self.q_ref.at[:, dst, rows_of(t)]
            sem = self.sems.at[t]
            if kind == "before":
                out.append(pltpu.make_async_copy(before.at[pl.ds(0, 5), src], q, sem))
            elif kind == "after":
                out.append(pltpu.make_async_copy(after.at[pl.ds(0, 5), src], q, sem))
            elif len(own) == 1:
                out.append(pltpu.make_async_copy(own[0].at[:, src, rows_of(t - 1)], q, sem))
            else:
                density, momentum, energy = own
                rows = rows_of(t - 1)
                place = self.q_ref.at
                out.append(pltpu.make_async_copy(density.at[src, rows], place[0, dst, rows_of(t)], sem))
                out.append(pltpu.make_async_copy(momentum.at[:, src, rows], place[pl.ds(1, 3), dst, rows_of(t)], sem))
                out.append(pltpu.make_async_copy(energy.at[src, rows], place[4, dst, rows_of(t)], sem))
        return out

    def each(self, t, act):
        @pl.when(t == 0)
        def _():
            for c in self.copies(t, "before"):
                act(c)

        @pl.when(t == TILES - 1)
        def _():
            for c in self.copies(t, "after"):
                act(c)

        @pl.when((t > 0) & (t < TILES - 1))
        def _():
            for c in self.copies(t, "own"):
                act(c)

    def start(self):
        def one(t, _):
            self.each(t, lambda c: c.start())
            return 0

        lax.fori_loop(0, TILES, one, 0)

    def wait(self, t):
        self.each(t, lambda c: c.wait())


def framed(ref):
    return ref.reshape(ref.shape[0] // STRIDE, STRIDE, NZ)


def dm_copies(dm, before, after, sem, dm_ref, own, place, count):
    src, dst = pl.ds(own, count), pl.ds(place, count)
    d3 = framed(dm_ref)
    return [
        pltpu.make_async_copy(dm.at[src], d3.at[dst, pl.ds(8, NY)], sem),
        pltpu.make_async_copy(before.at[5, src], d3.at[dst, pl.ds(0, 8)], sem),
        pltpu.make_async_copy(after.at[5, src], d3.at[dst, pl.ds(104, 8)], sem),
    ]


def out_copies(o_ref, planes, outs, sem, own, place, count):
    o4 = o_ref.reshape(5, planes, STRIDE, NZ)
    src, dst, mid = pl.ds(place, count), pl.ds(own, count), pl.ds(8, NY)
    density, momentum, energy = outs
    return [
        pltpu.make_async_copy(o4.at[0, src, mid], density.at[dst], sem),
        pltpu.make_async_copy(o4.at[pl.ds(1, 3), src, mid], momentum.at[:, dst], sem),
        pltpu.make_async_copy(o4.at[4, src, mid], energy.at[dst], sem),
    ]


def start_all(copies):
    for c in copies:
        c.start()


def wait_all(copies):
    for c in copies:
        c.wait()


def sums_copy(t_ref, base, count, out, sem):
    return pltpu.make_async_copy(framed(t_ref).at[pl.ds(base, count), pl.ds(0, FRAME)], out, sem)


def pack_kernel(density, momentum, energy, dm, y_last, y_first, x_last, x_first, c_ll, c_lf, c_fl, c_ff, sem):
    copies = []

    def fields(out, planes, rows):
        copies.append(pltpu.make_async_copy(density.at[planes, rows], out.at[0], sem))
        copies.append(pltpu.make_async_copy(momentum.at[:, planes, rows], out.at[pl.ds(1, 3)], sem))
        copies.append(pltpu.make_async_copy(energy.at[planes, rows], out.at[4], sem))

    ends = (pl.ds(NY - 8, 8), pl.ds(0, 8))
    for out, rows in zip((y_last, y_first), ends):
        fields(out, pl.ds(0, NX), rows)
        copies.append(pltpu.make_async_copy(dm.at[:, rows], out.at[5], sem))
    for x_out, c_out, planes in ((x_last, (c_ll, c_lf), pl.ds(NX - 3, 3)), (x_first, (c_fl, c_ff), pl.ds(0, 3))):
        fields(x_out, planes, pl.ds(0, NY))
        for n, rows in enumerate(ends):
            fields(c_out[n], planes, rows)
    start_all(copies)
    wait_all(copies)


WIDE = 24


def x_kernel(density, momentum, energy, out, q_ref, s_ref, sems, out_sem):
    held = pl.ds(1, WIDE + 6)

    def copies(t):
        rows = rows_of(t)
        return [
            pltpu.make_async_copy(density.at[held, rows], q_ref.at[0, :, rows], sems.at[t]),
            pltpu.make_async_copy(momentum.at[:, held, rows], q_ref.at[pl.ds(1, 3), :, rows], sems.at[t]),
            pltpu.make_async_copy(energy.at[held, rows], q_ref.at[4, :, rows], sems.at[t]),
        ]

    def leaving(t):
        return pltpu.make_async_copy(s_ref.at[:, :, rows_of(t)], out.at[:, :, rows_of(t)], out_sem)

    def begin(t, _):
        start_all(copies(t))
        return 0

    def tile(t, _):
        wait_all(copies(t))
        rows = rows_of(t)

        def write(f, x, value):
            s_ref[f, x, rows, :] = value

        x_lines(((0, 0, WIDE),), lambda f, i: q_ref[f, i, rows, :], write)
        leaving(t).start()
        return 0

    def end(t, _):
        leaving(t).wait()
        return 0

    lax.fori_loop(0, NY // 8, begin, 0)
    lax.fori_loop(0, NY // 8, tile, 0)
    lax.fori_loop(0, NY // 8, end, 0)


def inner_kernel(dest, weights, swept, dm, y_before, y_after,
                 out_density, out_momentum, out_energy, out_sums, send,
                 q_ref, s_ref, o_ref, dm_ref, t_ref, w_ref, swept_ref, edge_ref, x_ref, y_ref, sems, sem, out_sem):
    held = pl.ds(1, WIDE + 6)
    s4 = s_ref.reshape(5, WIDE, STRIDE, NZ)
    outs = (out_density, out_momentum, out_energy)

    def swept_copy(g):
        planes = pl.ds(g * 8, 8)
        return pltpu.make_async_copy(swept.at[:, planes], s4.at[:, planes, pl.ds(8, NY)], sems.at[g])

    def leaving(g):
        return out_copies(o_ref, WIDE, outs, out_sem, 4 + g * 8, g * 8, 8)

    halo = [
        pltpu.make_async_copy(y_before.at[pl.ds(0, 5), held], q_ref.at[:, :, pl.ds(0, 8)], sem),
        pltpu.make_async_copy(y_after.at[pl.ds(0, 5), held], q_ref.at[:, :, pl.ds(8, 8)], sem),
    ] + dm_copies(dm, y_before, y_after, sem, dm_ref, 4, 0, WIDE)
    halo.append(pltpu.make_async_copy(weights, w_ref, sem))
    start_all(halo)
    for g in range(WIDE // 8):
        swept_copy(g).start()
    clear(send)
    wait_all(halo)
    x_sweep(q_ref, s_ref, WIDE, ((0, 0, WIDE),), 2, lambda t: None, lambda t: t * 104)
    yz_sweep(s_ref, dm_ref, o_ref, t_ref, w_ref, swept_ref, edge_ref, WIDE, lambda g: swept_copy(g).wait(), lambda g: start_all(leaving(g)))
    sums = sums_copy(t_ref, 0, WIDE, out_sums, sem)
    sums.start()
    for row, base in ((0, 2), (8, 10)):
        smooth(lambda p, r: t_ref[pl.ds((base + p) * STRIDE + r, 8), :], dest, x_ref, y_ref, send, row)
    sums.wait()
    for g in range(WIDE // 8):
        wait_all(leaving(g))


def outer_kernel(weights, density, momentum, energy, dm, y_before, y_after, x_before, x_after, c_bb, c_ba, c_ab, c_aa,
                 in_density, in_momentum, in_energy,
                 out_density, out_momentum, out_energy, out_sums, to_next, to_prev,
                 q_ref, s_ref, o_ref, dm_ref, t_ref, w_ref, swept_ref, edge_ref, sems, sem, out_sem):
    fields = (density, momentum, energy)
    tiles = Tiles(q_ref, sems, [
        (fields, y_before, y_after, pl.ds(25, 7), pl.ds(0, 7)),
        ((x_after,), c_ab, c_aa, pl.ds(0, 3), pl.ds(7, 3)),
        ((x_before,), c_bb, c_ba, pl.ds(0, 3), pl.ds(10, 3)),
        (fields, y_before, y_after, pl.ds(0, 7), pl.ds(13, 7)),
    ])
    tiles.start()
    copies = (dm_copies(dm, y_before, y_after, sem, dm_ref, 28, 0, 4)
              + dm_copies(dm, y_before, y_after, sem, dm_ref, 0, 4, 4))
    copies.append(pltpu.make_async_copy(weights, w_ref, sem))
    start_all(copies)
    x_sweep(q_ref, s_ref, 8, ((0, 0, 4), (10, 4, 4)), TILES, tiles.wait, lambda t: t * 8)
    wait_all(copies)
    yz_sweep(s_ref, dm_ref, o_ref, t_ref, w_ref, swept_ref, edge_ref, 8, lambda g: None, lambda g: None)
    outs = (out_density, out_momentum, out_energy)
    leaving = out_copies(o_ref, 8, outs, out_sem, 28, 0, 4) + out_copies(o_ref, 8, outs, out_sem, 0, 4, 4)
    leaving.append(sums_copy(t_ref, 0, 8, out_sums, out_sem))
    leaving.append(sums_copy(t_ref, 2, 2, to_next, out_sem))
    leaving.append(sums_copy(t_ref, 4, 2, to_prev, out_sem))
    start_all(leaving)
    wait_all(leaving)


def rest_kernel(dest, sums_inner, sums_outer, from_prev, from_next, send, w_ref, x_ref, y_ref, sem):
    def part(src, own, place, count):
        return pltpu.make_async_copy(src.at[pl.ds(own, count)], w_ref.at[pl.ds(place, count)], sem)

    copies = [
        part(from_prev, 0, 0, 2),
        part(sums_outer, 4, 2, 4),
        part(sums_inner, 0, 6, 6),
        part(sums_inner, 18, 12, 6),
        part(sums_outer, 0, 18, 4),
        part(from_next, 0, 22, 2),
    ]
    start_all(copies)
    clear(send)
    wait_all(copies)
    for row, base in ((0, 0), (8, 12)):
        smooth(lambda p, r: w_ref[base + p, pl.ds(r, 8), :], dest, x_ref, y_ref, send, row)


ANY = pl.BlockSpec(memory_space=pl.ANY)
SMEM = pl.BlockSpec(memory_space=pltpu.SMEM)
VMEM = pl.BlockSpec(memory_space=pltpu.VMEM)


def shape(*dims):
    return jax.ShapeDtypeStruct(dims, F32)


def params():
    return pltpu.CompilerParams(vmem_limit_bytes=VMEM_LIMIT)


def cost(micros):
    return pl.CostEstimate(flops=int(micros * COST), bytes_accessed=0, transcendentals=0)


def main_scratch(planes, held, rows):
    return [
        pltpu.VMEM((5, held, rows, NZ), F32),
        pltpu.VMEM((5 * planes * STRIDE, NZ), F32),
        pltpu.VMEM((5 * planes * STRIDE, NZ), F32),
        pltpu.VMEM((planes * STRIDE, NZ), F32),
        pltpu.VMEM((planes * STRIDE, NZ), F32),
        pltpu.VMEM((2 * NZ, 3 * NZ), jnp.bfloat16),
        pltpu.VMEM((5 * U * 8, NZ), F32),
        pltpu.VMEM((10 * U * 8, NZ), F32),
    ]


def semaphores():
    return [pltpu.SemaphoreType.DMA((TILES,)), pltpu.SemaphoreType.DMA, pltpu.SemaphoreType.DMA]


def smooth_scratch():
    return [pltpu.VMEM((8 * FRAME, NZ), F32), pltpu.VMEM((8 * NY, NZ), F32)]


FIELD_SHAPES = (shape(NX, NY, NZ), shape(3, NX, NY, NZ), shape(NX, NY, NZ))


def shifted(value, axis, by):
    size = lax.axis_size(axis)
    return lax.ppermute(value, axis, [(i, (i + by) % size) for i in range(size)])


def diagonal(value, by_box, by_grp):
    boxes, grps = lax.axis_size("box"), lax.axis_size("grp")
    pairs = []
    for i in range(boxes):
        for j in range(grps):
            pairs.append((i * grps + j, (i + by_box) % boxes * grps + (j + by_grp) % grps))
    return lax.ppermute(value, ("box", "grp"), pairs)


def body(density, momentum, energy, dm_density, box_dest):
    dest = box_dest[0, 0, :, 0]
    fields = (density, momentum, energy)
    weights = lane_weights()
    halo_shapes = (shape(6, NX, 8, NZ),) * 2 + (shape(5, 3, NY, NZ),) * 2 + (shape(5, 3, 8, NZ),) * 4
    y_last, y_first, x_last, x_first, c_ll, c_lf, c_fl, c_ff = pl.pallas_call(
        pack_kernel,
        out_shape=halo_shapes,
        in_specs=[ANY] * 4,
        out_specs=[VMEM] * 8,
        scratch_shapes=[pltpu.SemaphoreType.DMA],
        compiler_params=params(),
        cost_estimate=cost(2),
        name="pack",
    )(density, momentum, energy, dm_density)
    y_before = shifted(y_last, "grp", 1)
    y_after = shifted(y_first, "grp", -1)
    x_before = shifted(x_last, "box", 1)
    x_after = shifted(x_first, "box", -1)
    c_bb = diagonal(c_ll, 1, 1)
    c_ba = diagonal(c_lf, 1, -1)
    c_ab = diagonal(c_fl, -1, 1)
    c_aa = diagonal(c_ff, -1, -1)

    swept = pl.pallas_call(
        x_kernel,
        out_shape=shape(5, WIDE, NY, NZ),
        in_specs=[ANY] * 3,
        out_specs=ANY,
        scratch_shapes=[
            pltpu.VMEM((5, WIDE + 6, NY, NZ), F32), pltpu.VMEM((5, WIDE, NY, NZ), F32),
            pltpu.SemaphoreType.DMA((NY // 8,)), pltpu.SemaphoreType.DMA],
        compiler_params=params(),
        cost_estimate=cost(9),
        name="x_own",
    )(*fields)

    def exchange(send, planes):
        return lax.all_to_all(send.reshape(16, 2, planes, 1024), "box", split_axis=0, concat_axis=0, tiled=True)

    inner = pl.pallas_call(
        inner_kernel,
        out_shape=FIELD_SHAPES + (shape(WIDE, FRAME, NZ), shape(32, 16, 1024)),
        in_specs=[SMEM] + [ANY] * 5,
        out_specs=[ANY] * 4 + [VMEM],
        scratch_shapes=main_scratch(WIDE, WIDE + 6, 16) + smooth_scratch() + semaphores(),
        compiler_params=params(),
        cost_estimate=cost(26),
        name="inner",
    )(dest, weights, swept, dm_density, y_before, y_after)
    *made, sums_inner, send_inner = inner
    got_inner = exchange(send_inner, 16)

    outer = pl.pallas_call(
        outer_kernel,
        out_shape=FIELD_SHAPES + (shape(8, FRAME, NZ), shape(2, FRAME, NZ), shape(2, FRAME, NZ)),
        in_specs=[ANY] * 16,
        out_specs=[ANY] * 6,
        scratch_shapes=main_scratch(8, 20, FRAME) + semaphores(),
        input_output_aliases={13: 0, 14: 1, 15: 2},
        compiler_params=params(),
        cost_estimate=cost(13),
        name="outer",
    )(weights, *fields, dm_density, y_before, y_after, x_before, x_after, c_bb, c_ba, c_ab, c_aa, *made)
    new_density, new_momentum, new_energy, sums_outer, to_next, to_prev = outer
    from_prev = shifted(to_next, "box", 1)
    from_next = shifted(to_prev, "box", -1)
    send_rest = pl.pallas_call(
        rest_kernel,
        out_shape=shape(32, 16, 1024),
        in_specs=[SMEM] + [ANY] * 4,
        out_specs=VMEM,
        scratch_shapes=[pltpu.VMEM((24, FRAME, NZ), F32)] + smooth_scratch() + [pltpu.SemaphoreType.DMA],
        compiler_params=params(),
        cost_estimate=cost(5),
        name="rest",
    )(dest, sums_inner, sums_outer, from_prev, from_next)
    send_rest, got_inner = lax.optimization_barrier((send_rest, got_inner))
    got_rest = exchange(send_rest, 16)
    kd = jnp.concatenate([got_rest[:, :, :8], got_inner, got_rest[:, :, 8:]], axis=2)
    return (new_density, new_momentum, new_energy, kd[None, None])


def solution(mesh):
    in_specs = (
        P("box", "grp", None),
        P(None, "box", "grp", None),
        P("box", "grp", None),
        P("box", "grp", None),
        P("grp", "box", None, None),
    )
    out_specs = (
        P("box", "grp", None),
        P(None, "box", "grp", None),
        P("box", "grp", None),
        P("grp", "box", None, None, None, None),
    )
    return jax.shard_map(body, mesh=mesh, in_specs=in_specs, out_specs=out_specs, check_vma=False)
```

```python
import functools
import math

import jax
import jax.numpy as jnp
import numpy as np
from jax import lax
from jax.experimental import pallas as pl
from jax.experimental.pallas import tpu as pltpu
from jax.sharding import PartitionSpec as P

F32 = jnp.float32
BOX = 32
BOX_Y = 3
BOX_Z = 4
NX = 32
NY = 96
NZ = 128
FRAME = 112
TILES = FRAME // 8
STRIDE = 120
STEP = 0.03
SCALES = (1.0, STEP, STEP, STEP, 2.0 * STEP * STEP)
UNSCALES = (1.0, 1.0 / STEP, 1.0 / STEP, 1.0 / STEP, 1.0 / (2.0 * STEP * STEP))
SOUND = math.sqrt(5.0 / 3.0)
TINY = 1e-30
COST = 1_100_000_000
VMEM_LIMIT = 54 * 1024 * 1024


def limit(value, other):
    bound = jnp.abs(other + other)
    return jnp.maximum(jnp.minimum(value, bound), -bound)


def between(value, end):
    return jnp.minimum(jnp.maximum(value, jnp.minimum(end, 0.0)), jnp.maximum(end, 0.0))


def deviation(d_prev, d_here, d_next):
    return between(0.5 * d_here + (d_prev - d_next) * (1.0 / 12.0), d_here)


def invert(x):
    return 1.0 / x


def state_of(u, normal):
    inverse = invert(u[0])
    squares = u[1] * u[1] + u[2] * u[2] + u[3] * u[3]
    pressure = u[4] - squares * inverse
    third = pressure * (1.0 / 3.0)
    velocity = u[normal] * inverse
    ratio = jnp.maximum(third * inverse, TINY)
    reach = jnp.abs(velocity) + SOUND * (ratio * lax.rsqrt(ratio))
    return velocity, third, reach


def flux(left, right, normal):
    v_left, p_left, reach_left = state_of(left, normal)
    v_right, p_right, reach_right = state_of(right, normal)
    reach = jnp.maximum(reach_left, reach_right)
    up = v_left + reach
    down = v_right - reach
    out = [left[f] * up + right[f] * down for f in range(5)]
    out[normal] = out[normal] + (p_left + p_right)
    work = p_left * v_left + p_right * v_right
    out[4] = out[4] + (work + work)
    return out


class Line:
    def __init__(self, normal):
        self.normal = normal
        self.q = []
        self.d = []
        self.dl = None
        self.er = None
        self.flux = None

    def load(self, q, carry):
        self.q = list(q)
        self.d = [carry[0:5], carry[5:10]]
        self.dl = carry[10:15]
        self.er = carry[15:20]
        self.flux = carry[20:25]

    def carry(self):
        return tuple(self.d[0]) + tuple(self.d[1]) + tuple(self.dl) + tuple(self.er) + tuple(self.flux)

    def push(self, new):
        q, d = self.q, self.d
        out = None
        if q:
            d0 = [a - b for a, b in zip(new, q[-1])]
            if len(d) >= 2:
                d2, d1 = d[-2], d[-1]
                dr = [deviation(*t) for t in zip(d2, d1, d0)]
                if self.dl is not None:
                    here = q[-2]
                    right = [c + limit(r, l) for c, r, l in zip(here, dr, self.dl)]
                    if self.er is not None:
                        left = [c + limit(l, r) for c, r, l in zip(here, dr, self.dl)]
                        now = flux(self.er, left, self.normal)
                        if self.flux is not None:
                            out = [c - (a - b) for c, a, b in zip(q[-3], now, self.flux)]
                        self.flux = now
                    self.er = right
                self.dl = [r - s for r, s in zip(dr, d1)]
            d.append(d0)
            self.d = d[-2:]
        q.append(new)
        self.q = q[-3:]
        return out


def turn(x, shift):
    return pltpu.roll(x, shift % NZ, 1)


def lane_weights():
    parts = []
    for taps in (((1, 1), (0, -1)), ((0, -5), (1, 7), (-1, -1), (2, -1)), tuple((k, 1) for k in range(-2, 3))):
        w = np.zeros((NZ, NZ), np.float32)
        for offset, value in taps:
            for j in range(NZ):
                w[(j + offset) % NZ, j] = value
        parts.append(w)
    w = np.concatenate(parts, axis=1)
    return jnp.asarray(np.concatenate([w, w], axis=0), jnp.bfloat16)


def mixed(x, weights):
    high = x.astype(jnp.bfloat16)
    low = (x - high.astype(F32)).astype(jnp.bfloat16)
    return jnp.dot(jnp.concatenate([high, low], axis=1), weights, preferred_element_type=F32)


def x_lines(segments, read, write):
    for base, out_base, count in segments:
        line = Line(1)
        for i in range(count + 6):
            new = [read(f, base + i) * SCALES[f] if f else read(f, base + i) for f in range(5)]
            out = line.push(new)
            if out is not None:
                for f in range(5):
                    write(f, out_base + i - 6, out[f])


def x_sweep(q_ref, s_ref, planes, segments, tiles, ready, place):
    def tile(t, _):
        ready(t)
        row = pl.multiple_of(t * 8, 8)
        to = pl.multiple_of(place(t), 8)

        def write(f, x, value):
            s_ref[pl.ds((f * planes + x) * STRIDE + to, 8), :] = value

        x_lines(segments, lambda f, i: q_ref[f, i, pl.ds(row, 8), :], write)
        return 0

    lax.fori_loop(0, tiles, tile, 0)


U = 20
PAIR = 2


def yz_sweep(s_ref, dm_ref, o_ref, t_ref, w_ref, swept_ref, edge_ref, planes, ready, done):
    def group(g, _):
        ready(g)

        def at(f, row):
            return pl.ds((f * planes + g * 8) * STRIDE + row, 8, stride=STRIDE)

        def rows(row):
            return [s_ref[at(f, row), :] for f in range(5)]

        def block(k, row, count):
            return pl.ds((k * U + row) * 8, count * 8)

        first = Line(2)
        for row in range(3, 9):
            first.push(rows(row))

        def some(b, carry):
            base = b * U + 6
            line = Line(2)
            line.load([rows(base), rows(base + 1), rows(base + 2)], carry)
            for r in range(U):
                swept = line.push(rows(base + 3 + r))
                for f in range(5):
                    swept_ref[block(f, r, 1), :] = swept[f]
            for f in range(5):
                q = swept_ref[block(f, 0, U), :]
                both = mixed(q, w_ref[:, :2 * NZ])
                d = both[:, :NZ]
                dr = between(both[:, NZ:] * (1.0 / 12.0), d)
                dl = turn(dr - d, 1)
                edge_ref[block(f, 0, U), :] = q + limit(dr, dl)
                edge_ref[block(5 + f, 0, U), :] = turn(q + limit(dl, dr), -1)
            for r in range(0, U, PAIR):
                left = [edge_ref[block(f, r, PAIR), :] for f in range(5)]
                right = [edge_ref[block(5 + f, r, PAIR), :] for f in range(5)]
                now = flux(left, right, 3)
                for f in range(5):
                    final = swept_ref[block(f, r, PAIR), :] - (now[f] - turn(now[f], 1))
                    if f == 0:
                        density = final
                    else:
                        final = final * UNSCALES[f]
                    for i in range(PAIR):
                        o_ref[at(f, base + r + i), :] = final[8 * i:8 * i + 8]
                for i in range(PAIR):
                    total = density[8 * i:8 * i + 8] + dm_ref[at(0, base + r + i), :]
                    edge_ref[block(0, r + i, 1), :] = total
            sums = mixed(edge_ref[block(0, 0, U), :], w_ref[:, 2 * NZ:])
            for r in range(U):
                t_ref[at(0, base + r), :] = sums[8 * r:8 * r + 8]
            return line.carry()

        lax.fori_loop(0, 100 // U, some, first.carry())
        done(g)
        return 0

    lax.fori_loop(0, planes // 8, group, 0)


def smooth(planes, dest_ref, x_ref, y_ref, send_ref, send_row):
    def x_tile(t, _):
        row = pl.multiple_of(t * 8, 8)
        values = [planes(p, row) for p in range(12)]
        pairs = [values[p] + values[p + 1] for p in range(11)]
        for p in range(8):
            x_ref[pl.ds(p * FRAME + row, 8), :] = pairs[p] + pairs[p + 2] + values[p + 4]
        return 0

    lax.fori_loop(0, TILES, x_tile, 0)

    def y_plane(p, _):
        for t in range(NY // 8):
            start = p * FRAME + 8 + 8 * t
            parts = [x_ref[pl.ds(start + k, 8), :] for k in range(-2, 3)]
            total = ((parts[0] + parts[1]) + (parts[3] + parts[4])) + parts[2]
            y_ref[pl.ds(p * NY + 8 * t, 8), :] = total * (1.0 / 125.0)
        return 0

    lax.fori_loop(0, 8, y_plane, 0)

    places = []
    dests = [dest_ref[k] for k in range(12)]
    for k in range(12):
        slot = jnp.int32(0)
        for other in range(k):
            slot = slot + (dests[other] == dests[k]).astype(jnp.int32)
        places.append(dests[k] * 2 + slot)

    quarter = lax.broadcasted_iota(jnp.int32, (8, NZ), 1) // BOX

    def pick(values):
        out = values[3]
        for b in range(3):
            out = jnp.where(quarter == b, values[b], out)
        return out

    for by in range(BOX_Y):
        for m in range(8):
            s = [y_ref[pl.ds(by * BOX + 4 * m + q, 8, stride=NY), :] for q in range(4)]
            moved = []
            for k in range(4):
                mixed = pick([s[(b + k) % 4] for b in range(4)])
                moved.append(turn(mixed, k * BOX) if k else mixed)
            for bz in range(4):
                out = pick([moved[(q - bz) % 4] for q in range(4)])
                send_ref[places[by * 4 + bz], pl.ds(send_row, 8), pl.ds(m * NZ, NZ)] = out


def clear(send_ref):
    def one(i, _):
        send_ref[i] = jnp.zeros(send_ref.shape[1:], jnp.float32)
        return 0

    lax.fori_loop(0, send_ref.shape[0], one, 0)


def rows_of(t):
    return pl.ds(pl.multiple_of(t * 8, 8), 8)


class Tiles:
    def __init__(self, q_ref, sems, parts):
        self.q_ref, self.sems, self.parts = q_ref, sems, parts

    def copies(self, t, kind):
        out = []
        for own, before, after, src, dst in self.parts:
            q = self.q_ref.at[:, dst, rows_of(t)]
            sem = self.sems.at[t]
            if len(own) == 1:
                out.append(pltpu.make_async_copy(own[0].at[:, src, rows_of(t)], q, sem))
            elif kind == "before":
                out.append(pltpu.make_async_copy(before.at[pl.ds(0, 5), src], q, sem))
            elif kind == "after":
                out.append(pltpu.make_async_copy(after.at[pl.ds(0, 5), src], q, sem))
            else:
                density, momentum, energy = own
                rows = rows_of(t - 1)
                place = self.q_ref.at
                out.append(pltpu.make_async_copy(density.at[src, rows], place[0, dst, rows_of(t)], sem))
                out.append(pltpu.make_async_copy(momentum.at[:, src, rows], place[pl.ds(1, 3), dst, rows_of(t)], sem))
                out.append(pltpu.make_async_copy(energy.at[src, rows], place[4, dst, rows_of(t)], sem))
        return out

    def each(self, t, act):
        @pl.when(t == 0)
        def _():
            for c in self.copies(t, "before"):
                act(c)

        @pl.when(t == TILES - 1)
        def _():
            for c in self.copies(t, "after"):
                act(c)

        @pl.when((t > 0) & (t < TILES - 1))
        def _():
            for c in self.copies(t, "own"):
                act(c)

    def start(self):
        def one(t, _):
            self.each(t, lambda c: c.start())
            return 0

        lax.fori_loop(0, TILES, one, 0)

    def wait(self, t):
        self.each(t, lambda c: c.wait())


def framed(ref):
    return ref.reshape(ref.shape[0] // STRIDE, STRIDE, NZ)


def dm_copies(dm, before, after, sem, dm_ref, own, place, count):
    src, dst = pl.ds(own, count), pl.ds(place, count)
    d3 = framed(dm_ref)
    return [
        pltpu.make_async_copy(dm.at[src], d3.at[dst, pl.ds(8, NY)], sem),
        pltpu.make_async_copy(before.at[5, src], d3.at[dst, pl.ds(0, 8)], sem),
        pltpu.make_async_copy(after.at[5, src], d3.at[dst, pl.ds(104, 8)], sem),
    ]


def out_copies(o_ref, planes, outs, sem, own, place, count):
    o4 = o_ref.reshape(5, planes, STRIDE, NZ)
    src, dst, mid = pl.ds(place, count), pl.ds(own, count), pl.ds(8, NY)
    density, momentum, energy = outs
    return [
        pltpu.make_async_copy(o4.at[0, src, mid], density.at[dst], sem),
        pltpu.make_async_copy(o4.at[pl.ds(1, 3), src, mid], momentum.at[:, dst], sem),
        pltpu.make_async_copy(o4.at[4, src, mid], energy.at[dst], sem),
    ]


def start_all(copies):
    for c in copies:
        c.start()


def wait_all(copies):
    for c in copies:
        c.wait()


def sums_copy(t_ref, base, count, out, sem):
    return pltpu.make_async_copy(framed(t_ref).at[pl.ds(base, count), pl.ds(0, FRAME)], out, sem)


def field_copies(density, momentum, energy, planes, rows, out, to, sem):
    return [
        pltpu.make_async_copy(density.at[planes, rows], out.at[0, :, to], sem),
        pltpu.make_async_copy(momentum.at[:, planes, rows], out.at[pl.ds(1, 3), :, to], sem),
        pltpu.make_async_copy(energy.at[planes, rows], out.at[4, :, to], sem),
    ]


def pack_y_kernel(density, momentum, energy, dm, y_last, y_first, sem):
    copies = []
    for out, rows in ((y_last, pl.ds(NY - 8, 8)), (y_first, pl.ds(0, 8))):
        copies += field_copies(density, momentum, energy, pl.ds(0, NX), rows, out, pl.ds(0, 8), sem)
        copies.append(pltpu.make_async_copy(dm.at[:, rows], out.at[5], sem))
    start_all(copies)
    wait_all(copies)


def pack_x_kernel(density, momentum, energy, y_before, y_after, x_last, x_first, sem):
    copies = []
    for out, planes in ((x_last, pl.ds(NX - 3, 3)), (x_first, pl.ds(0, 3))):
        copies += field_copies(density, momentum, energy, planes, pl.ds(0, NY), out, pl.ds(8, NY), sem)
        for side, to in ((y_before, pl.ds(0, 8)), (y_after, pl.ds(104, 8))):
            copies.append(pltpu.make_async_copy(side.at[pl.ds(0, 5), planes], out.at[:, :, to], sem))
    start_all(copies)
    wait_all(copies)


WIDE = 24


def x_kernel(density, momentum, energy, out, q_ref, s_ref, sems, out_sem):
    held = pl.ds(1, WIDE + 6)

    def copies(t):
        rows = rows_of(t)
        return [
            pltpu.make_async_copy(density.at[held, rows], q_ref.at[0, :, rows], sems.at[t]),
            pltpu.make_async_copy(momentum.at[:, held, rows], q_ref.at[pl.ds(1, 3), :, rows], sems.at[t]),
            pltpu.make_async_copy(energy.at[held, rows], q_ref.at[4, :, rows], sems.at[t]),
        ]

    def leaving(t):
        return pltpu.make_async_copy(s_ref.at[:, :, rows_of(t)], out.at[:, :, rows_of(t)], out_sem)

    def begin(t, _):
        start_all(copies(t))
        return 0

    def tile(t, _):
        wait_all(copies(t))
        rows = rows_of(t)

        def write(f, x, value):
            s_ref[f, x, rows, :] = value

        x_lines(((0, 0, WIDE),), lambda f, i: q_ref[f, i, rows, :], write)
        leaving(t).start()
        return 0

    def end(t, _):
        leaving(t).wait()
        return 0

    lax.fori_loop(0, NY // 8, begin, 0)
    lax.fori_loop(0, NY // 8, tile, 0)
    lax.fori_loop(0, NY // 8, end, 0)


def inner_kernel(dest, weights, swept, dm, y_before, y_after,
                 out_density, out_momentum, out_energy, out_sums, send,
                 q_ref, s_ref, o_ref, dm_ref, t_ref, w_ref, swept_ref, edge_ref, x_ref, y_ref, sems, sem, out_sem):
    held = pl.ds(1, WIDE + 6)
    s4 = s_ref.reshape(5, WIDE, STRIDE, NZ)
    outs = (out_density, out_momentum, out_energy)

    def swept_copy(g):
        planes = pl.ds(g * 8, 8)
        return pltpu.make_async_copy(swept.at[:, planes], s4.at[:, planes, pl.ds(8, NY)], sems.at[g])

    def leaving(g):
        return out_copies(o_ref, WIDE, outs, out_sem, 4 + g * 8, g * 8, 8)

    halo = [
        pltpu.make_async_copy(y_before.at[pl.ds(0, 5), held], q_ref.at[:, :, pl.ds(0, 8)], sem),
        pltpu.make_async_copy(y_after.at[pl.ds(0, 5), held], q_ref.at[:, :, pl.ds(8, 8)], sem),
    ] + dm_copies(dm, y_before, y_after, sem, dm_ref, 4, 0, WIDE)
    halo.append(pltpu.make_async_copy(weights, w_ref, sem))
    start_all(halo)
    for g in range(WIDE // 8):
        swept_copy(g).start()
    clear(send)
    wait_all(halo)
    x_sweep(q_ref, s_ref, WIDE, ((0, 0, WIDE),), 2, lambda t: None, lambda t: t * 104)
    yz_sweep(s_ref, dm_ref, o_ref, t_ref, w_ref, swept_ref, edge_ref, WIDE, lambda g: swept_copy(g).wait(), lambda g: start_all(leaving(g)))
    sums = sums_copy(t_ref, 0, WIDE, out_sums, sem)
    sums.start()
    for row, base in ((0, 2), (8, 10)):
        smooth(lambda p, r: t_ref[pl.ds((base + p) * STRIDE + r, 8), :], dest, x_ref, y_ref, send, row)
    sums.wait()
    for g in range(WIDE // 8):
        wait_all(leaving(g))


def outer_kernel(weights, density, momentum, energy, dm, y_before, y_after, x_before, x_after,
                 in_density, in_momentum, in_energy,
                 out_density, out_momentum, out_energy, out_sums, to_next, to_prev,
                 q_ref, s_ref, o_ref, dm_ref, t_ref, w_ref, swept_ref, edge_ref, sems, sem, out_sem):
    fields = (density, momentum, energy)
    tiles = Tiles(q_ref, sems, [
        (fields, y_before, y_after, pl.ds(25, 7), pl.ds(0, 7)),
        ((x_after,), None, None, pl.ds(0, 3), pl.ds(7, 3)),
        ((x_before,), None, None, pl.ds(0, 3), pl.ds(10, 3)),
        (fields, y_before, y_after, pl.ds(0, 7), pl.ds(13, 7)),
    ])
    tiles.start()
    copies = (dm_copies(dm, y_before, y_after, sem, dm_ref, 28, 0, 4)
              + dm_copies(dm, y_before, y_after, sem, dm_ref, 0, 4, 4))
    copies.append(pltpu.make_async_copy(weights, w_ref, sem))
    start_all(copies)
    x_sweep(q_ref, s_ref, 8, ((0, 0, 4), (10, 4, 4)), TILES, tiles.wait, lambda t: t * 8)
    wait_all(copies)
    yz_sweep(s_ref, dm_ref, o_ref, t_ref, w_ref, swept_ref, edge_ref, 8, lambda g: None, lambda g: None)
    outs = (out_density, out_momentum, out_energy)
    leaving = out_copies(o_ref, 8, outs, out_sem, 28, 0, 4) + out_copies(o_ref, 8, outs, out_sem, 0, 4, 4)
    leaving.append(sums_copy(t_ref, 0, 8, out_sums, out_sem))
    leaving.append(sums_copy(t_ref, 2, 2, to_next, out_sem))
    leaving.append(sums_copy(t_ref, 4, 2, to_prev, out_sem))
    start_all(leaving)
    wait_all(leaving)


def rest_kernel(dest, sums_inner, sums_outer, from_prev, from_next, send, w_ref, x_ref, y_ref, sem):
    def part(src, own, place, count):
        return pltpu.make_async_copy(src.at[pl.ds(own, count)], w_ref.at[pl.ds(place, count)], sem)

    copies = [
        part(from_prev, 0, 0, 2),
        part(sums_outer, 4, 2, 4),
        part(sums_inner, 0, 6, 6),
        part(sums_inner, 18, 12, 6),
        part(sums_outer, 0, 18, 4),
        part(from_next, 0, 22, 2),
    ]
    start_all(copies)
    clear(send)
    wait_all(copies)
    for row, base in ((0, 0), (8, 12)):
        smooth(lambda p, r: w_ref[base + p, pl.ds(r, 8), :], dest, x_ref, y_ref, send, row)


ANY = pl.BlockSpec(memory_space=pl.ANY)
SMEM = pl.BlockSpec(memory_space=pltpu.SMEM)
VMEM = pl.BlockSpec(memory_space=pltpu.VMEM)


def shape(*dims):
    return jax.ShapeDtypeStruct(dims, F32)


def params():
    return pltpu.CompilerParams(vmem_limit_bytes=VMEM_LIMIT)


def cost(micros):
    return pl.CostEstimate(flops=int(micros * COST), bytes_accessed=0, transcendentals=0)


def main_scratch(planes, held, rows):
    return [
        pltpu.VMEM((5, held, rows, NZ), F32),
        pltpu.VMEM((5 * planes * STRIDE, NZ), F32),
        pltpu.VMEM((5 * planes * STRIDE, NZ), F32),
        pltpu.VMEM((planes * STRIDE, NZ), F32),
        pltpu.VMEM((planes * STRIDE, NZ), F32),
        pltpu.VMEM((2 * NZ, 3 * NZ), jnp.bfloat16),
        pltpu.VMEM((5 * U * 8, NZ), F32),
        pltpu.VMEM((10 * U * 8, NZ), F32),
    ]


def semaphores():
    return [pltpu.SemaphoreType.DMA((TILES,)), pltpu.SemaphoreType.DMA, pltpu.SemaphoreType.DMA]


def smooth_scratch():
    return [pltpu.VMEM((8 * FRAME, NZ), F32), pltpu.VMEM((8 * NY, NZ), F32)]


FIELD_SHAPES = (shape(NX, NY, NZ), shape(3, NX, NY, NZ), shape(NX, NY, NZ))


def shifted(value, axis, by):
    size = lax.axis_size(axis)
    return lax.ppermute(value, axis, [(i, (i + by) % size) for i in range(size)])


def body(density, momentum, energy, dm_density, box_dest):
    dest = box_dest[0, 0, :, 0]
    fields = (density, momentum, energy)
    weights = lane_weights()
    y_last, y_first = pl.pallas_call(
        pack_y_kernel,
        out_shape=(shape(6, NX, 8, NZ),) * 2,
        in_specs=[ANY] * 4,
        out_specs=[VMEM] * 2,
        scratch_shapes=[pltpu.SemaphoreType.DMA],
        compiler_params=params(),
        cost_estimate=cost(3),
        name="pack_y",
    )(density, momentum, energy, dm_density)
    y_before = shifted(y_last, "grp", 1)
    y_after = shifted(y_first, "grp", -1)

    swept = pl.pallas_call(
        x_kernel,
        out_shape=shape(5, WIDE, NY, NZ),
        in_specs=[ANY] * 3,
        out_specs=ANY,
        scratch_shapes=[
            pltpu.VMEM((5, WIDE + 6, NY, NZ), F32), pltpu.VMEM((5, WIDE, NY, NZ), F32),
            pltpu.SemaphoreType.DMA((NY // 8,)), pltpu.SemaphoreType.DMA],
        compiler_params=params(),
        cost_estimate=cost(9),
        name="x_own",
    )(*fields)

    x_last, x_first = pl.pallas_call(
        pack_x_kernel,
        out_shape=(shape(5, 3, FRAME, NZ),) * 2,
        in_specs=[ANY] * 5,
        out_specs=[VMEM] * 2,
        scratch_shapes=[pltpu.SemaphoreType.DMA],
        compiler_params=params(),
        cost_estimate=cost(3),
        name="pack_x",
    )(*fields, y_before, y_after)
    x_before = shifted(x_last, "box", 1)
    x_after = shifted(x_first, "box", -1)

    def exchange(send, planes):
        return lax.all_to_all(send.reshape(16, 2, planes, 1024), "box", split_axis=0, concat_axis=0, tiled=True)

    inner = pl.pallas_call(
        inner_kernel,
        out_shape=FIELD_SHAPES + (shape(WIDE, FRAME, NZ), shape(32, 16, 1024)),
        in_specs=[SMEM] + [ANY] * 5,
        out_specs=[ANY] * 4 + [VMEM],
        scratch_shapes=main_scratch(WIDE, WIDE + 6, 16) + smooth_scratch() + semaphores(),
        compiler_params=params(),
        cost_estimate=cost(26),
        name="inner",
    )(dest, weights, swept, dm_density, y_before, y_after)
    *made, sums_inner, send_inner = inner
    got_inner = exchange(send_inner, 16)

    outer = pl.pallas_call(
        outer_kernel,
        out_shape=FIELD_SHAPES + (shape(8, FRAME, NZ), shape(2, FRAME, NZ), shape(2, FRAME, NZ)),
        in_specs=[ANY] * 12,
        out_specs=[ANY] * 6,
        scratch_shapes=main_scratch(8, 20, FRAME) + semaphores(),
        input_output_aliases={9: 0, 10: 1, 11: 2},
        compiler_params=params(),
        cost_estimate=cost(13),
        name="outer",
    )(weights, *fields, dm_density, y_before, y_after, x_before, x_after, *made)
    new_density, new_momentum, new_energy, sums_outer, to_next, to_prev = outer
    from_prev = shifted(to_next, "box", 1)
    from_next = shifted(to_prev, "box", -1)
    send_rest = pl.pallas_call(
        rest_kernel,
        out_shape=shape(32, 16, 1024),
        in_specs=[SMEM] + [ANY] * 4,
        out_specs=VMEM,
        scratch_shapes=[pltpu.VMEM((24, FRAME, NZ), F32)] + smooth_scratch() + [pltpu.SemaphoreType.DMA],
        compiler_params=params(),
        cost_estimate=cost(5),
        name="rest",
    )(dest, sums_inner, sums_outer, from_prev, from_next)
    send_rest, got_inner = lax.optimization_barrier((send_rest, got_inner))
    got_rest = exchange(send_rest, 16)
    kd = jnp.concatenate([got_rest[:, :, :8], got_inner, got_rest[:, :, 8:]], axis=2)
    return (new_density, new_momentum, new_energy, kd[None, None])


def solution(mesh):
    in_specs = (
        P("box", "grp", None),
        P(None, "box", "grp", None),
        P("box", "grp", None),
        P("box", "grp", None),
        P("grp", "box", None, None),
    )
    out_specs = (
        P("box", "grp", None),
        P(None, "box", "grp", None),
        P("box", "grp", None),
        P("grp", "box", None, None, None, None),
    )
    return jax.shard_map(body, mesh=mesh, in_specs=in_specs, out_specs=out_specs, check_vma=False)
```

```python
import functools
import math

import jax
import jax.numpy as jnp
import numpy as np
from jax import lax
from jax.experimental import pallas as pl
from jax.experimental.pallas import tpu as pltpu
from jax.sharding import PartitionSpec as P

F32 = jnp.float32
BOX = 32
BOX_Y = 3
BOX_Z = 4
NX = 32
NY = 96
NZ = 128
FRAME = 112
TILES = FRAME // 8
STRIDE = 120
STEP = 0.03
SCALES = (1.0, STEP, STEP, STEP, 2.0 * STEP * STEP)
UNSCALES = (1.0, 1.0 / STEP, 1.0 / STEP, 1.0 / STEP, 1.0 / (2.0 * STEP * STEP))
SOUND = math.sqrt(5.0 / 3.0)
TINY = 1e-30
COST = 1_100_000_000
VMEM_LIMIT = 64 * 1024 * 1024


def limit(value, other):
    bound = jnp.abs(other + other)
    return jnp.maximum(jnp.minimum(value, bound), -bound)


def between(value, end):
    return jnp.minimum(jnp.maximum(value, jnp.minimum(end, 0.0)), jnp.maximum(end, 0.0))


def deviation(d_prev, d_here, d_next):
    return between(0.5 * d_here + (d_prev - d_next) * (1.0 / 12.0), d_here)


def invert(x):
    return 1.0 / x


def state_of(u, normal):
    inverse = invert(u[0])
    squares = u[1] * u[1] + u[2] * u[2] + u[3] * u[3]
    pressure = u[4] - squares * inverse
    third = pressure * (1.0 / 3.0)
    velocity = u[normal] * inverse
    ratio = jnp.maximum(third * inverse, TINY)
    reach = jnp.abs(velocity) + SOUND * (ratio * lax.rsqrt(ratio))
    return velocity, third, reach


def flux(left, right, normal):
    v_left, p_left, reach_left = state_of(left, normal)
    v_right, p_right, reach_right = state_of(right, normal)
    reach = jnp.maximum(reach_left, reach_right)
    up = v_left + reach
    down = v_right - reach
    out = [left[f] * up + right[f] * down for f in range(5)]
    out[normal] = out[normal] + (p_left + p_right)
    work = p_left * v_left + p_right * v_right
    out[4] = out[4] + (work + work)
    return out


class Line:
    def __init__(self, normal):
        self.normal = normal
        self.q = []
        self.d = []
        self.dl = None
        self.er = None
        self.flux = None

    def load(self, q, carry):
        self.q = list(q)
        self.d = [carry[0:5], carry[5:10]]
        self.dl = carry[10:15]
        self.er = carry[15:20]
        self.flux = carry[20:25]

    def carry(self):
        return tuple(self.d[0]) + tuple(self.d[1]) + tuple(self.dl) + tuple(self.er) + tuple(self.flux)

    def push(self, new):
        q, d = self.q, self.d
        out = None
        if q:
            d0 = [a - b for a, b in zip(new, q[-1])]
            if len(d) >= 2:
                d2, d1 = d[-2], d[-1]
                dr = [deviation(*t) for t in zip(d2, d1, d0)]
                if self.dl is not None:
                    here = q[-2]
                    right = [c + limit(r, l) for c, r, l in zip(here, dr, self.dl)]
                    if self.er is not None:
                        left = [c + limit(l, r) for c, r, l in zip(here, dr, self.dl)]
                        now = flux(self.er, left, self.normal)
                        if self.flux is not None:
                            out = [c - (a - b) for c, a, b in zip(q[-3], now, self.flux)]
                        self.flux = now
                    self.er = right
                self.dl = [r - s for r, s in zip(dr, d1)]
            d.append(d0)
            self.d = d[-2:]
        q.append(new)
        self.q = q[-3:]
        return out


def turn(x, shift):
    return pltpu.roll(x, shift % NZ, 1)


def lane_weights():
    parts = []
    for taps in (((1, 1), (0, -1)), ((0, -5), (1, 7), (-1, -1), (2, -1)), tuple((k, 1) for k in range(-2, 3))):
        w = np.zeros((NZ, NZ), np.float32)
        for offset, value in taps:
            for j in range(NZ):
                w[(j + offset) % NZ, j] = value
        parts.append(w)
    w = np.concatenate(parts, axis=1)
    return jnp.asarray(np.concatenate([w, w], axis=0), jnp.bfloat16)


def mixed(x, weights):
    high = x.astype(jnp.bfloat16)
    low = (x - high.astype(F32)).astype(jnp.bfloat16)
    return jnp.dot(jnp.concatenate([high, low], axis=1), weights, preferred_element_type=F32)


def x_lines(segments, read, write):
    for base, out_base, count in segments:
        line = Line(1)
        for i in range(count + 6):
            new = [read(f, base + i) * SCALES[f] if f else read(f, base + i) for f in range(5)]
            out = line.push(new)
            if out is not None:
                for f in range(5):
                    write(f, out_base + i - 6, out[f])


def x_sweep(q_ref, s_ref, planes, segments, tiles, ready, place):
    def tile(t, _):
        ready(t)
        row = pl.multiple_of(t * 8, 8)
        to = pl.multiple_of(place(t), 8)

        def write(f, x, value):
            s_ref[pl.ds((f * planes + x) * STRIDE + to, 8), :] = value

        x_lines(segments, lambda f, i: q_ref[f, i, pl.ds(row, 8), :], write)
        return 0

    lax.fori_loop(0, tiles, tile, 0)


U = 50
PAIR = 2


def yz_sweep(s_ref, dm_ref, o_ref, t_ref, w_ref, swept_ref, edge_ref, planes, ready, done):
    def group(g, _):
        ready(g)

        def at(f, row):
            return pl.ds((f * planes + g * 8) * STRIDE + row, 8, stride=STRIDE)

        def rows(row):
            return [s_ref[at(f, row), :] for f in range(5)]

        def block(k, row, count):
            return pl.ds((k * U + row) * 8, count * 8)

        first = Line(2)
        for row in range(3, 9):
            first.push(rows(row))

        def some(b, carry):
            base = b * U + 6
            line = Line(2)
            line.load([rows(base), rows(base + 1), rows(base + 2)], carry)
            for r in range(U):
                swept = line.push(rows(base + 3 + r))
                for f in range(5):
                    swept_ref[block(f, r, 1), :] = swept[f]
            for f in range(5):
                q = swept_ref[block(f, 0, U), :]
                both = mixed(q, w_ref[:, :2 * NZ])
                d = both[:, :NZ]
                dr = between(both[:, NZ:] * (1.0 / 12.0), d)
                dl = turn(dr - d, 1)
                edge_ref[block(f, 0, U), :] = q + limit(dr, dl)
                edge_ref[block(5 + f, 0, U), :] = turn(q + limit(dl, dr), -1)
            for r in range(0, U, PAIR):
                left = [edge_ref[block(f, r, PAIR), :] for f in range(5)]
                right = [edge_ref[block(5 + f, r, PAIR), :] for f in range(5)]
                now = flux(left, right, 3)
                for f in range(5):
                    final = swept_ref[block(f, r, PAIR), :] - (now[f] - turn(now[f], 1))
                    if f == 0:
                        density = final
                    else:
                        final = final * UNSCALES[f]
                    for i in range(PAIR):
                        o_ref[at(f, base + r + i), :] = final[8 * i:8 * i + 8]
                for i in range(PAIR):
                    total = density[8 * i:8 * i + 8] + dm_ref[at(0, base + r + i), :]
                    edge_ref[block(0, r + i, 1), :] = total
            sums = mixed(edge_ref[block(0, 0, U), :], w_ref[:, 2 * NZ:])
            for r in range(U):
                t_ref[at(0, base + r), :] = sums[8 * r:8 * r + 8]
            return line.carry()

        lax.fori_loop(0, 100 // U, some, first.carry())
        done(g)
        return 0

    lax.fori_loop(0, planes // 8, group, 0)


def smooth(planes, dest_ref, x_ref, y_ref, send_ref, send_row):
    def x_tile(t, _):
        row = pl.multiple_of(t * 8, 8)
        values = [planes(p, row) for p in range(12)]
        pairs = [values[p] + values[p + 1] for p in range(11)]
        for p in range(8):
            x_ref[pl.ds(p * FRAME + row, 8), :] = pairs[p] + pairs[p + 2] + values[p + 4]
        return 0

    lax.fori_loop(0, TILES, x_tile, 0)

    def y_plane(p, _):
        for t in range(NY // 8):
            start = p * FRAME + 8 + 8 * t
            parts = [x_ref[pl.ds(start + k, 8), :] for k in range(-2, 3)]
            total = ((parts[0] + parts[1]) + (parts[3] + parts[4])) + parts[2]
            y_ref[pl.ds(p * NY + 8 * t, 8), :] = total * (1.0 / 125.0)
        return 0

    lax.fori_loop(0, 8, y_plane, 0)

    places = []
    dests = [dest_ref[k] for k in range(12)]
    for k in range(12):
        slot = jnp.int32(0)
        for other in range(k):
            slot = slot + (dests[other] == dests[k]).astype(jnp.int32)
        places.append(dests[k] * 2 + slot)

    quarter = lax.broadcasted_iota(jnp.int32, (8, NZ), 1) // BOX

    def pick(values):
        out = values[3]
        for b in range(3):
            out = jnp.where(quarter == b, values[b], out)
        return out

    for by in range(BOX_Y):
        for m in range(8):
            s = [y_ref[pl.ds(by * BOX + 4 * m + q, 8, stride=NY), :] for q in range(4)]
            moved = []
            for k in range(4):
                mixed = pick([s[(b + k) % 4] for b in range(4)])
                moved.append(turn(mixed, k * BOX) if k else mixed)
            for bz in range(4):
                out = pick([moved[(q - bz) % 4] for q in range(4)])
                send_ref[places[by * 4 + bz], pl.ds(send_row, 8), pl.ds(m * NZ, NZ)] = out


def clear(send_ref):
    def one(i, _):
        send_ref[i] = jnp.zeros(send_ref.shape[1:], jnp.float32)
        return 0

    lax.fori_loop(0, send_ref.shape[0], one, 0)


def rows_of(t):
    return pl.ds(pl.multiple_of(t * 8, 8), 8)


class Tiles:
    def __init__(self, q_ref, sems, parts):
        self.q_ref, self.sems, self.parts = q_ref, sems, parts

    def copies(self, t, kind):
        out = []
        for own, before, after, src, dst in self.parts:
            q = self.q_ref.at[:, dst, rows_of(t)]
            sem = self.sems.at[t]
            if len(own) == 1:
                out.append(pltpu.make_async_copy(own[0].at[:, src, rows_of(t)], q, sem))
            elif kind == "before":
                out.append(pltpu.make_async_copy(before.at[pl.ds(0, 5), src], q, sem))
            elif kind == "after":
                out.append(pltpu.make_async_copy(after.at[pl.ds(0, 5), src], q, sem))
            else:
                density, momentum, energy = own
                rows = rows_of(t - 1)
                place = self.q_ref.at
                out.append(pltpu.make_async_copy(density.at[src, rows], place[0, dst, rows_of(t)], sem))
                out.append(pltpu.make_async_copy(momentum.at[:, src, rows], place[pl.ds(1, 3), dst, rows_of(t)], sem))
                out.append(pltpu.make_async_copy(energy.at[src, rows], place[4, dst, rows_of(t)], sem))
        return out

    def each(self, t, act):
        @pl.when(t == 0)
        def _():
            for c in self.copies(t, "before"):
                act(c)

        @pl.when(t == TILES - 1)
        def _():
            for c in self.copies(t, "after"):
                act(c)

        @pl.when((t > 0) & (t < TILES - 1))
        def _():
            for c in self.copies(t, "own"):
                act(c)

    def start(self):
        def one(t, _):
            self.each(t, lambda c: c.start())
            return 0

        lax.fori_loop(0, TILES, one, 0)

    def wait(self, t):
        self.each(t, lambda c: c.wait())


def framed(ref):
    return ref.reshape(ref.shape[0] // STRIDE, STRIDE, NZ)


def dm_copies(dm, before, after, sem, dm_ref, own, place, count):
    src, dst = pl.ds(own, count), pl.ds(place, count)
    d3 = framed(dm_ref)
    return [
        pltpu.make_async_copy(dm.at[src], d3.at[dst, pl.ds(8, NY)], sem),
        pltpu.make_async_copy(before.at[5, src], d3.at[dst, pl.ds(0, 8)], sem),
        pltpu.make_async_copy(after.at[5, src], d3.at[dst, pl.ds(104, 8)], sem),
    ]


def out_copies(o_ref, planes, outs, sem, own, place, count):
    o4 = o_ref.reshape(5, planes, STRIDE, NZ)
    src, dst, mid = pl.ds(place, count), pl.ds(own, count), pl.ds(8, NY)
    density, momentum, energy = outs
    return [
        pltpu.make_async_copy(o4.at[0, src, mid], density.at[dst], sem),
        pltpu.make_async_copy(o4.at[pl.ds(1, 3), src, mid], momentum.at[:, dst], sem),
        pltpu.make_async_copy(o4.at[4, src, mid], energy.at[dst], sem),
    ]


def start_all(copies):
    for c in copies:
        c.start()


def wait_all(copies):
    for c in copies:
        c.wait()


def sums_copy(t_ref, base, count, out, sem):
    return pltpu.make_async_copy(framed(t_ref).at[pl.ds(base, count), pl.ds(0, FRAME)], out, sem)


def field_copies(density, momentum, energy, planes, rows, out, to, sem):
    return [
        pltpu.make_async_copy(density.at[planes, rows], out.at[0, :, to], sem),
        pltpu.make_async_copy(momentum.at[:, planes, rows], out.at[pl.ds(1, 3), :, to], sem),
        pltpu.make_async_copy(energy.at[planes, rows], out.at[4, :, to], sem),
    ]


def pack_y_kernel(density, momentum, energy, dm, y_last, y_first, sem):
    copies = []
    for out, rows in ((y_last, pl.ds(NY - 8, 8)), (y_first, pl.ds(0, 8))):
        copies += field_copies(density, momentum, energy, pl.ds(0, NX), rows, out, pl.ds(0, 8), sem)
        copies.append(pltpu.make_async_copy(dm.at[:, rows], out.at[5], sem))
    start_all(copies)
    wait_all(copies)


def pack_x_kernel(density, momentum, energy, y_before, y_after, x_last, x_first, sem):
    copies = []
    for out, planes in ((x_last, pl.ds(NX - 3, 3)), (x_first, pl.ds(0, 3))):
        copies += field_copies(density, momentum, energy, planes, pl.ds(0, NY), out, pl.ds(8, NY), sem)
        for side, to in ((y_before, pl.ds(0, 8)), (y_after, pl.ds(104, 8))):
            copies.append(pltpu.make_async_copy(side.at[pl.ds(0, 5), planes], out.at[:, :, to], sem))
    start_all(copies)
    wait_all(copies)


WIDE = 24


def x_kernel(density, momentum, energy, out, q_ref, s_ref, sems, out_sem):
    held = pl.ds(1, WIDE + 6)

    def copies(t):
        rows = rows_of(t)
        return [
            pltpu.make_async_copy(density.at[held, rows], q_ref.at[0, :, rows], sems.at[t]),
            pltpu.make_async_copy(momentum.at[:, held, rows], q_ref.at[pl.ds(1, 3), :, rows], sems.at[t]),
            pltpu.make_async_copy(energy.at[held, rows], q_ref.at[4, :, rows], sems.at[t]),
        ]

    def leaving(t):
        return pltpu.make_async_copy(s_ref.at[:, :, rows_of(t)], out.at[:, :, rows_of(t)], out_sem)

    def begin(t, _):
        start_all(copies(t))
        return 0

    def tile(t, _):
        wait_all(copies(t))
        rows = rows_of(t)

        def write(f, x, value):
            s_ref[f, x, rows, :] = value

        x_lines(((0, 0, WIDE),), lambda f, i: q_ref[f, i, rows, :], write)
        leaving(t).start()
        return 0

    def end(t, _):
        leaving(t).wait()
        return 0

    lax.fori_loop(0, NY // 8, begin, 0)
    lax.fori_loop(0, NY // 8, tile, 0)
    lax.fori_loop(0, NY // 8, end, 0)


def inner_kernel(dest, weights, swept, dm, y_before, y_after,
                 out_density, out_momentum, out_energy, out_sums, send,
                 q_ref, s_ref, o_ref, dm_ref, t_ref, w_ref, swept_ref, edge_ref, x_ref, y_ref, sems, sem, out_sem):
    held = pl.ds(1, WIDE + 6)
    s4 = s_ref.reshape(5, WIDE, STRIDE, NZ)
    outs = (out_density, out_momentum, out_energy)

    def swept_copy(g):
        planes = pl.ds(g * 8, 8)
        return pltpu.make_async_copy(swept.at[:, planes], s4.at[:, planes, pl.ds(8, NY)], sems.at[g])

    def leaving(g):
        return out_copies(o_ref, WIDE, outs, out_sem, 4 + g * 8, g * 8, 8)

    halo = [
        pltpu.make_async_copy(y_before.at[pl.ds(0, 5), held], q_ref.at[:, :, pl.ds(0, 8)], sem),
        pltpu.make_async_copy(y_after.at[pl.ds(0, 5), held], q_ref.at[:, :, pl.ds(8, 8)], sem),
    ] + dm_copies(dm, y_before, y_after, sem, dm_ref, 4, 0, WIDE)
    halo.append(pltpu.make_async_copy(weights, w_ref, sem))
    start_all(halo)
    for g in range(WIDE // 8):
        swept_copy(g).start()
    clear(send)
    wait_all(halo)
    x_sweep(q_ref, s_ref, WIDE, ((0, 0, WIDE),), 2, lambda t: None, lambda t: t * 104)
    yz_sweep(s_ref, dm_ref, o_ref, t_ref, w_ref, swept_ref, edge_ref, WIDE, lambda g: swept_copy(g).wait(), lambda g: start_all(leaving(g)))
    sums = sums_copy(t_ref, 0, WIDE, out_sums, sem)
    sums.start()
    for row, base in ((0, 2), (8, 10)):
        smooth(lambda p, r: t_ref[pl.ds((base + p) * STRIDE + r, 8), :], dest, x_ref, y_ref, send, row)
    sums.wait()
    for g in range(WIDE // 8):
        wait_all(leaving(g))


def outer_kernel(weights, density, momentum, energy, dm, y_before, y_after, x_before, x_after,
                 in_density, in_momentum, in_energy,
                 out_density, out_momentum, out_energy, out_sums, to_next, to_prev,
                 q_ref, s_ref, o_ref, dm_ref, t_ref, w_ref, swept_ref, edge_ref, sems, sem, out_sem):
    fields = (density, momentum, energy)
    tiles = Tiles(q_ref, sems, [
        (fields, y_before, y_after, pl.ds(25, 7), pl.ds(0, 7)),
        ((x_after,), None, None, pl.ds(0, 3), pl.ds(7, 3)),
        ((x_before,), None, None, pl.ds(0, 3), pl.ds(10, 3)),
        (fields, y_before, y_after, pl.ds(0, 7), pl.ds(13, 7)),
    ])
    tiles.start()
    copies = (dm_copies(dm, y_before, y_after, sem, dm_ref, 28, 0, 4)
              + dm_copies(dm, y_before, y_after, sem, dm_ref, 0, 4, 4))
    copies.append(pltpu.make_async_copy(weights, w_ref, sem))
    start_all(copies)
    x_sweep(q_ref, s_ref, 8, ((0, 0, 4), (10, 4, 4)), TILES, tiles.wait, lambda t: t * 8)
    wait_all(copies)
    yz_sweep(s_ref, dm_ref, o_ref, t_ref, w_ref, swept_ref, edge_ref, 8, lambda g: None, lambda g: None)
    outs = (out_density, out_momentum, out_energy)
    leaving = out_copies(o_ref, 8, outs, out_sem, 28, 0, 4) + out_copies(o_ref, 8, outs, out_sem, 0, 4, 4)
    leaving.append(sums_copy(t_ref, 0, 8, out_sums, out_sem))
    leaving.append(sums_copy(t_ref, 2, 2, to_next, out_sem))
    leaving.append(sums_copy(t_ref, 4, 2, to_prev, out_sem))
    start_all(leaving)
    wait_all(leaving)


def rest_kernel(dest, sums_inner, sums_outer, from_prev, from_next, send, w_ref, x_ref, y_ref, sem):
    def part(src, own, place, count):
        return pltpu.make_async_copy(src.at[pl.ds(own, count)], w_ref.at[pl.ds(place, count)], sem)

    copies = [
        part(from_prev, 0, 0, 2),
        part(sums_outer, 4, 2, 4),
        part(sums_inner, 0, 6, 6),
        part(sums_inner, 18, 12, 6),
        part(sums_outer, 0, 18, 4),
        part(from_next, 0, 22, 2),
    ]
    start_all(copies)
    clear(send)
    wait_all(copies)
    for row, base in ((0, 0), (8, 12)):
        smooth(lambda p, r: w_ref[base + p, pl.ds(r, 8), :], dest, x_ref, y_ref, send, row)


ANY = pl.BlockSpec(memory_space=pl.ANY)
SMEM = pl.BlockSpec(memory_space=pltpu.SMEM)
VMEM = pl.BlockSpec(memory_space=pltpu.VMEM)


def shape(*dims):
    return jax.ShapeDtypeStruct(dims, F32)


def params():
    return pltpu.CompilerParams(vmem_limit_bytes=VMEM_LIMIT)


def cost(micros):
    return pl.CostEstimate(flops=int(micros * COST), bytes_accessed=0, transcendentals=0)


def main_scratch(planes, held, rows):
    return [
        pltpu.VMEM((5, held, rows, NZ), F32),
        pltpu.VMEM((5 * planes * STRIDE, NZ), F32),
        pltpu.VMEM((5 * planes * STRIDE, NZ), F32),
        pltpu.VMEM((planes * STRIDE, NZ), F32),
        pltpu.VMEM((planes * STRIDE, NZ), F32),
        pltpu.VMEM((2 * NZ, 3 * NZ), jnp.bfloat16),
        pltpu.VMEM((5 * U * 8, NZ), F32),
        pltpu.VMEM((10 * U * 8, NZ), F32),
    ]


def semaphores():
    return [pltpu.SemaphoreType.DMA((TILES,)), pltpu.SemaphoreType.DMA, pltpu.SemaphoreType.DMA]


def smooth_scratch():
    return [pltpu.VMEM((8 * FRAME, NZ), F32), pltpu.VMEM((8 * NY, NZ), F32)]


FIELD_SHAPES = (shape(NX, NY, NZ), shape(3, NX, NY, NZ), shape(NX, NY, NZ))


def shifted(value, axis, by):
    size = lax.axis_size(axis)
    return lax.ppermute(value, axis, [(i, (i + by) % size) for i in range(size)])


def body(density, momentum, energy, dm_density, box_dest):
    dest = box_dest[0, 0, :, 0]
    fields = (density, momentum, energy)
    weights = lane_weights()
    y_last, y_first = pl.pallas_call(
        pack_y_kernel,
        out_shape=(shape(6, NX, 8, NZ),) * 2,
        in_specs=[ANY] * 4,
        out_specs=[VMEM] * 2,
        scratch_shapes=[pltpu.SemaphoreType.DMA],
        compiler_params=params(),
        cost_estimate=cost(3),
        name="pack_y",
    )(density, momentum, energy, dm_density)
    y_before = shifted(y_last, "grp", 1)
    y_after = shifted(y_first, "grp", -1)

    swept = pl.pallas_call(
        x_kernel,
        out_shape=shape(5, WIDE, NY, NZ),
        in_specs=[ANY] * 3,
        out_specs=ANY,
        scratch_shapes=[
            pltpu.VMEM((5, WIDE + 6, NY, NZ), F32), pltpu.VMEM((5, WIDE, NY, NZ), F32),
            pltpu.SemaphoreType.DMA((NY // 8,)), pltpu.SemaphoreType.DMA],
        compiler_params=params(),
        cost_estimate=cost(9),
        name="x_own",
    )(*fields)

    x_last, x_first = pl.pallas_call(
        pack_x_kernel,
        out_shape=(shape(5, 3, FRAME, NZ),) * 2,
        in_specs=[ANY] * 5,
        out_specs=[VMEM] * 2,
        scratch_shapes=[pltpu.SemaphoreType.DMA],
        compiler_params=params(),
        cost_estimate=cost(3),
        name="pack_x",
    )(*fields, y_before, y_after)
    x_before = shifted(x_last, "box", 1)
    x_after = shifted(x_first, "box", -1)

    def exchange(send, planes):
        return lax.all_to_all(send.reshape(16, 2, planes, 1024), "box", split_axis=0, concat_axis=0, tiled=True)

    inner = pl.pallas_call(
        inner_kernel,
        out_shape=FIELD_SHAPES + (shape(WIDE, FRAME, NZ), shape(32, 16, 1024)),
        in_specs=[SMEM] + [ANY] * 5,
        out_specs=[ANY] * 4 + [VMEM],
        scratch_shapes=main_scratch(WIDE, WIDE + 6, 16) + smooth_scratch() + semaphores(),
        compiler_params=params(),
        cost_estimate=cost(26),
        name="inner",
    )(dest, weights, swept, dm_density, y_before, y_after)
    *made, sums_inner, send_inner = inner
    got_inner = exchange(send_inner, 16)

    outer = pl.pallas_call(
        outer_kernel,
        out_shape=FIELD_SHAPES + (shape(8, FRAME, NZ), shape(2, FRAME, NZ), shape(2, FRAME, NZ)),
        in_specs=[ANY] * 12,
        out_specs=[ANY] * 6,
        scratch_shapes=main_scratch(8, 20, FRAME) + semaphores(),
        input_output_aliases={9: 0, 10: 1, 11: 2},
        compiler_params=params(),
        cost_estimate=cost(13),
        name="outer",
    )(weights, *fields, dm_density, y_before, y_after, x_before, x_after, *made)
    new_density, new_momentum, new_energy, sums_outer, to_next, to_prev = outer
    from_prev = shifted(to_next, "box", 1)
    from_next = shifted(to_prev, "box", -1)
    send_rest = pl.pallas_call(
        rest_kernel,
        out_shape=shape(32, 16, 1024),
        in_specs=[SMEM] + [ANY] * 4,
        out_specs=VMEM,
        scratch_shapes=[pltpu.VMEM((24, FRAME, NZ), F32)] + smooth_scratch() + [pltpu.SemaphoreType.DMA],
        compiler_params=params(),
        cost_estimate=cost(5),
        name="rest",
    )(dest, sums_inner, sums_outer, from_prev, from_next)
    send_rest, got_inner = lax.optimization_barrier((send_rest, got_inner))
    got_rest = exchange(send_rest, 16)
    kd = jnp.concatenate([got_rest[:, :, :8], got_inner, got_rest[:, :, 8:]], axis=2)
    return (new_density, new_momentum, new_energy, kd[None, None])


def solution(mesh):
    in_specs = (
        P("box", "grp", None),
        P(None, "box", "grp", None),
        P("box", "grp", None),
        P("box", "grp", None),
        P("grp", "box", None, None),
    )
    out_specs = (
        P("box", "grp", None),
        P(None, "box", "grp", None),
        P("box", "grp", None),
        P("grp", "box", None, None, None, None),
    )
    return jax.shard_map(body, mesh=mesh, in_specs=in_specs, out_specs=out_specs, check_vma=False)
```

```python
import functools
import math

import jax
import jax.numpy as jnp
import numpy as np
from jax import lax
from jax.experimental import pallas as pl
from jax.experimental.pallas import tpu as pltpu
from jax.sharding import PartitionSpec as P

F32 = jnp.float32
BOX = 32
BOX_Y = 3
BOX_Z = 4
NX = 32
NY = 96
NZ = 128
FRAME = 112
TILES = FRAME // 8
STRIDE = 120
STEP = 0.03
SCALES = (1.0, STEP, STEP, STEP, 2.0 * STEP * STEP)
UNSCALES = (1.0, 1.0 / STEP, 1.0 / STEP, 1.0 / STEP, 1.0 / (2.0 * STEP * STEP))
SOUND = math.sqrt(5.0 / 3.0)
TINY = 1e-30
COST = 1_100_000_000
MIB = 1024 * 1024


def limit(value, other):
    bound = jnp.abs(other + other)
    return jnp.maximum(jnp.minimum(value, bound), -bound)


def between(value, end):
    return jnp.minimum(jnp.maximum(value, jnp.minimum(end, 0.0)), jnp.maximum(end, 0.0))


def deviation(d_prev, d_here, d_next):
    return between(0.5 * d_here + (d_prev - d_next) * (1.0 / 12.0), d_here)


def invert(x):
    return 1.0 / x


def state_of(u, normal):
    inverse = invert(u[0])
    squares = u[1] * u[1] + u[2] * u[2] + u[3] * u[3]
    pressure = u[4] - squares * inverse
    third = pressure * (1.0 / 3.0)
    velocity = u[normal] * inverse
    ratio = jnp.maximum(third * inverse, TINY)
    reach = jnp.abs(velocity) + SOUND * (ratio * lax.rsqrt(ratio))
    return velocity, third, reach


def flux(left, right, normal):
    v_left, p_left, reach_left = state_of(left, normal)
    v_right, p_right, reach_right = state_of(right, normal)
    reach = jnp.maximum(reach_left, reach_right)
    up = v_left + reach
    down = v_right - reach
    out = [left[f] * up + right[f] * down for f in range(5)]
    out[normal] = out[normal] + (p_left + p_right)
    work = p_left * v_left + p_right * v_right
    out[4] = out[4] + (work + work)
    return out


class Line:
    def __init__(self, normal):
        self.normal = normal
        self.q = []
        self.d = []
        self.dl = None
        self.er = None
        self.flux = None

    def load(self, q, carry):
        self.q = list(q)
        self.d = [carry[0:5], carry[5:10]]
        self.dl = carry[10:15]
        self.er = carry[15:20]
        self.flux = carry[20:25]

    def carry(self):
        return tuple(self.d[0]) + tuple(self.d[1]) + tuple(self.dl) + tuple(self.er) + tuple(self.flux)

    def push(self, new):
        q, d = self.q, self.d
        out = None
        if q:
            d0 = [a - b for a, b in zip(new, q[-1])]
            if len(d) >= 2:
                d2, d1 = d[-2], d[-1]
                dr = [deviation(*t) for t in zip(d2, d1, d0)]
                if self.dl is not None:
                    here = q[-2]
                    right = [c + limit(r, l) for c, r, l in zip(here, dr, self.dl)]
                    if self.er is not None:
                        left = [c + limit(l, r) for c, r, l in zip(here, dr, self.dl)]
                        now = flux(self.er, left, self.normal)
                        if self.flux is not None:
                            out = [c - (a - b) for c, a, b in zip(q[-3], now, self.flux)]
                        self.flux = now
                    self.er = right
                self.dl = [r - s for r, s in zip(dr, d1)]
            d.append(d0)
            self.d = d[-2:]
        q.append(new)
        self.q = q[-3:]
        return out


def turn(x, shift):
    return pltpu.roll(x, shift % NZ, 1)


def lane_weights():
    parts = []
    for taps in (((1, 1), (0, -1)), ((0, -5), (1, 7), (-1, -1), (2, -1)), tuple((k, 1) for k in range(-2, 3))):
        w = np.zeros((NZ, NZ), np.float32)
        for offset, value in taps:
            for j in range(NZ):
                w[(j + offset) % NZ, j] = value
        parts.append(w)
    w = np.concatenate(parts, axis=1)
    return jnp.asarray(np.concatenate([w, w], axis=0), jnp.bfloat16)


def mixed(x, weights):
    high = x.astype(jnp.bfloat16)
    low = (x - high.astype(F32)).astype(jnp.bfloat16)
    return jnp.dot(jnp.concatenate([high, low], axis=1), weights, preferred_element_type=F32)


def x_lines(segments, read, write):
    for base, out_base, count in segments:
        line = Line(1)
        for i in range(count + 6):
            new = [read(f, base + i) * SCALES[f] if f else read(f, base + i) for f in range(5)]
            out = line.push(new)
            if out is not None:
                for f in range(5):
                    write(f, out_base + i - 6, out[f])


def x_sweep(q_ref, s_ref, planes, segments, tiles, ready, place):
    def tile(t, _):
        ready(t)
        row = pl.multiple_of(t * 8, 8)
        to = pl.multiple_of(place(t), 8)

        def write(f, x, value):
            s_ref[pl.ds((f * planes + x) * STRIDE + to, 8), :] = value

        x_lines(segments, lambda f, i: q_ref[f, i, pl.ds(row, 8), :], write)
        return 0

    lax.fori_loop(0, tiles, tile, 0)


U = 50
PAIR = 2


def yz_sweep(s_ref, dm_ref, o_ref, t_ref, w_ref, swept_ref, edge_ref, planes, ready, done):
    def group(g, _):
        ready(g)

        def at(f, row):
            return pl.ds((f * planes + g * 8) * STRIDE + row, 8, stride=STRIDE)

        def rows(row):
            return [s_ref[at(f, row), :] for f in range(5)]

        def block(k, row, count):
            return pl.ds((k * U + row) * 8, count * 8)

        first = Line(2)
        for row in range(3, 9):
            first.push(rows(row))

        def some(b, carry):
            base = b * U + 6
            line = Line(2)
            line.load([rows(base), rows(base + 1), rows(base + 2)], carry)
            for r in range(U):
                swept = line.push(rows(base + 3 + r))
                for f in range(5):
                    swept_ref[block(f, r, 1), :] = swept[f]
            for f in range(5):
                q = swept_ref[block(f, 0, U), :]
                both = mixed(q, w_ref[:, :2 * NZ])
                d = both[:, :NZ]
                dr = between(both[:, NZ:] * (1.0 / 12.0), d)
                dl = turn(dr - d, 1)
                edge_ref[block(f, 0, U), :] = q + limit(dr, dl)
                edge_ref[block(5 + f, 0, U), :] = turn(q + limit(dl, dr), -1)
            for r in range(0, U, PAIR):
                left = [edge_ref[block(f, r, PAIR), :] for f in range(5)]
                right = [edge_ref[block(5 + f, r, PAIR), :] for f in range(5)]
                now = flux(left, right, 3)
                for f in range(5):
                    final = swept_ref[block(f, r, PAIR), :] - (now[f] - turn(now[f], 1))
                    if f == 0:
                        density = final
                    else:
                        final = final * UNSCALES[f]
                    for i in range(PAIR):
                        o_ref[at(f, base + r + i), :] = final[8 * i:8 * i + 8]
                for i in range(PAIR):
                    total = density[8 * i:8 * i + 8] + dm_ref[at(0, base + r + i), :]
                    edge_ref[block(0, r + i, 1), :] = total
            sums = mixed(edge_ref[block(0, 0, U), :], w_ref[:, 2 * NZ:])
            for r in range(U):
                t_ref[at(0, base + r), :] = sums[8 * r:8 * r + 8]
            return line.carry()

        lax.fori_loop(0, 100 // U, some, first.carry())
        done(g)
        return 0

    lax.fori_loop(0, planes // 8, group, 0)


def smooth(planes, dest_ref, x_ref, y_ref, send_ref, send_row):
    def x_tile(t, _):
        row = pl.multiple_of(t * 8, 8)
        values = [planes(p, row) for p in range(12)]
        pairs = [values[p] + values[p + 1] for p in range(11)]
        for p in range(8):
            x_ref[pl.ds(p * FRAME + row, 8), :] = pairs[p] + pairs[p + 2] + values[p + 4]
        return 0

    lax.fori_loop(0, TILES, x_tile, 0)

    def y_plane(p, _):
        for t in range(NY // 8):
            start = p * FRAME + 8 + 8 * t
            parts = [x_ref[pl.ds(start + k, 8), :] for k in range(-2, 3)]
            total = ((parts[0] + parts[1]) + (parts[3] + parts[4])) + parts[2]
            y_ref[pl.ds(p * NY + 8 * t, 8), :] = total * (1.0 / 125.0)
        return 0

    lax.fori_loop(0, 8, y_plane, 0)

    places = []
    dests = [dest_ref[k] for k in range(12)]
    for k in range(12):
        slot = jnp.int32(0)
        for other in range(k):
            slot = slot + (dests[other] == dests[k]).astype(jnp.int32)
        places.append(dests[k] * 2 + slot)

    quarter = lax.broadcasted_iota(jnp.int32, (8, NZ), 1) // BOX

    def pick(values):
        out = values[3]
        for b in range(3):
            out = jnp.where(quarter == b, values[b], out)
        return out

    for by in range(BOX_Y):
        for m in range(8):
            s = [y_ref[pl.ds(by * BOX + 4 * m + q, 8, stride=NY), :] for q in range(4)]
            moved = []
            for k in range(4):
                mixed = pick([s[(b + k) % 4] for b in range(4)])
                moved.append(turn(mixed, k * BOX) if k else mixed)
            for bz in range(4):
                out = pick([moved[(q - bz) % 4] for q in range(4)])
                send_ref[places[by * 4 + bz], pl.ds(send_row, 8), pl.ds(m * NZ, NZ)] = out


def clear(send_ref):
    def one(i, _):
        send_ref[i] = jnp.zeros(send_ref.shape[1:], jnp.float32)
        return 0

    lax.fori_loop(0, send_ref.shape[0], one, 0)


def rows_of(t):
    return pl.ds(pl.multiple_of(t * 8, 8), 8)


class Tiles:
    def __init__(self, q_ref, sems, parts):
        self.q_ref, self.sems, self.parts = q_ref, sems, parts

    def copies(self, t, kind):
        out = []
        for own, before, after, src, dst in self.parts:
            q = self.q_ref.at[:, dst, rows_of(t)]
            sem = self.sems.at[t]
            if len(own) == 1:
                out.append(pltpu.make_async_copy(own[0].at[:, src, rows_of(t)], q, sem))
            elif kind == "before":
                out.append(pltpu.make_async_copy(before.at[pl.ds(0, 5), src], q, sem))
            elif kind == "after":
                out.append(pltpu.make_async_copy(after.at[pl.ds(0, 5), src], q, sem))
            else:
                density, momentum, energy = own
                rows = rows_of(t - 1)
                place = self.q_ref.at
                out.append(pltpu.make_async_copy(density.at[src, rows], place[0, dst, rows_of(t)], sem))
                out.append(pltpu.make_async_copy(momentum.at[:, src, rows], place[pl.ds(1, 3), dst, rows_of(t)], sem))
                out.append(pltpu.make_async_copy(energy.at[src, rows], place[4, dst, rows_of(t)], sem))
        return out

    def each(self, t, act):
        @pl.when(t == 0)
        def _():
            for c in self.copies(t, "before"):
                act(c)

        @pl.when(t == TILES - 1)
        def _():
            for c in self.copies(t, "after"):
                act(c)

        @pl.when((t > 0) & (t < TILES - 1))
        def _():
            for c in self.copies(t, "own"):
                act(c)

    def start(self):
        def one(t, _):
            self.each(t, lambda c: c.start())
            return 0

        lax.fori_loop(0, TILES, one, 0)

    def wait(self, t):
        self.each(t, lambda c: c.wait())


def framed(ref):
    return ref.reshape(ref.shape[0] // STRIDE, STRIDE, NZ)


def dm_copies(dm, before, after, sem, dm_ref, own, place, count):
    src, dst = pl.ds(own, count), pl.ds(place, count)
    d3 = framed(dm_ref)
    return [
        pltpu.make_async_copy(dm.at[src], d3.at[dst, pl.ds(8, NY)], sem),
        pltpu.make_async_copy(before.at[5, src], d3.at[dst, pl.ds(0, 8)], sem),
        pltpu.make_async_copy(after.at[5, src], d3.at[dst, pl.ds(104, 8)], sem),
    ]


def out_copies(o_ref, planes, outs, sem, own, place, count):
    o4 = o_ref.reshape(5, planes, STRIDE, NZ)
    src, dst, mid = pl.ds(place, count), pl.ds(own, count), pl.ds(8, NY)
    density, momentum, energy = outs
    return [
        pltpu.make_async_copy(o4.at[0, src, mid], density.at[dst], sem),
        pltpu.make_async_copy(o4.at[pl.ds(1, 3), src, mid], momentum.at[:, dst], sem),
        pltpu.make_async_copy(o4.at[4, src, mid], energy.at[dst], sem),
    ]


def start_all(copies):
    for c in copies:
        c.start()


def wait_all(copies):
    for c in copies:
        c.wait()


def sums_copy(t_ref, base, count, out, sem):
    return pltpu.make_async_copy(framed(t_ref).at[pl.ds(base, count), pl.ds(0, FRAME)], out, sem)


def field_copies(density, momentum, energy, planes, rows, out, to, sem):
    return [
        pltpu.make_async_copy(density.at[planes, rows], out.at[0, :, to], sem),
        pltpu.make_async_copy(momentum.at[:, planes, rows], out.at[pl.ds(1, 3), :, to], sem),
        pltpu.make_async_copy(energy.at[planes, rows], out.at[4, :, to], sem),
    ]


def pack_y_kernel(density, momentum, energy, dm, y_last, y_first, sem):
    copies = []
    for out, rows in ((y_last, pl.ds(NY - 8, 8)), (y_first, pl.ds(0, 8))):
        copies += field_copies(density, momentum, energy, pl.ds(0, NX), rows, out, pl.ds(0, 8), sem)
        copies.append(pltpu.make_async_copy(dm.at[:, rows], out.at[5], sem))
    start_all(copies)
    wait_all(copies)


def pack_x_kernel(density, momentum, energy, y_before, y_after, x_last, x_first, sem):
    copies = []
    for out, planes in ((x_last, pl.ds(NX - 3, 3)), (x_first, pl.ds(0, 3))):
        copies += field_copies(density, momentum, energy, planes, pl.ds(0, NY), out, pl.ds(8, NY), sem)
        for side, to in ((y_before, pl.ds(0, 8)), (y_after, pl.ds(104, 8))):
            copies.append(pltpu.make_async_copy(side.at[pl.ds(0, 5), planes], out.at[:, :, to], sem))
    start_all(copies)
    wait_all(copies)


WIDE = 24


def x_kernel(density, momentum, energy, out, q_ref, s_ref, sems, out_sem):
    held = pl.ds(1, WIDE + 6)

    def copies(t):
        rows = rows_of(t)
        return [
            pltpu.make_async_copy(density.at[held, rows], q_ref.at[0, :, rows], sems.at[t]),
            pltpu.make_async_copy(momentum.at[:, held, rows], q_ref.at[pl.ds(1, 3), :, rows], sems.at[t]),
            pltpu.make_async_copy(energy.at[held, rows], q_ref.at[4, :, rows], sems.at[t]),
        ]

    def leaving(t):
        return pltpu.make_async_copy(s_ref.at[:, :, rows_of(t)], out.at[:, :, rows_of(t)], out_sem)

    def begin(t, _):
        start_all(copies(t))
        return 0

    def tile(t, _):
        wait_all(copies(t))
        rows = rows_of(t)

        def write(f, x, value):
            s_ref[f, x, rows, :] = value

        x_lines(((0, 0, WIDE),), lambda f, i: q_ref[f, i, rows, :], write)
        leaving(t).start()
        return 0

    def end(t, _):
        leaving(t).wait()
        return 0

    lax.fori_loop(0, NY // 8, begin, 0)
    lax.fori_loop(0, NY // 8, tile, 0)
    lax.fori_loop(0, NY // 8, end, 0)


def inner_kernel(dest, weights, swept, dm, y_before, y_after,
                 out_density, out_momentum, out_energy, out_sums, send,
                 q_ref, s_ref, o_ref, dm_ref, t_ref, w_ref, swept_ref, edge_ref, x_ref, y_ref, sems, sem, out_sem):
    held = pl.ds(1, WIDE + 6)
    s4 = s_ref.reshape(5, WIDE, STRIDE, NZ)
    outs = (out_density, out_momentum, out_energy)

    def swept_copy(g):
        planes = pl.ds(g * 8, 8)
        return pltpu.make_async_copy(swept.at[:, planes], s4.at[:, planes, pl.ds(8, NY)], sems.at[g])

    def leaving(g):
        return out_copies(o_ref, WIDE, outs, out_sem, 4 + g * 8, g * 8, 8)

    halo = [
        pltpu.make_async_copy(y_before.at[pl.ds(0, 5), held], q_ref.at[:, :, pl.ds(0, 8)], sem),
        pltpu.make_async_copy(y_after.at[pl.ds(0, 5), held], q_ref.at[:, :, pl.ds(8, 8)], sem),
    ] + dm_copies(dm, y_before, y_after, sem, dm_ref, 4, 0, WIDE)
    halo.append(pltpu.make_async_copy(weights, w_ref, sem))
    start_all(halo)
    for g in range(WIDE // 8):
        swept_copy(g).start()
    clear(send)
    wait_all(halo)
    x_sweep(q_ref, s_ref, WIDE, ((0, 0, WIDE),), 2, lambda t: None, lambda t: t * 104)
    yz_sweep(s_ref, dm_ref, o_ref, t_ref, w_ref, swept_ref, edge_ref, WIDE, lambda g: swept_copy(g).wait(), lambda g: start_all(leaving(g)))
    sums = sums_copy(t_ref, 0, WIDE, out_sums, sem)
    sums.start()
    for row, base in ((0, 2), (8, 10)):
        smooth(lambda p, r: t_ref[pl.ds((base + p) * STRIDE + r, 8), :], dest, x_ref, y_ref, send, row)
    sums.wait()
    for g in range(WIDE // 8):
        wait_all(leaving(g))


def outer_kernel(weights, density, momentum, energy, dm, y_before, y_after, x_before, x_after,
                 in_density, in_momentum, in_energy,
                 out_density, out_momentum, out_energy, out_sums, to_next, to_prev,
                 q_ref, s_ref, o_ref, dm_ref, t_ref, w_ref, swept_ref, edge_ref, sems, sem, out_sem):
    fields = (density, momentum, energy)
    tiles = Tiles(q_ref, sems, [
        (fields, y_before, y_after, pl.ds(25, 7), pl.ds(0, 7)),
        ((x_after,), None, None, pl.ds(0, 3), pl.ds(7, 3)),
        ((x_before,), None, None, pl.ds(0, 3), pl.ds(10, 3)),
        (fields, y_before, y_after, pl.ds(0, 7), pl.ds(13, 7)),
    ])
    tiles.start()
    copies = (dm_copies(dm, y_before, y_after, sem, dm_ref, 28, 0, 4)
              + dm_copies(dm, y_before, y_after, sem, dm_ref, 0, 4, 4))
    copies.append(pltpu.make_async_copy(weights, w_ref, sem))
    start_all(copies)
    x_sweep(q_ref, s_ref, 8, ((0, 0, 4), (10, 4, 4)), TILES, tiles.wait, lambda t: t * 8)
    wait_all(copies)
    yz_sweep(s_ref, dm_ref, o_ref, t_ref, w_ref, swept_ref, edge_ref, 8, lambda g: None, lambda g: None)
    outs = (out_density, out_momentum, out_energy)
    leaving = out_copies(o_ref, 8, outs, out_sem, 28, 0, 4) + out_copies(o_ref, 8, outs, out_sem, 0, 4, 4)
    leaving.append(sums_copy(t_ref, 0, 8, out_sums, out_sem))
    leaving.append(sums_copy(t_ref, 2, 2, to_next, out_sem))
    leaving.append(sums_copy(t_ref, 4, 2, to_prev, out_sem))
    start_all(leaving)
    wait_all(leaving)


def rest_kernel(dest, sums_inner, sums_outer, from_prev, from_next, send, w_ref, x_ref, y_ref, sem):
    def part(src, own, place, count):
        return pltpu.make_async_copy(src.at[pl.ds(own, count)], w_ref.at[pl.ds(place, count)], sem)

    copies = [
        part(from_prev, 0, 0, 2),
        part(sums_outer, 4, 2, 4),
        part(sums_inner, 0, 6, 6),
        part(sums_inner, 18, 12, 6),
        part(sums_outer, 0, 18, 4),
        part(from_next, 0, 22, 2),
    ]
    start_all(copies)
    clear(send)
    wait_all(copies)
    for row, base in ((0, 0), (8, 12)):
        smooth(lambda p, r: w_ref[base + p, pl.ds(r, 8), :], dest, x_ref, y_ref, send, row)


ANY = pl.BlockSpec(memory_space=pl.ANY)
SMEM = pl.BlockSpec(memory_space=pltpu.SMEM)
VMEM = pl.BlockSpec(memory_space=pltpu.VMEM)


def shape(*dims):
    return jax.ShapeDtypeStruct(dims, F32)


def params(mib):
    return pltpu.CompilerParams(vmem_limit_bytes=mib * MIB)


def cost(micros):
    return pl.CostEstimate(flops=int(micros * COST), bytes_accessed=0, transcendentals=0)


def main_scratch(planes, held, rows):
    return [
        pltpu.VMEM((5, held, rows, NZ), F32),
        pltpu.VMEM((5 * planes * STRIDE, NZ), F32),
        pltpu.VMEM((5 * planes * STRIDE, NZ), F32),
        pltpu.VMEM((planes * STRIDE, NZ), F32),
        pltpu.VMEM((planes * STRIDE, NZ), F32),
        pltpu.VMEM((2 * NZ, 3 * NZ), jnp.bfloat16),
        pltpu.VMEM((5 * U * 8, NZ), F32),
        pltpu.VMEM((10 * U * 8, NZ), F32),
    ]


def semaphores():
    return [pltpu.SemaphoreType.DMA((TILES,)), pltpu.SemaphoreType.DMA, pltpu.SemaphoreType.DMA]


def smooth_scratch():
    return [pltpu.VMEM((8 * FRAME, NZ), F32), pltpu.VMEM((8 * NY, NZ), F32)]


FIELD_SHAPES = (shape(NX, NY, NZ), shape(3, NX, NY, NZ), shape(NX, NY, NZ))


def shifted(value, axis, by):
    size = lax.axis_size(axis)
    return lax.ppermute(value, axis, [(i, (i + by) % size) for i in range(size)])


def body(density, momentum, energy, dm_density, box_dest):
    dest = box_dest[0, 0, :, 0]
    fields = (density, momentum, energy)
    weights = lane_weights()
    y_last, y_first = pl.pallas_call(
        pack_y_kernel,
        out_shape=(shape(6, NX, 8, NZ),) * 2,
        in_specs=[ANY] * 4,
        out_specs=[VMEM] * 2,
        scratch_shapes=[pltpu.SemaphoreType.DMA],
        compiler_params=params(64),
        cost_estimate=cost(3),
        name="pack_y",
    )(density, momentum, energy, dm_density)
    y_before = shifted(y_last, "grp", 1)
    y_after = shifted(y_first, "grp", -1)

    swept = pl.pallas_call(
        x_kernel,
        out_shape=shape(5, WIDE, NY, NZ),
        in_specs=[ANY] * 3,
        out_specs=ANY,
        scratch_shapes=[
            pltpu.VMEM((5, WIDE + 6, NY, NZ), F32), pltpu.VMEM((5, WIDE, NY, NZ), F32),
            pltpu.SemaphoreType.DMA((NY // 8,)), pltpu.SemaphoreType.DMA],
        compiler_params=params(64),
        cost_estimate=cost(9),
        name="x_own",
    )(*fields)

    x_last, x_first = pl.pallas_call(
        pack_x_kernel,
        out_shape=(shape(5, 3, FRAME, NZ),) * 2,
        in_specs=[ANY] * 5,
        out_specs=[VMEM] * 2,
        scratch_shapes=[pltpu.SemaphoreType.DMA],
        compiler_params=params(64),
        cost_estimate=cost(3),
        name="pack_x",
    )(*fields, y_before, y_after)
    x_before = shifted(x_last, "box", 1)
    x_after = shifted(x_first, "box", -1)

    def exchange(send, planes):
        return lax.all_to_all(send.reshape(16, 2, planes, 1024), "box", split_axis=0, concat_axis=0, tiled=True)

    inner = pl.pallas_call(
        inner_kernel,
        out_shape=FIELD_SHAPES + (shape(WIDE, FRAME, NZ), shape(32, 16, 1024)),
        in_specs=[SMEM] + [ANY] * 5,
        out_specs=[ANY] * 4 + [VMEM],
        scratch_shapes=main_scratch(WIDE, WIDE + 6, 16) + smooth_scratch() + semaphores(),
        compiler_params=params(64),
        cost_estimate=cost(26),
        name="inner",
    )(dest, weights, swept, dm_density, y_before, y_after)
    *made, sums_inner, send_inner = inner
    got_inner = exchange(send_inner, 16)

    outer = pl.pallas_call(
        outer_kernel,
        out_shape=FIELD_SHAPES + (shape(8, FRAME, NZ), shape(2, FRAME, NZ), shape(2, FRAME, NZ)),
        in_specs=[ANY] * 12,
        out_specs=[ANY] * 6,
        scratch_shapes=main_scratch(8, 20, FRAME) + semaphores(),
        input_output_aliases={9: 0, 10: 1, 11: 2},
        compiler_params=params(54),
        cost_estimate=cost(13),
        name="outer",
    )(weights, *fields, dm_density, y_before, y_after, x_before, x_after, *made)
    new_density, new_momentum, new_energy, sums_outer, to_next, to_prev = outer
    from_prev = shifted(to_next, "box", 1)
    from_next = shifted(to_prev, "box", -1)
    send_rest = pl.pallas_call(
        rest_kernel,
        out_shape=shape(32, 16, 1024),
        in_specs=[SMEM] + [ANY] * 4,
        out_specs=VMEM,
        scratch_shapes=[pltpu.VMEM((24, FRAME, NZ), F32)] + smooth_scratch() + [pltpu.SemaphoreType.DMA],
        compiler_params=params(54),
        cost_estimate=cost(5),
        name="rest",
    )(dest, sums_inner, sums_outer, from_prev, from_next)
    send_rest, got_inner = lax.optimization_barrier((send_rest, got_inner))
    got_rest = exchange(send_rest, 16)
    kd = jnp.concatenate([got_rest[:, :, :8], got_inner, got_rest[:, :, 8:]], axis=2)
    return (new_density, new_momentum, new_energy, kd[None, None])


def solution(mesh):
    in_specs = (
        P("box", "grp", None),
        P(None, "box", "grp", None),
        P("box", "grp", None),
        P("box", "grp", None),
        P("grp", "box", None, None),
    )
    out_specs = (
        P("box", "grp", None),
        P(None, "box", "grp", None),
        P("box", "grp", None),
        P("grp", "box", None, None, None, None),
    )
    return jax.shard_map(body, mesh=mesh, in_specs=in_specs, out_specs=out_specs, check_vma=False)
```

```python
import functools
import math

import jax
import jax.numpy as jnp
import numpy as np
from jax import lax
from jax.experimental import pallas as pl
from jax.experimental.pallas import tpu as pltpu
from jax.sharding import PartitionSpec as P

F32 = jnp.float32
BOX = 32
BOX_Y = 3
BOX_Z = 4
NX = 32
NY = 96
NZ = 128
FRAME = 112
TILES = FRAME // 8
STRIDE = 120
STEP = 0.03
SCALES = (1.0, STEP, STEP, STEP, 2.0 * STEP * STEP)
UNSCALES = (1.0, 1.0 / STEP, 1.0 / STEP, 1.0 / STEP, 1.0 / (2.0 * STEP * STEP))
SOUND = math.sqrt(5.0 / 3.0)
TINY = 1e-30
COST = 1_100_000_000
MIB = 1024 * 1024


def limit(value, other):
    bound = jnp.abs(other + other)
    return jnp.maximum(jnp.minimum(value, bound), -bound)


def between(value, end):
    return jnp.minimum(jnp.maximum(value, jnp.minimum(end, 0.0)), jnp.maximum(end, 0.0))


def deviation(d_prev, d_here, d_next):
    return between(0.5 * d_here + (d_prev - d_next) * (1.0 / 12.0), d_here)


def invert(x):
    return 1.0 / x


def state_of(u, normal):
    inverse = invert(u[0])
    squares = u[1] * u[1] + u[2] * u[2] + u[3] * u[3]
    pressure = u[4] - squares * inverse
    third = pressure * (1.0 / 3.0)
    velocity = u[normal] * inverse
    ratio = jnp.maximum(third * inverse, TINY)
    reach = jnp.abs(velocity) + SOUND * (ratio * lax.rsqrt(ratio))
    return velocity, third, reach


def flux(left, right, normal):
    v_left, p_left, reach_left = state_of(left, normal)
    v_right, p_right, reach_right = state_of(right, normal)
    reach = jnp.maximum(reach_left, reach_right)
    up = v_left + reach
    down = v_right - reach
    out = [left[f] * up + right[f] * down for f in range(5)]
    out[normal] = out[normal] + (p_left + p_right)
    work = p_left * v_left + p_right * v_right
    out[4] = out[4] + (work + work)
    return out


class Line:
    def __init__(self, normal):
        self.normal = normal
        self.q = []
        self.d = []
        self.dl = None
        self.er = None
        self.flux = None

    def load(self, q, carry):
        self.q = list(q)
        self.d = [carry[0:5], carry[5:10]]
        self.dl = carry[10:15]
        self.er = carry[15:20]
        self.flux = carry[20:25]

    def carry(self):
        return tuple(self.d[0]) + tuple(self.d[1]) + tuple(self.dl) + tuple(self.er) + tuple(self.flux)

    def push(self, new):
        q, d = self.q, self.d
        out = None
        if q:
            d0 = [a - b for a, b in zip(new, q[-1])]
            if len(d) >= 2:
                d2, d1 = d[-2], d[-1]
                dr = [deviation(*t) for t in zip(d2, d1, d0)]
                if self.dl is not None:
                    here = q[-2]
                    right = [c + limit(r, l) for c, r, l in zip(here, dr, self.dl)]
                    if self.er is not None:
                        left = [c + limit(l, r) for c, r, l in zip(here, dr, self.dl)]
                        now = flux(self.er, left, self.normal)
                        if self.flux is not None:
                            out = [c - (a - b) for c, a, b in zip(q[-3], now, self.flux)]
                        self.flux = now
                    self.er = right
                self.dl = [r - s for r, s in zip(dr, d1)]
            d.append(d0)
            self.d = d[-2:]
        q.append(new)
        self.q = q[-3:]
        return out


def turn(x, shift):
    return pltpu.roll(x, shift % NZ, 1)


def lane_weights():
    parts = []
    for taps in (((1, 1), (0, -1)), ((0, -5), (1, 7), (-1, -1), (2, -1)), tuple((k, 1) for k in range(-2, 3))):
        w = np.zeros((NZ, NZ), np.float32)
        for offset, value in taps:
            for j in range(NZ):
                w[(j + offset) % NZ, j] = value
        parts.append(w)
    w = np.concatenate(parts, axis=1)
    return jnp.asarray(np.concatenate([w, w], axis=0), jnp.bfloat16)


def mixed(x, weights):
    high = x.astype(jnp.bfloat16)
    low = (x - high.astype(F32)).astype(jnp.bfloat16)
    return jnp.dot(jnp.concatenate([high, low], axis=1), weights, preferred_element_type=F32)


def x_lines(segments, read, write):
    for base, out_base, count in segments:
        line = Line(1)
        for i in range(count + 6):
            new = [read(f, base + i) * SCALES[f] if f else read(f, base + i) for f in range(5)]
            out = line.push(new)
            if out is not None:
                for f in range(5):
                    write(f, out_base + i - 6, out[f])


def x_sweep(q_ref, s_ref, planes, segments, tiles, ready, place):
    def tile(t, _):
        ready(t)
        row = pl.multiple_of(t * 8, 8)
        to = pl.multiple_of(place(t), 8)

        def write(f, x, value):
            s_ref[pl.ds((f * planes + x) * STRIDE + to, 8), :] = value

        x_lines(segments, lambda f, i: q_ref[f, i, pl.ds(row, 8), :], write)
        return 0

    lax.fori_loop(0, tiles, tile, 0)


U = 50
PAIR = 2


def yz_sweep(s_ref, dm_ref, o_ref, t_ref, w_ref, swept_ref, edge_ref, planes, ready, done):
    def group(g, _):
        ready(g)

        def at(f, row):
            return pl.ds((f * planes + g * 8) * STRIDE + row, 8, stride=STRIDE)

        def rows(row):
            return [s_ref[at(f, row), :] for f in range(5)]

        def block(k, row, count):
            return pl.ds((k * U + row) * 8, count * 8)

        first = Line(2)
        for row in range(3, 9):
            first.push(rows(row))

        def some(b, carry):
            base = b * U + 6
            line = Line(2)
            line.load([rows(base), rows(base + 1), rows(base + 2)], carry)
            for r in range(U):
                swept = line.push(rows(base + 3 + r))
                for f in range(5):
                    swept_ref[block(f, r, 1), :] = swept[f]
            for f in range(5):
                q = swept_ref[block(f, 0, U), :]
                both = mixed(q, w_ref[:, :2 * NZ])
                d = both[:, :NZ]
                dr = between(both[:, NZ:] * (1.0 / 12.0), d)
                dl = turn(dr - d, 1)
                edge_ref[block(f, 0, U), :] = q + limit(dr, dl)
                edge_ref[block(5 + f, 0, U), :] = turn(q + limit(dl, dr), -1)
            for r in range(0, U, PAIR):
                left = [edge_ref[block(f, r, PAIR), :] for f in range(5)]
                right = [edge_ref[block(5 + f, r, PAIR), :] for f in range(5)]
                now = flux(left, right, 3)
                for f in range(5):
                    final = swept_ref[block(f, r, PAIR), :] - (now[f] - turn(now[f], 1))
                    if f == 0:
                        density = final
                    else:
                        final = final * UNSCALES[f]
                    for i in range(PAIR):
                        o_ref[at(f, base + r + i), :] = final[8 * i:8 * i + 8]
                for i in range(PAIR):
                    total = density[8 * i:8 * i + 8] + dm_ref[at(0, base + r + i), :]
                    edge_ref[block(0, r + i, 1), :] = total
            sums = mixed(edge_ref[block(0, 0, U), :], w_ref[:, 2 * NZ:])
            for r in range(U):
                t_ref[at(0, base + r), :] = sums[8 * r:8 * r + 8]
            return line.carry()

        lax.fori_loop(0, 100 // U, some, first.carry())
        done(g)
        return 0

    lax.fori_loop(0, planes // 8, group, 0)


def smooth(planes, dest_ref, x_ref, y_ref, send_ref, send_row):
    average(planes, x_ref, y_ref, 0)
    put_boxes(dest_ref, y_ref, 0, send_ref, send_row)


def five_rows(load):
    parts = [load(k) for k in range(-2, 3)]
    return (((parts[0] + parts[1]) + (parts[3] + parts[4])) + parts[2]) * (1.0 / 125.0)


def average(planes, x_ref, y_ref, y_base):

    def x_tile(t, _):
        row = pl.multiple_of(t * 8, 8)
        values = [planes(p, row) for p in range(12)]
        pairs = [values[p] + values[p + 1] for p in range(11)]
        for p in range(8):
            x_ref[pl.ds(p * FRAME + row, 8), :] = pairs[p] + pairs[p + 2] + values[p + 4]
        return 0

    lax.fori_loop(0, TILES, x_tile, 0)

    def y_plane(p, _):
        for t in range(NY // 8):
            start = p * FRAME + 8 + 8 * t
            y_ref[pl.ds(y_base + p * NY + 8 * t, 8), :] = five_rows(lambda k: x_ref[pl.ds(start + k, 8), :])
        return 0

    lax.fori_loop(0, 8, y_plane, 0)


def put_boxes(dest_ref, y_ref, y_base, send_ref, send_row):
    places = []
    dests = [dest_ref[k] for k in range(12)]
    for k in range(12):
        slot = jnp.int32(0)
        for other in range(k):
            slot = slot + (dests[other] == dests[k]).astype(jnp.int32)
        places.append(dests[k] * 2 + slot)

    quarter = lax.broadcasted_iota(jnp.int32, (8, NZ), 1) // BOX

    def pick(values):
        out = values[3]
        for b in range(3):
            out = jnp.where(quarter == b, values[b], out)
        return out

    for by in range(BOX_Y):
        for m in range(8):
            s = [y_ref[pl.ds(y_base + by * BOX + 4 * m + q, 8, stride=NY), :] for q in range(4)]
            moved = []
            for k in range(4):
                mixed = pick([s[(b + k) % 4] for b in range(4)])
                moved.append(turn(mixed, k * BOX) if k else mixed)
            for bz in range(4):
                out = pick([moved[(q - bz) % 4] for q in range(4)])
                send_ref[places[by * 4 + bz], pl.ds(send_row, 8), pl.ds(m * NZ, NZ)] = out


def clear(send_ref):
    def one(i, _):
        send_ref[i] = jnp.zeros(send_ref.shape[1:], jnp.float32)
        return 0

    lax.fori_loop(0, send_ref.shape[0], one, 0)


def rows_of(t):
    return pl.ds(pl.multiple_of(t * 8, 8), 8)


class Tiles:
    def __init__(self, q_ref, sems, parts):
        self.q_ref, self.sems, self.parts = q_ref, sems, parts

    def copies(self, t, kind):
        out = []
        for own, before, after, src, dst in self.parts:
            q = self.q_ref.at[:, dst, rows_of(t)]
            sem = self.sems.at[t]
            if len(own) == 1:
                out.append(pltpu.make_async_copy(own[0].at[:, src, rows_of(t)], q, sem))
            elif kind == "before":
                out.append(pltpu.make_async_copy(before.at[pl.ds(0, 5), src], q, sem))
            elif kind == "after":
                out.append(pltpu.make_async_copy(after.at[pl.ds(0, 5), src], q, sem))
            else:
                density, momentum, energy = own
                rows = rows_of(t - 1)
                place = self.q_ref.at
                out.append(pltpu.make_async_copy(density.at[src, rows], place[0, dst, rows_of(t)], sem))
                out.append(pltpu.make_async_copy(momentum.at[:, src, rows], place[pl.ds(1, 3), dst, rows_of(t)], sem))
                out.append(pltpu.make_async_copy(energy.at[src, rows], place[4, dst, rows_of(t)], sem))
        return out

    def each(self, t, act):
        @pl.when(t == 0)
        def _():
            for c in self.copies(t, "before"):
                act(c)

        @pl.when(t == TILES - 1)
        def _():
            for c in self.copies(t, "after"):
                act(c)

        @pl.when((t > 0) & (t < TILES - 1))
        def _():
            for c in self.copies(t, "own"):
                act(c)

    def start(self):
        def one(t, _):
            self.each(t, lambda c: c.start())
            return 0

        lax.fori_loop(0, TILES, one, 0)

    def wait(self, t):
        self.each(t, lambda c: c.wait())


def framed(ref):
    return ref.reshape(ref.shape[0] // STRIDE, STRIDE, NZ)


def dm_copies(dm, before, after, sem, dm_ref, own, place, count):
    src, dst = pl.ds(own, count), pl.ds(place, count)
    d3 = framed(dm_ref)
    return [
        pltpu.make_async_copy(dm.at[src], d3.at[dst, pl.ds(8, NY)], sem),
        pltpu.make_async_copy(before.at[5, src], d3.at[dst, pl.ds(0, 8)], sem),
        pltpu.make_async_copy(after.at[5, src], d3.at[dst, pl.ds(104, 8)], sem),
    ]


def out_copies(o_ref, planes, outs, sem, own, place, count):
    o4 = o_ref.reshape(5, planes, STRIDE, NZ)
    src, dst, mid = pl.ds(place, count), pl.ds(own, count), pl.ds(8, NY)
    density, momentum, energy = outs
    return [
        pltpu.make_async_copy(o4.at[0, src, mid], density.at[dst], sem),
        pltpu.make_async_copy(o4.at[pl.ds(1, 3), src, mid], momentum.at[:, dst], sem),
        pltpu.make_async_copy(o4.at[4, src, mid], energy.at[dst], sem),
    ]


def start_all(copies):
    for c in copies:
        c.start()


def wait_all(copies):
    for c in copies:
        c.wait()


def sums_copy(t_ref, base, count, out, sem):
    return pltpu.make_async_copy(framed(t_ref).at[pl.ds(base, count), pl.ds(0, FRAME)], out, sem)


def field_copies(density, momentum, energy, planes, rows, out, to, sem):
    return [
        pltpu.make_async_copy(density.at[planes, rows], out.at[0, :, to], sem),
        pltpu.make_async_copy(momentum.at[:, planes, rows], out.at[pl.ds(1, 3), :, to], sem),
        pltpu.make_async_copy(energy.at[planes, rows], out.at[4, :, to], sem),
    ]


def pack_y_kernel(density, momentum, energy, dm, y_last, y_first, sem):
    copies = []
    for out, rows in ((y_last, pl.ds(NY - 8, 8)), (y_first, pl.ds(0, 8))):
        copies += field_copies(density, momentum, energy, pl.ds(0, NX), rows, out, pl.ds(0, 8), sem)
        copies.append(pltpu.make_async_copy(dm.at[:, rows], out.at[5], sem))
    start_all(copies)
    wait_all(copies)


def pack_x_kernel(density, momentum, energy, y_before, y_after, x_last, x_first, sem):
    copies = []
    for out, planes in ((x_last, pl.ds(NX - 3, 3)), (x_first, pl.ds(0, 3))):
        copies += field_copies(density, momentum, energy, planes, pl.ds(0, NY), out, pl.ds(8, NY), sem)
        for side, to in ((y_before, pl.ds(0, 8)), (y_after, pl.ds(104, 8))):
            copies.append(pltpu.make_async_copy(side.at[pl.ds(0, 5), planes], out.at[:, :, to], sem))
    start_all(copies)
    wait_all(copies)


WIDE = 24


def x_kernel(density, momentum, energy, out, q_ref, s_ref, sems, out_sem):
    held = pl.ds(1, WIDE + 6)

    def copies(t):
        rows = rows_of(t)
        return [
            pltpu.make_async_copy(density.at[held, rows], q_ref.at[0, :, rows], sems.at[t]),
            pltpu.make_async_copy(momentum.at[:, held, rows], q_ref.at[pl.ds(1, 3), :, rows], sems.at[t]),
            pltpu.make_async_copy(energy.at[held, rows], q_ref.at[4, :, rows], sems.at[t]),
        ]

    def leaving(t):
        return pltpu.make_async_copy(s_ref.at[:, :, rows_of(t)], out.at[:, :, rows_of(t)], out_sem)

    def begin(t, _):
        start_all(copies(t))
        return 0

    def tile(t, _):
        wait_all(copies(t))
        rows = rows_of(t)

        def write(f, x, value):
            s_ref[f, x, rows, :] = value

        x_lines(((0, 0, WIDE),), lambda f, i: q_ref[f, i, rows, :], write)
        leaving(t).start()
        return 0

    def end(t, _):
        leaving(t).wait()
        return 0

    lax.fori_loop(0, NY // 8, begin, 0)
    lax.fori_loop(0, NY // 8, tile, 0)
    lax.fori_loop(0, NY // 8, end, 0)


def inner_kernel(dest, weights, swept, dm, y_before, y_after,
                 out_density, out_momentum, out_energy, out_sums, send,
                 q_ref, s_ref, o_ref, dm_ref, t_ref, w_ref, swept_ref, edge_ref, x_ref, y_ref, sems, sem, out_sem):
    held = pl.ds(1, WIDE + 6)
    s4 = s_ref.reshape(5, WIDE, STRIDE, NZ)
    outs = (out_density, out_momentum, out_energy)

    def swept_copy(g):
        planes = pl.ds(g * 8, 8)
        return pltpu.make_async_copy(swept.at[:, planes], s4.at[:, planes, pl.ds(8, NY)], sems.at[g])

    def leaving(g):
        return out_copies(o_ref, WIDE, outs, out_sem, 4 + g * 8, g * 8, 8)

    halo = [
        pltpu.make_async_copy(y_before.at[pl.ds(0, 5), held], q_ref.at[:, :, pl.ds(0, 8)], sem),
        pltpu.make_async_copy(y_after.at[pl.ds(0, 5), held], q_ref.at[:, :, pl.ds(8, 8)], sem),
    ] + dm_copies(dm, y_before, y_after, sem, dm_ref, 4, 0, WIDE)
    halo.append(pltpu.make_async_copy(weights, w_ref, sem))
    start_all(halo)
    for g in range(WIDE // 8):
        swept_copy(g).start()
    clear(send)
    wait_all(halo)
    x_sweep(q_ref, s_ref, WIDE, ((0, 0, WIDE),), 2, lambda t: None, lambda t: t * 104)
    yz_sweep(s_ref, dm_ref, o_ref, t_ref, w_ref, swept_ref, edge_ref, WIDE, lambda g: swept_copy(g).wait(), lambda g: start_all(leaving(g)))
    sums = sums_copy(t_ref, 0, WIDE, out_sums, sem)
    sums.start()
    for row, base in ((0, 2), (8, 10)):
        smooth(lambda p, r: t_ref[pl.ds((base + p) * STRIDE + r, 8), :], dest, x_ref, y_ref, send, row)
    sums.wait()
    for g in range(WIDE // 8):
        wait_all(leaving(g))


def outer_kernel(weights, density, momentum, energy, dm, y_before, y_after, x_before, x_after,
                 in_density, in_momentum, in_energy,
                 out_density, out_momentum, out_energy, out_sums, to_next, to_prev,
                 q_ref, s_ref, o_ref, dm_ref, t_ref, w_ref, swept_ref, edge_ref, sems, sem, out_sem):
    fields = (density, momentum, energy)
    tiles = Tiles(q_ref, sems, [
        (fields, y_before, y_after, pl.ds(25, 7), pl.ds(0, 7)),
        ((x_after,), None, None, pl.ds(0, 3), pl.ds(7, 3)),
        ((x_before,), None, None, pl.ds(0, 3), pl.ds(10, 3)),
        (fields, y_before, y_after, pl.ds(0, 7), pl.ds(13, 7)),
    ])
    tiles.start()
    copies = (dm_copies(dm, y_before, y_after, sem, dm_ref, 28, 0, 4)
              + dm_copies(dm, y_before, y_after, sem, dm_ref, 0, 4, 4))
    copies.append(pltpu.make_async_copy(weights, w_ref, sem))
    start_all(copies)
    x_sweep(q_ref, s_ref, 8, ((0, 0, 4), (10, 4, 4)), TILES, tiles.wait, lambda t: t * 8)
    wait_all(copies)
    yz_sweep(s_ref, dm_ref, o_ref, t_ref, w_ref, swept_ref, edge_ref, 8, lambda g: None, lambda g: None)
    outs = (out_density, out_momentum, out_energy)
    leaving = out_copies(o_ref, 8, outs, out_sem, 28, 0, 4) + out_copies(o_ref, 8, outs, out_sem, 0, 4, 4)
    leaving.append(sums_copy(t_ref, 0, 8, out_sums, out_sem))
    leaving.append(sums_copy(t_ref, 2, 2, to_next, out_sem))
    leaving.append(sums_copy(t_ref, 4, 2, to_prev, out_sem))
    start_all(leaving)
    wait_all(leaving)


def near_kernel(sums_inner, sums_outer, part, w_ref, x_ref, sem):
    def planes(src, own, place, count):
        return pltpu.make_async_copy(src.at[pl.ds(own, count)], w_ref.at[pl.ds(place, count)], sem)

    copies = [
        planes(sums_outer, 4, 2, 4),
        planes(sums_inner, 0, 6, 6),
        planes(sums_inner, 18, 12, 6),
        planes(sums_outer, 0, 18, 4),
    ]
    start_all(copies)
    for p in (0, 1, 22, 23):
        w_ref[p] = jnp.zeros((FRAME, NZ), F32)
    wait_all(copies)
    for n in range(2):
        average(lambda p, r: w_ref[12 * n + p, pl.ds(r, 8), :], x_ref, part, n * 8 * NY)


def rest_kernel(dest, part, from_prev, from_next, send, y_ref, f_ref, sem):
    copies = [
        pltpu.make_async_copy(part, y_ref, sem),
        pltpu.make_async_copy(from_prev, f_ref.at[pl.ds(0, 2)], sem),
        pltpu.make_async_copy(from_next, f_ref.at[pl.ds(2, 2)], sem),
    ]
    start_all(copies)
    clear(send)
    wait_all(copies)
    for t in range(NY // 8):
        mean = [five_rows(lambda k: f_ref[i, pl.ds(8 + 8 * t + k, 8), :]) for i in range(4)]
        for plane, more in ((0, mean[0] + mean[1]), (1, mean[1]), (14, mean[2]), (15, mean[2] + mean[3])):
            at = pl.ds(plane * NY + 8 * t, 8)
            y_ref[at, :] = y_ref[at, :] + more
    for n in range(2):
        put_boxes(dest, y_ref, n * 8 * NY, send, 8 * n)


ANY = pl.BlockSpec(memory_space=pl.ANY)
SMEM = pl.BlockSpec(memory_space=pltpu.SMEM)
VMEM = pl.BlockSpec(memory_space=pltpu.VMEM)


def shape(*dims):
    return jax.ShapeDtypeStruct(dims, F32)


def params(mib):
    return pltpu.CompilerParams(vmem_limit_bytes=mib * MIB)


def cost(micros):
    return pl.CostEstimate(flops=int(micros * COST), bytes_accessed=0, transcendentals=0)


def main_scratch(planes, held, rows):
    return [
        pltpu.VMEM((5, held, rows, NZ), F32),
        pltpu.VMEM((5 * planes * STRIDE, NZ), F32),
        pltpu.VMEM((5 * planes * STRIDE, NZ), F32),
        pltpu.VMEM((planes * STRIDE, NZ), F32),
        pltpu.VMEM((planes * STRIDE, NZ), F32),
        pltpu.VMEM((2 * NZ, 3 * NZ), jnp.bfloat16),
        pltpu.VMEM((5 * U * 8, NZ), F32),
        pltpu.VMEM((10 * U * 8, NZ), F32),
    ]


def semaphores():
    return [pltpu.SemaphoreType.DMA((TILES,)), pltpu.SemaphoreType.DMA, pltpu.SemaphoreType.DMA]


def smooth_scratch():
    return [pltpu.VMEM((8 * FRAME, NZ), F32), pltpu.VMEM((8 * NY, NZ), F32)]


FIELD_SHAPES = (shape(NX, NY, NZ), shape(3, NX, NY, NZ), shape(NX, NY, NZ))


def shifted(value, axis, by):
    size = lax.axis_size(axis)
    return lax.ppermute(value, axis, [(i, (i + by) % size) for i in range(size)])


def body(density, momentum, energy, dm_density, box_dest):
    dest = box_dest[0, 0, :, 0]
    fields = (density, momentum, energy)
    weights = lane_weights()
    y_last, y_first = pl.pallas_call(
        pack_y_kernel,
        out_shape=(shape(6, NX, 8, NZ),) * 2,
        in_specs=[ANY] * 4,
        out_specs=[VMEM] * 2,
        scratch_shapes=[pltpu.SemaphoreType.DMA],
        compiler_params=params(64),
        cost_estimate=cost(3),
        name="pack_y",
    )(density, momentum, energy, dm_density)
    y_before = shifted(y_last, "grp", 1)
    y_after = shifted(y_first, "grp", -1)

    swept = pl.pallas_call(
        x_kernel,
        out_shape=shape(5, WIDE, NY, NZ),
        in_specs=[ANY] * 3,
        out_specs=ANY,
        scratch_shapes=[
            pltpu.VMEM((5, WIDE + 6, NY, NZ), F32), pltpu.VMEM((5, WIDE, NY, NZ), F32),
            pltpu.SemaphoreType.DMA((NY // 8,)), pltpu.SemaphoreType.DMA],
        compiler_params=params(64),
        cost_estimate=cost(9),
        name="x_own",
    )(*fields)

    x_last, x_first = pl.pallas_call(
        pack_x_kernel,
        out_shape=(shape(5, 3, FRAME, NZ),) * 2,
        in_specs=[ANY] * 5,
        out_specs=[VMEM] * 2,
        scratch_shapes=[pltpu.SemaphoreType.DMA],
        compiler_params=params(64),
        cost_estimate=cost(3),
        name="pack_x",
    )(*fields, y_before, y_after)
    x_before = shifted(x_last, "box", 1)
    x_after = shifted(x_first, "box", -1)

    def exchange(send, planes):
        return lax.all_to_all(send.reshape(16, 2, planes, 1024), "box", split_axis=0, concat_axis=0, tiled=True)

    inner = pl.pallas_call(
        inner_kernel,
        out_shape=FIELD_SHAPES + (shape(WIDE, FRAME, NZ), shape(32, 16, 1024)),
        in_specs=[SMEM] + [ANY] * 5,
        out_specs=[ANY] * 4 + [VMEM],
        scratch_shapes=main_scratch(WIDE, WIDE + 6, 16) + smooth_scratch() + semaphores(),
        compiler_params=params(64),
        cost_estimate=cost(26),
        name="inner",
    )(dest, weights, swept, dm_density, y_before, y_after)
    *made, sums_inner, send_inner = inner
    got_inner = exchange(send_inner, 16)

    outer = pl.pallas_call(
        outer_kernel,
        out_shape=FIELD_SHAPES + (shape(8, FRAME, NZ), shape(2, FRAME, NZ), shape(2, FRAME, NZ)),
        in_specs=[ANY] * 12,
        out_specs=[ANY] * 6,
        scratch_shapes=main_scratch(8, 20, FRAME) + semaphores(),
        input_output_aliases={9: 0, 10: 1, 11: 2},
        compiler_params=params(54),
        cost_estimate=cost(13),
        name="outer",
    )(weights, *fields, dm_density, y_before, y_after, x_before, x_after, *made)
    new_density, new_momentum, new_energy, sums_outer, to_next, to_prev = outer
    from_prev = shifted(to_next, "box", 1)
    from_next = shifted(to_prev, "box", -1)
    part = pl.pallas_call(
        near_kernel,
        out_shape=shape(16 * NY, NZ),
        in_specs=[ANY] * 2,
        out_specs=VMEM,
        scratch_shapes=[pltpu.VMEM((24, FRAME, NZ), F32), pltpu.VMEM((8 * FRAME, NZ), F32), pltpu.SemaphoreType.DMA],
        compiler_params=params(54),
        cost_estimate=cost(3),
        name="near",
    )(sums_inner, sums_outer)
    send_rest = pl.pallas_call(
        rest_kernel,
        out_shape=shape(32, 16, 1024),
        in_specs=[SMEM] + [ANY] * 3,
        out_specs=VMEM,
        scratch_shapes=[pltpu.VMEM((16 * NY, NZ), F32), pltpu.VMEM((4, FRAME, NZ), F32), pltpu.SemaphoreType.DMA],
        compiler_params=params(54),
        cost_estimate=cost(3),
        name="rest",
    )(dest, part, from_prev, from_next)
    send_rest, got_inner = lax.optimization_barrier((send_rest, got_inner))
    got_rest = exchange(send_rest, 16)
    kd = jnp.concatenate([got_rest[:, :, :8], got_inner, got_rest[:, :, 8:]], axis=2)
    return (new_density, new_momentum, new_energy, kd[None, None])


def solution(mesh):
    in_specs = (
        P("box", "grp", None),
        P(None, "box", "grp", None),
        P("box", "grp", None),
        P("box", "grp", None),
        P("grp", "box", None, None),
    )
    out_specs = (
        P("box", "grp", None),
        P(None, "box", "grp", None),
        P("box", "grp", None),
        P("grp", "box", None, None, None, None),
    )
    return jax.shard_map(body, mesh=mesh, in_specs=in_specs, out_specs=out_specs, check_vma=False)
```

```python
import functools
import math

import jax
import jax.numpy as jnp
import numpy as np
from jax import lax
from jax.experimental import pallas as pl
from jax.experimental.pallas import tpu as pltpu
from jax.sharding import PartitionSpec as P

F32 = jnp.float32
BOX = 32
BOX_Y = 3
BOX_Z = 4
NX = 32
NY = 96
NZ = 128
FRAME = 112
TILES = FRAME // 8
STRIDE = 120
STEP = 0.03
SCALES = (1.0, STEP, STEP, STEP, 2.0 * STEP * STEP)
UNSCALES = (1.0, 1.0 / STEP, 1.0 / STEP, 1.0 / STEP, 1.0 / (2.0 * STEP * STEP))
SOUND = math.sqrt(5.0 / 3.0)
TINY = 1e-30
COST = 1_100_000_000
MIB = 1024 * 1024


def limit(value, other):
    bound = jnp.abs(other + other)
    return jnp.maximum(jnp.minimum(value, bound), -bound)


def between(value, end):
    return jnp.minimum(jnp.maximum(value, jnp.minimum(end, 0.0)), jnp.maximum(end, 0.0))


def deviation(d_prev, d_here, d_next):
    return between(0.5 * d_here + (d_prev - d_next) * (1.0 / 12.0), d_here)


def invert(x):
    return 1.0 / x


def state_of(u, normal):
    inverse = invert(u[0])
    squares = u[1] * u[1] + u[2] * u[2] + u[3] * u[3]
    pressure = u[4] - squares * inverse
    third = pressure * (1.0 / 3.0)
    velocity = u[normal] * inverse
    ratio = jnp.maximum(third * inverse, TINY)
    reach = jnp.abs(velocity) + SOUND * (ratio * lax.rsqrt(ratio))
    return velocity, third, reach


def flux(left, right, normal):
    v_left, p_left, reach_left = state_of(left, normal)
    v_right, p_right, reach_right = state_of(right, normal)
    reach = jnp.maximum(reach_left, reach_right)
    up = v_left + reach
    down = v_right - reach
    out = [left[f] * up + right[f] * down for f in range(5)]
    out[normal] = out[normal] + (p_left + p_right)
    work = p_left * v_left + p_right * v_right
    out[4] = out[4] + (work + work)
    return out


class Line:
    def __init__(self, normal):
        self.normal = normal
        self.q = []
        self.d = []
        self.dl = None
        self.er = None
        self.flux = None

    def load(self, q, carry):
        self.q = list(q)
        self.d = [carry[0:5], carry[5:10]]
        self.dl = carry[10:15]
        self.er = carry[15:20]
        self.flux = carry[20:25]

    def carry(self):
        return tuple(self.d[0]) + tuple(self.d[1]) + tuple(self.dl) + tuple(self.er) + tuple(self.flux)

    def push(self, new):
        q, d = self.q, self.d
        out = None
        if q:
            d0 = [a - b for a, b in zip(new, q[-1])]
            if len(d) >= 2:
                d2, d1 = d[-2], d[-1]
                dr = [deviation(*t) for t in zip(d2, d1, d0)]
                if self.dl is not None:
                    here = q[-2]
                    right = [c + limit(r, l) for c, r, l in zip(here, dr, self.dl)]
                    if self.er is not None:
                        left = [c + limit(l, r) for c, r, l in zip(here, dr, self.dl)]
                        now = flux(self.er, left, self.normal)
                        if self.flux is not None:
                            out = [c - (a - b) for c, a, b in zip(q[-3], now, self.flux)]
                        self.flux = now
                    self.er = right
                self.dl = [r - s for r, s in zip(dr, d1)]
            d.append(d0)
            self.d = d[-2:]
        q.append(new)
        self.q = q[-3:]
        return out


def turn(x, shift):
    return pltpu.roll(x, shift % NZ, 1)


def lane_weights():
    parts = []
    for taps in (((1, 1), (0, -1)), ((0, -5), (1, 7), (-1, -1), (2, -1)), tuple((k, 1) for k in range(-2, 3))):
        w = np.zeros((NZ, NZ), np.float32)
        for offset, value in taps:
            for j in range(NZ):
                w[(j + offset) % NZ, j] = value
        parts.append(w)
    w = np.concatenate(parts, axis=1)
    return jnp.asarray(np.concatenate([w, w], axis=0), jnp.bfloat16)


def mixed(x, weights):
    high = x.astype(jnp.bfloat16)
    low = (x - high.astype(F32)).astype(jnp.bfloat16)
    return jnp.dot(jnp.concatenate([high, low], axis=1), weights, preferred_element_type=F32)


def x_lines(segments, read, write):
    for base, out_base, count in segments:
        line = Line(1)
        for i in range(count + 6):
            new = [read(f, base + i) * SCALES[f] if f else read(f, base + i) for f in range(5)]
            out = line.push(new)
            if out is not None:
                for f in range(5):
                    write(f, out_base + i - 6, out[f])


def x_sweep(q_ref, s_ref, planes, segments, tiles, ready, place):
    def tile(t, _):
        ready(t)
        row = pl.multiple_of(t * 8, 8)
        to = pl.multiple_of(place(t), 8)

        def write(f, x, value):
            s_ref[pl.ds((f * planes + x) * STRIDE + to, 8), :] = value

        x_lines(segments, lambda f, i: q_ref[f, i, pl.ds(row, 8), :], write)
        return 0

    lax.fori_loop(0, tiles, tile, 0)


U = 50
PAIR = 2


def yz_sweep(s_ref, dm_ref, o_ref, t_ref, w_ref, swept_ref, edge_ref, planes, ready, done):
    def group(g, _):
        ready(g)

        def at(f, row):
            return pl.ds((f * planes + g * 8) * STRIDE + row, 8, stride=STRIDE)

        def rows(row):
            return [s_ref[at(f, row), :] for f in range(5)]

        def block(k, row, count):
            return pl.ds((k * U + row) * 8, count * 8)

        first = Line(2)
        for row in range(3, 9):
            first.push(rows(row))

        def some(b, carry):
            base = b * U + 6
            line = Line(2)
            line.load([rows(base), rows(base + 1), rows(base + 2)], carry)
            for r in range(U):
                swept = line.push(rows(base + 3 + r))
                for f in range(5):
                    swept_ref[block(f, r, 1), :] = swept[f]
            for f in range(5):
                q = swept_ref[block(f, 0, U), :]
                both = mixed(q, w_ref[:, :2 * NZ])
                d = both[:, :NZ]
                dr = between(both[:, NZ:] * (1.0 / 12.0), d)
                dl = turn(dr - d, 1)
                edge_ref[block(f, 0, U), :] = q + limit(dr, dl)
                edge_ref[block(5 + f, 0, U), :] = turn(q + limit(dl, dr), -1)
            for r in range(0, U, PAIR):
                left = [edge_ref[block(f, r, PAIR), :] for f in range(5)]
                right = [edge_ref[block(5 + f, r, PAIR), :] for f in range(5)]
                now = flux(left, right, 3)
                for f in range(5):
                    final = swept_ref[block(f, r, PAIR), :] - (now[f] - turn(now[f], 1))
                    if f == 0:
                        density = final
                    else:
                        final = final * UNSCALES[f]
                    for i in range(PAIR):
                        o_ref[at(f, base + r + i), :] = final[8 * i:8 * i + 8]
                for i in range(PAIR):
                    total = density[8 * i:8 * i + 8] + dm_ref[at(0, base + r + i), :]
                    edge_ref[block(0, r + i, 1), :] = total
            sums = mixed(edge_ref[block(0, 0, U), :], w_ref[:, 2 * NZ:])
            for r in range(U):
                t_ref[at(0, base + r), :] = sums[8 * r:8 * r + 8]
            return line.carry()

        lax.fori_loop(0, 100 // U, some, first.carry())
        done(g)
        return 0

    lax.fori_loop(0, planes // 8, group, 0)


def smooth(planes, dest_ref, x_ref, y_ref, send_ref, send_row):
    def x_tile(t, _):
        row = pl.multiple_of(t * 8, 8)
        values = [planes(p, row) for p in range(12)]
        pairs = [values[p] + values[p + 1] for p in range(11)]
        for p in range(8):
            x_ref[pl.ds(p * FRAME + row, 8), :] = pairs[p] + pairs[p + 2] + values[p + 4]
        return 0

    lax.fori_loop(0, TILES, x_tile, 0)

    def y_plane(p, _):
        for t in range(NY // 8):
            start = p * FRAME + 8 + 8 * t
            parts = [x_ref[pl.ds(start + k, 8), :] for k in range(-2, 3)]
            total = ((parts[0] + parts[1]) + (parts[3] + parts[4])) + parts[2]
            y_ref[pl.ds(p * NY + 8 * t, 8), :] = total * (1.0 / 125.0)
        return 0

    lax.fori_loop(0, 8, y_plane, 0)

    places = []
    dests = [dest_ref[k] for k in range(12)]
    for k in range(12):
        slot = jnp.int32(0)
        for other in range(k):
            slot = slot + (dests[other] == dests[k]).astype(jnp.int32)
        places.append(dests[k] * 2 + slot)

    quarter = lax.broadcasted_iota(jnp.int32, (8, NZ), 1) // BOX

    def pick(values):
        out = values[3]
        for b in range(3):
            out = jnp.where(quarter == b, values[b], out)
        return out

    for by in range(BOX_Y):
        for m in range(8):
            s = [y_ref[pl.ds(by * BOX + 4 * m + q, 8, stride=NY), :] for q in range(4)]
            moved = []
            for k in range(4):
                mixed = pick([s[(b + k) % 4] for b in range(4)])
                moved.append(turn(mixed, k * BOX) if k else mixed)
            for bz in range(4):
                out = pick([moved[(q - bz) % 4] for q in range(4)])
                send_ref[places[by * 4 + bz], pl.ds(send_row, 8), pl.ds(m * NZ, NZ)] = out


def clear(send_ref):
    def one(i, _):
        send_ref[i] = jnp.zeros(send_ref.shape[1:], jnp.float32)
        return 0

    lax.fori_loop(0, send_ref.shape[0], one, 0)


def rows_of(t):
    return pl.ds(pl.multiple_of(t * 8, 8), 8)


class Tiles:
    def __init__(self, q_ref, sems, parts):
        self.q_ref, self.sems, self.parts = q_ref, sems, parts

    def copies(self, t, kind):
        out = []
        for own, before, after, src, dst in self.parts:
            q = self.q_ref.at[:, dst, rows_of(t)]
            sem = self.sems.at[t]
            if len(own) == 1:
                out.append(pltpu.make_async_copy(own[0].at[:, src, rows_of(t)], q, sem))
            elif kind == "before":
                out.append(pltpu.make_async_copy(before.at[pl.ds(0, 5), src], q, sem))
            elif kind == "after":
                out.append(pltpu.make_async_copy(after.at[pl.ds(0, 5), src], q, sem))
            else:
                density, momentum, energy = own
                rows = rows_of(t - 1)
                place = self.q_ref.at
                out.append(pltpu.make_async_copy(density.at[src, rows], place[0, dst, rows_of(t)], sem))
                out.append(pltpu.make_async_copy(momentum.at[:, src, rows], place[pl.ds(1, 3), dst, rows_of(t)], sem))
                out.append(pltpu.make_async_copy(energy.at[src, rows], place[4, dst, rows_of(t)], sem))
        return out

    def each(self, t, act):
        @pl.when(t == 0)
        def _():
            for c in self.copies(t, "before"):
                act(c)

        @pl.when(t == TILES - 1)
        def _():
            for c in self.copies(t, "after"):
                act(c)

        @pl.when((t > 0) & (t < TILES - 1))
        def _():
            for c in self.copies(t, "own"):
                act(c)

    def start(self):
        def one(t, _):
            self.each(t, lambda c: c.start())
            return 0

        lax.fori_loop(0, TILES, one, 0)

    def wait(self, t):
        self.each(t, lambda c: c.wait())


def framed(ref):
    return ref.reshape(ref.shape[0] // STRIDE, STRIDE, NZ)


def dm_copies(dm, before, after, sem, dm_ref, own, place, count):
    src, dst = pl.ds(own, count), pl.ds(place, count)
    d3 = framed(dm_ref)
    return [
        pltpu.make_async_copy(dm.at[src], d3.at[dst, pl.ds(8, NY)], sem),
        pltpu.make_async_copy(before.at[5, src], d3.at[dst, pl.ds(0, 8)], sem),
        pltpu.make_async_copy(after.at[5, src], d3.at[dst, pl.ds(104, 8)], sem),
    ]


def out_copies(o_ref, planes, outs, sem, own, place, count):
    o4 = o_ref.reshape(5, planes, STRIDE, NZ)
    src, dst, mid = pl.ds(place, count), pl.ds(own, count), pl.ds(8, NY)
    density, momentum, energy = outs
    return [
        pltpu.make_async_copy(o4.at[0, src, mid], density.at[dst], sem),
        pltpu.make_async_copy(o4.at[pl.ds(1, 3), src, mid], momentum.at[:, dst], sem),
        pltpu.make_async_copy(o4.at[4, src, mid], energy.at[dst], sem),
    ]


def start_all(copies):
    for c in copies:
        c.start()


def wait_all(copies):
    for c in copies:
        c.wait()


def sums_copy(t_ref, base, count, out, sem):
    return pltpu.make_async_copy(framed(t_ref).at[pl.ds(base, count), pl.ds(0, FRAME)], out, sem)


def field_copies(density, momentum, energy, planes, rows, out, to, sem):
    return [
        pltpu.make_async_copy(density.at[planes, rows], out.at[0, :, to], sem),
        pltpu.make_async_copy(momentum.at[:, planes, rows], out.at[pl.ds(1, 3), :, to], sem),
        pltpu.make_async_copy(energy.at[planes, rows], out.at[4, :, to], sem),
    ]


def pack_y_kernel(density, momentum, energy, dm, y_last, y_first, sem):
    copies = []
    for out, rows in ((y_last, pl.ds(NY - 8, 8)), (y_first, pl.ds(0, 8))):
        copies += field_copies(density, momentum, energy, pl.ds(0, NX), rows, out, pl.ds(0, 8), sem)
        copies.append(pltpu.make_async_copy(dm.at[:, rows], out.at[5], sem))
    start_all(copies)
    wait_all(copies)


def pack_x_kernel(density, momentum, energy, y_before, y_after, x_last, x_first, sem):
    copies = []
    for out, planes in ((x_last, pl.ds(NX - 3, 3)), (x_first, pl.ds(0, 3))):
        copies += field_copies(density, momentum, energy, planes, pl.ds(0, NY), out, pl.ds(8, NY), sem)
        for side, to in ((y_before, pl.ds(0, 8)), (y_after, pl.ds(104, 8))):
            copies.append(pltpu.make_async_copy(side.at[pl.ds(0, 5), planes], out.at[:, :, to], sem))
    start_all(copies)
    wait_all(copies)


WIDE = 24


def x_kernel(density, momentum, energy, out, q_ref, s_ref, sems, out_sem):
    held = pl.ds(1, WIDE + 6)

    def copies(t):
        rows = rows_of(t)
        return [
            pltpu.make_async_copy(density.at[held, rows], q_ref.at[0, :, rows], sems.at[t]),
            pltpu.make_async_copy(momentum.at[:, held, rows], q_ref.at[pl.ds(1, 3), :, rows], sems.at[t]),
            pltpu.make_async_copy(energy.at[held, rows], q_ref.at[4, :, rows], sems.at[t]),
        ]

    def leaving(t):
        return pltpu.make_async_copy(s_ref.at[:, :, rows_of(t)], out.at[:, :, rows_of(t)], out_sem)

    def begin(t, _):
        start_all(copies(t))
        return 0

    def tile(t, _):
        wait_all(copies(t))
        rows = rows_of(t)

        def write(f, x, value):
            s_ref[f, x, rows, :] = value

        x_lines(((0, 0, WIDE),), lambda f, i: q_ref[f, i, rows, :], write)
        leaving(t).start()
        return 0

    def end(t, _):
        leaving(t).wait()
        return 0

    lax.fori_loop(0, NY // 8, begin, 0)
    lax.fori_loop(0, NY // 8, tile, 0)
    lax.fori_loop(0, NY // 8, end, 0)


def half_copy(send, out, row, sem):
    rows = pl.ds(row, 8)
    return pltpu.make_async_copy(send.at[:, rows], out.at[:, rows], sem)


def inner_kernel(dest, weights, swept, dm, y_before, y_after,
                 out_density, out_momentum, out_energy, out_sums, send_out,
                 q_ref, s_ref, o_ref, dm_ref, t_ref, w_ref, swept_ref, edge_ref, x_ref, y_ref, send, sems, sem, out_sem):
    held = pl.ds(1, WIDE + 6)
    s4 = s_ref.reshape(5, WIDE, STRIDE, NZ)
    outs = (out_density, out_momentum, out_energy)

    def swept_copy(g):
        planes = pl.ds(g * 8, 8)
        return pltpu.make_async_copy(swept.at[:, planes], s4.at[:, planes, pl.ds(8, NY)], sems.at[g])

    def leaving(g):
        return out_copies(o_ref, WIDE, outs, out_sem, 4 + g * 8, g * 8, 8)

    halo = [
        pltpu.make_async_copy(y_before.at[pl.ds(0, 5), held], q_ref.at[:, :, pl.ds(0, 8)], sem),
        pltpu.make_async_copy(y_after.at[pl.ds(0, 5), held], q_ref.at[:, :, pl.ds(8, 8)], sem),
    ] + dm_copies(dm, y_before, y_after, sem, dm_ref, 4, 0, WIDE)
    halo.append(pltpu.make_async_copy(weights, w_ref, sem))
    start_all(halo)
    for g in range(WIDE // 8):
        swept_copy(g).start()
    clear(send)
    wait_all(halo)
    x_sweep(q_ref, s_ref, WIDE, ((0, 0, WIDE),), 2, lambda t: None, lambda t: t * 104)
    yz_sweep(s_ref, dm_ref, o_ref, t_ref, w_ref, swept_ref, edge_ref, WIDE, lambda g: swept_copy(g).wait(), lambda g: start_all(leaving(g)))
    sums = sums_copy(t_ref, 0, WIDE, out_sums, sem)
    sums.start()
    for row, base in ((0, 2), (8, 10)):
        smooth(lambda p, r: t_ref[pl.ds((base + p) * STRIDE + r, 8), :], dest, x_ref, y_ref, send, row)
        half_copy(send, send_out, row, sems.at[4 + row // 8]).start()
    sums.wait()
    for row in (0, 8):
        half_copy(send, send_out, row, sems.at[4 + row // 8]).wait()
    for g in range(WIDE // 8):
        wait_all(leaving(g))


def outer_kernel(weights, density, momentum, energy, dm, y_before, y_after, x_before, x_after,
                 in_density, in_momentum, in_energy,
                 out_density, out_momentum, out_energy, out_sums, to_next, to_prev,
                 q_ref, s_ref, o_ref, dm_ref, t_ref, w_ref, swept_ref, edge_ref, sems, sem, out_sem):
    fields = (density, momentum, energy)
    tiles = Tiles(q_ref, sems, [
        (fields, y_before, y_after, pl.ds(25, 7), pl.ds(0, 7)),
        ((x_after,), None, None, pl.ds(0, 3), pl.ds(7, 3)),
        ((x_before,), None, None, pl.ds(0, 3), pl.ds(10, 3)),
        (fields, y_before, y_after, pl.ds(0, 7), pl.ds(13, 7)),
    ])
    tiles.start()
    copies = (dm_copies(dm, y_before, y_after, sem, dm_ref, 28, 0, 4)
              + dm_copies(dm, y_before, y_after, sem, dm_ref, 0, 4, 4))
    copies.append(pltpu.make_async_copy(weights, w_ref, sem))
    start_all(copies)
    x_sweep(q_ref, s_ref, 8, ((0, 0, 4), (10, 4, 4)), TILES, tiles.wait, lambda t: t * 8)
    wait_all(copies)
    yz_sweep(s_ref, dm_ref, o_ref, t_ref, w_ref, swept_ref, edge_ref, 8, lambda g: None, lambda g: None)
    outs = (out_density, out_momentum, out_energy)
    leaving = out_copies(o_ref, 8, outs, out_sem, 28, 0, 4) + out_copies(o_ref, 8, outs, out_sem, 0, 4, 4)
    leaving.append(sums_copy(t_ref, 0, 8, out_sums, out_sem))
    leaving.append(sums_copy(t_ref, 2, 2, to_next, out_sem))
    leaving.append(sums_copy(t_ref, 4, 2, to_prev, out_sem))
    start_all(leaving)
    wait_all(leaving)


def rest_kernel(dest, sums_inner, sums_outer, from_prev, from_next, send_out, w_ref, x_ref, y_ref, send, sem, out_sems):
    def part(src, own, place, count):
        return pltpu.make_async_copy(src.at[pl.ds(own, count)], w_ref.at[pl.ds(place, count)], sem)

    copies = [
        part(from_prev, 0, 0, 2),
        part(sums_outer, 4, 2, 4),
        part(sums_inner, 0, 6, 6),
        part(sums_inner, 18, 12, 6),
        part(sums_outer, 0, 18, 4),
        part(from_next, 0, 22, 2),
    ]
    start_all(copies)
    clear(send)
    wait_all(copies)
    for row, base in ((0, 0), (8, 12)):
        smooth(lambda p, r: w_ref[base + p, pl.ds(r, 8), :], dest, x_ref, y_ref, send, row)
        half_copy(send, send_out, row, out_sems.at[row // 8]).start()
    for row in (0, 8):
        half_copy(send, send_out, row, out_sems.at[row // 8]).wait()


ANY = pl.BlockSpec(memory_space=pl.ANY)
SMEM = pl.BlockSpec(memory_space=pltpu.SMEM)
VMEM = pl.BlockSpec(memory_space=pltpu.VMEM)


def shape(*dims):
    return jax.ShapeDtypeStruct(dims, F32)


def params(mib):
    return pltpu.CompilerParams(vmem_limit_bytes=mib * MIB)


def cost(micros):
    return pl.CostEstimate(flops=int(micros * COST), bytes_accessed=0, transcendentals=0)


def main_scratch(planes, held, rows):
    return [
        pltpu.VMEM((5, held, rows, NZ), F32),
        pltpu.VMEM((5 * planes * STRIDE, NZ), F32),
        pltpu.VMEM((5 * planes * STRIDE, NZ), F32),
        pltpu.VMEM((planes * STRIDE, NZ), F32),
        pltpu.VMEM((planes * STRIDE, NZ), F32),
        pltpu.VMEM((2 * NZ, 3 * NZ), jnp.bfloat16),
        pltpu.VMEM((5 * U * 8, NZ), F32),
        pltpu.VMEM((10 * U * 8, NZ), F32),
    ]


def semaphores():
    return [pltpu.SemaphoreType.DMA((TILES,)), pltpu.SemaphoreType.DMA, pltpu.SemaphoreType.DMA]


def smooth_scratch():
    return [pltpu.VMEM((8 * FRAME, NZ), F32), pltpu.VMEM((8 * NY, NZ), F32)]


FIELD_SHAPES = (shape(NX, NY, NZ), shape(3, NX, NY, NZ), shape(NX, NY, NZ))


def shifted(value, axis, by):
    size = lax.axis_size(axis)
    return lax.ppermute(value, axis, [(i, (i + by) % size) for i in range(size)])


def body(density, momentum, energy, dm_density, box_dest):
    dest = box_dest[0, 0, :, 0]
    fields = (density, momentum, energy)
    weights = lane_weights()
    y_last, y_first = pl.pallas_call(
        pack_y_kernel,
        out_shape=(shape(6, NX, 8, NZ),) * 2,
        in_specs=[ANY] * 4,
        out_specs=[VMEM] * 2,
        scratch_shapes=[pltpu.SemaphoreType.DMA],
        compiler_params=params(64),
        cost_estimate=cost(3),
        name="pack_y",
    )(density, momentum, energy, dm_density)
    y_before = shifted(y_last, "grp", 1)
    y_after = shifted(y_first, "grp", -1)

    swept = pl.pallas_call(
        x_kernel,
        out_shape=shape(5, WIDE, NY, NZ),
        in_specs=[ANY] * 3,
        out_specs=ANY,
        scratch_shapes=[
            pltpu.VMEM((5, WIDE + 6, NY, NZ), F32), pltpu.VMEM((5, WIDE, NY, NZ), F32),
            pltpu.SemaphoreType.DMA((NY // 8,)), pltpu.SemaphoreType.DMA],
        compiler_params=params(64),
        cost_estimate=cost(9),
        name="x_own",
    )(*fields)

    x_last, x_first = pl.pallas_call(
        pack_x_kernel,
        out_shape=(shape(5, 3, FRAME, NZ),) * 2,
        in_specs=[ANY] * 5,
        out_specs=[VMEM] * 2,
        scratch_shapes=[pltpu.SemaphoreType.DMA],
        compiler_params=params(64),
        cost_estimate=cost(3),
        name="pack_x",
    )(*fields, y_before, y_after)
    x_before = shifted(x_last, "box", 1)
    x_after = shifted(x_first, "box", -1)

    def exchange(send, planes):
        return lax.all_to_all(send.reshape(16, 2, planes, 1024), "box", split_axis=0, concat_axis=0, tiled=True)

    inner = pl.pallas_call(
        inner_kernel,
        out_shape=FIELD_SHAPES + (shape(WIDE, FRAME, NZ), shape(32, 16, 1024)),
        in_specs=[SMEM] + [ANY] * 5,
        out_specs=[ANY] * 5,
        scratch_shapes=main_scratch(WIDE, WIDE + 6, 16) + smooth_scratch() + [pltpu.VMEM((32, 16, 1024), F32)] + semaphores(),
        compiler_params=params(64),
        cost_estimate=cost(26),
        name="inner",
    )(dest, weights, swept, dm_density, y_before, y_after)
    *made, sums_inner, send_inner = inner
    got_inner = exchange(send_inner, 16)

    outer = pl.pallas_call(
        outer_kernel,
        out_shape=FIELD_SHAPES + (shape(8, FRAME, NZ), shape(2, FRAME, NZ), shape(2, FRAME, NZ)),
        in_specs=[ANY] * 12,
        out_specs=[ANY] * 6,
        scratch_shapes=main_scratch(8, 20, FRAME) + semaphores(),
        input_output_aliases={9: 0, 10: 1, 11: 2},
        compiler_params=params(54),
        cost_estimate=cost(13),
        name="outer",
    )(weights, *fields, dm_density, y_before, y_after, x_before, x_after, *made)
    new_density, new_momentum, new_energy, sums_outer, to_next, to_prev = outer
    from_prev = shifted(to_next, "box", 1)
    from_next = shifted(to_prev, "box", -1)
    send_rest = pl.pallas_call(
        rest_kernel,
        out_shape=shape(32, 16, 1024),
        in_specs=[SMEM] + [ANY] * 4,
        out_specs=ANY,
        scratch_shapes=[pltpu.VMEM((24, FRAME, NZ), F32)] + smooth_scratch() + [
            pltpu.VMEM((32, 16, 1024), F32), pltpu.SemaphoreType.DMA, pltpu.SemaphoreType.DMA((2,))],
        compiler_params=params(54),
        cost_estimate=cost(5),
        name="rest",
    )(dest, sums_inner, sums_outer, from_prev, from_next)
    send_rest, got_inner = lax.optimization_barrier((send_rest, got_inner))
    got_rest = exchange(send_rest, 16)
    kd = jnp.concatenate([got_rest[:, :, :8], got_inner, got_rest[:, :, 8:]], axis=2)
    return (new_density, new_momentum, new_energy, kd[None, None])


def solution(mesh):
    in_specs = (
        P("box", "grp", None),
        P(None, "box", "grp", None),
        P("box", "grp", None),
        P("box", "grp", None),
        P("grp", "box", None, None),
    )
    out_specs = (
        P("box", "grp", None),
        P(None, "box", "grp", None),
        P("box", "grp", None),
        P("grp", "box", None, None, None, None),
    )
    return jax.shard_map(body, mesh=mesh, in_specs=in_specs, out_specs=out_specs, check_vma=False)
```
